32 devices in a mesh: station: 4 (over z), band: 4 (over y, x), tm: 2 (over core).
Axes of the slice: x: 2, y: 2, z: 4, core: 2. Of those that a mesh axis runs over, the one named last changes fastest.
Arguments:
- volts: bfloat16 [2, 4, 1024, 36864], P(None, 'band', 'station', 'tm'), may hold values from -300 to 300
- flagged: int32 [4, 36], replicated, may hold values from 0 to 143, as said below
Outputs:
- visibilities: float32 [4, 16, 2, 1024, 1024], P('band', 'station', None, 'tm')
The draws below stay inside these ranges and needn't reach their ends.
Inputs may be any that keep to these rules, and one draw needn't show every extreme that they name: `flagged`: each coarse channel's list holds fine channels 0 and 143, a run of 18 consecutive fine channels (counted cyclically), and further channels; entries may repeat.
All inputs are finite; a program needn't handle non-finite values.
Results may differ from the reference program's by a relative error of at most 0.0041.
Values may be sent and summed in bfloat16 or wider, within the bound.
No kernel may reach another device: no remote copies, remote signals or barrier semaphores. Data moves between devices by JAX's collectives and lax.ppermute only.
A program may use at most 192 MiB of HBM per device.

```python
import math
import jax
import jax.numpy as jnp
from jax import lax

INPUTS = 1024
SUBBAND_COUNT = 144
TAPS = 12
GROUP = 9
VGROUPS = 16
MASKED_NUMBER = 36
COARSE = 4
FRAMES = 256
SAMPLES = 36864


def draw_volts(key, part):
    key = jax.random.fold_in(key, 11)
    noise_key, amp_key = jax.random.split(key, 2)
    shape = (2, COARSE, INPUTS, SAMPLES)
    base = jnp.clip(jax.random.normal(noise_key, shape, jnp.float32), -6.0, 6.0)
    amp = jnp.exp(jax.random.uniform(amp_key, (INPUTS,), jnp.float32, 0.0, math.log(10.0)))
    coarse_ramp = jnp.sqrt(1.0 + 2.0 * jnp.arange(COARSE, dtype=jnp.float32) / max(COARSE - 1, 1))
    time_ramp = jnp.sqrt(1.0 + 2.0 * jnp.arange(SAMPLES, dtype=jnp.float32) / (SAMPLES - 1))
    return (base * amp[None, None, :, None] * coarse_ramp[None, :, None, None] * time_ramp[None, None, None, :]).astype(jnp.bfloat16)


def draw_flagged(key, part):
    key = jax.random.fold_in(key, 23)
    start_key, extra_key = jax.random.split(key, 2)
    beginning_position = jax.random.randint(start_key, (COARSE, 1), 0, SUBBAND_COUNT)
    voltage_group = (beginning_position + jnp.arange(MASKED_NUMBER // 2, dtype=jnp.int32)[None, :]) % SUBBAND_COUNT
    surplus_voltages = jax.random.randint(extra_key, (COARSE, MASKED_NUMBER - MASKED_NUMBER // 2 - 2), 0, SUBBAND_COUNT)
    subband_bounds = jnp.broadcast_to(jnp.array([0, SUBBAND_COUNT - 1], jnp.int32)[None, :], (COARSE, 2))
    return jnp.concatenate([subband_bounds, voltage_group.astype(jnp.int32), surplus_voltages.astype(jnp.int32)], 1)


def setup_inputs(seed: int = 0) -> dict:
    seeds = jax.random.split(jax.random.key(seed), 3)
    return {
        "volts": draw_volts(jax.random.fold_in(seeds[2], 71), 0),
        "flagged": draw_flagged(jax.random.fold_in(seeds[2], 71), 0),
    }


def window_table():
    total = TAPS * SUBBAND_COUNT
    place = jnp.arange(total, dtype=jnp.float32)
    shape = jnp.sinc((place - total / 2.0 + 0.5) / SUBBAND_COUNT)
    taper = 0.5 - 0.5 * jnp.cos(2.0 * math.pi * (place + 0.5) / total)
    return (shape * taper).reshape(TAPS, SUBBAND_COUNT)

def rotation_factor_table():
    left = jnp.arange(SUBBAND_COUNT, dtype=jnp.int32)[:, None]
    right = jnp.arange(SUBBAND_COUNT, dtype=jnp.int32)[None, :]
    angle = 2.0 * math.pi * (left * right % SUBBAND_COUNT).astype(jnp.float32) / SUBBAND_COUNT
    cosines = jnp.cos(angle)
    sines = jnp.sin(angle)
    upper = jnp.stack([cosines, -sines], 1)
    lower = jnp.stack([sines, cosines], 1)
    return jnp.concatenate([upper, lower], 0).astype(jnp.bfloat16)

def reference(volts, flagged):
    window = window_table()
    table = rotation_factor_table().astype(jnp.float32)
    fine_ids = jnp.arange(SUBBAND_COUNT, dtype=jnp.int32)
    keep = jnp.all(flagged[:, :, None] != fine_ids[None, None, :], axis=1).astype(jnp.float32)

    def channelize(single):
        frames = single.reshape(2, INPUTS, FRAMES, SUBBAND_COUNT).astype(jnp.float32)
        padded = jnp.pad(frames, ((0, 0), (0, 0), (TAPS - 1, 0), (0, 0)))
        filtered = jnp.zeros((2, INPUTS, FRAMES, SUBBAND_COUNT), jnp.float32)
        for tap in range(TAPS):
            filtered = filtered + window[tap][None, None, None, :] * padded[:, :, tap:tap + FRAMES, :]
        filtered = filtered.astype(jnp.bfloat16)
        joined_spectra = jnp.concatenate([filtered[0], filtered[1]], -1).astype(jnp.float32)
        spectra = jnp.einsum('itn,nrf->firt', joined_spectra, table, precision=lax.Precision.HIGHEST)
        return spectra.astype(jnp.bfloat16)
    spectra = lax.map(channelize, jnp.moveaxis(volts, 1, 0))

    def squares(single):
        values = single.astype(jnp.float32)
        return lax.optimization_barrier(jnp.sum(values * values, axis=(2, 3)))
    energy = lax.map(squares, spectra)
    power = lax.optimization_barrier(jnp.sum(energy * keep[:, :, None], axis=(0, 1))) / (FRAMES * jnp.sum(keep))
    scales = lax.rsqrt(power + 1e-06)

    def correlate(item):
        single, kept = item
        blocks = (single.astype(jnp.float32) * kept[:, None, None, None]).reshape(VGROUPS, GROUP, INPUTS, 2, FRAMES)

        def one_group(block):
            swapped = jnp.stack([block[:, :, 1], -block[:, :, 0]], 2)
            real = jnp.einsum('fird,fjrd->ij', block, block, precision=lax.Precision.HIGHEST)
            imag = jnp.einsum('fird,fjrd->ij', swapped, block, precision=lax.Precision.HIGHEST)
            return jnp.stack([real, imag], 0)
        return lax.map(one_group, blocks)
    raw = lax.map(correlate, (spectra, keep))
    counts = keep.reshape(COARSE, VGROUPS, GROUP).sum(-1)
    denom = FRAMES * jnp.maximum(counts, 1.0)
    pair_scales = scales[:, None] * scales[None, :]
    return raw * pair_scales[None, None, None, :, :] / denom[:, :, None, None, None]
```

```python
import functools
import math

import jax
import jax.numpy as jnp
import numpy as np
from jax import lax
from jax.experimental import pallas as pl
from jax.experimental.pallas import tpu as pltpu
from jax.sharding import PartitionSpec as P

SUBBAND_COUNT = 144
TAPS = 12
GROUP = 9
BLOCK = 16
FIRST = 1
SPREAD = BLOCK + 1
VMEM = 48 * 1024 * 1024


def window_values():
    total = TAPS * SUBBAND_COUNT
    place = np.arange(total, dtype=np.float64)
    shape = np.sinc((place - total / 2.0 + 0.5) / SUBBAND_COUNT)
    taper = 0.5 - 0.5 * np.cos(2.0 * math.pi * (place + 0.5) / total)
    return (shape * taper).reshape(TAPS, SUBBAND_COUNT).astype(np.float32)


def twiddle_values():
    f = np.arange(SUBBAND_COUNT, dtype=np.int64)[:, None]
    n = np.arange(SUBBAND_COUNT, dtype=np.int64)[None, :]
    angle = 2.0 * math.pi * (f * n % SUBBAND_COUNT) / SUBBAND_COUNT
    cosines, sines = np.cos(angle), np.sin(angle)
    real = np.concatenate([cosines, sines], 1)
    imag = np.concatenate([-sines, cosines], 1)
    return np.stack([real, imag], 1).astype(np.float32)


def front_kernel(splits, owners, keep_ref, hist_ref, volts_ref, window_ref, table_ref, *rest):
    outs, power_ref = rest[: owners * splits], rest[owners * splits]
    ring, filt, spread = rest[owners * splits + 1 :]
    step = pl.program_id(0)
    now = lax.rem(step, 2)
    before = 1 - now
    inputs = ring.shape[-1]
    tiles = inputs // 128
    span = BLOCK * SUBBAND_COUNT

    def turn(ref, slot):
        def columns(c, _):
            at = pl.multiple_of(c * 128, 128)
            for part in range(2):
                ring[slot, part, pl.ds(at, 128), :] = ref[part, 0, :, pl.ds(at, 128)].T
            return 0

        lax.fori_loop(0, span // 128, columns, 0)

    @pl.when(step == 0)
    def _():
        turn(hist_ref, 1)
        power_ref[...] = jnp.zeros_like(power_ref)

    turn(volts_ref, now)

    def filter_rows(j, _):
        base = pl.multiple_of(j * 16, 16)
        for tile in range(tiles):
            lanes = pl.ds(tile * 128, 128)
            weights = [window_ref[k, pl.ds(base, 16), :] for k in range(TAPS)]
            for part in range(2):
                samples = []
                for t in range(1 - TAPS, BLOCK):
                    slot, frame = (now, t) if t >= 0 else (before, BLOCK + t)
                    at = pl.multiple_of(frame * SUBBAND_COUNT + base, 16)
                    samples.append(ring[slot, part, pl.ds(at, 16), lanes].astype(jnp.float32))
                for t in range(BLOCK):
                    total = weights[0] * samples[t]
                    for k in range(1, TAPS):
                        total = total + weights[k] * samples[t + k]
                    at = pl.multiple_of(part * SUBBAND_COUNT + base, 16)
                    filt[t, pl.ds(at, 16), lanes] = total.astype(jnp.bfloat16)
        return 0

    lax.fori_loop(0, SUBBAND_COUNT // 16, filter_rows, 0)

    def transform(t, _):
        result = jnp.dot(table_ref[...], filt[t], preferred_element_type=jnp.float32)
        for tile in range(tiles):
            spread[tile, pl.ds(t, 2 * SUBBAND_COUNT, stride=SPREAD), :] = result[
                :, tile * 128 : (tile + 1) * 128
            ]
        return 0

    lax.fori_loop(0, BLOCK, transform, 0)

    groups = SUBBAND_COUNT // owners // GROUP
    power = [jnp.zeros((BLOCK, 128), jnp.float32) for _ in range(tiles)]
    for d in range(owners):
        for j in range(groups):
            out = outs[d * splits + j] if splits > 1 else outs[d]
            place = 0 if splits > 1 else j

            def channel(f, power, d=d, j=j, out=out, place=place):
                keep = keep_ref[(d * groups + j) * GROUP + f]
                power = list(power)
                for part in range(2):
                    row = ((d * groups + j) * 2 + part) * GROUP + f
                    for tile in range(tiles):
                        value = spread[tile, pl.ds(row * SPREAD, BLOCK), :] * keep
                        value = value.astype(jnp.bfloat16)
                        out[place, part, f, :, tile * 128 : (tile + 1) * 128] = value
                        value = value.astype(jnp.float32)
                        power[tile] = power[tile] + value * value
                return tuple(power)

            power = lax.fori_loop(0, GROUP, channel, tuple(power))
    for tile in range(tiles):
        power_ref[:, tile * 128 : (tile + 1) * 128] += power[tile]


def front(volts, hist, hist_block, first, steps, splits, owners, keep, window, table):
    inputs = volts.shape[2]
    span = BLOCK * SUBBAND_COUNT
    groups = SUBBAND_COUNT // owners // GROUP
    each = groups // splits
    frames = steps * BLOCK
    outs = [
        jax.ShapeDtypeStruct((each, 2, GROUP, frames, inputs), jnp.bfloat16)
        for _ in range(owners * splits)
    ]
    out_specs = [
        pl.BlockSpec((each, 2, GROUP, BLOCK, inputs), lambda s: (0, 0, 0, s, 0))
        for _ in range(owners * splits)
    ]
    outs.append(jax.ShapeDtypeStruct((BLOCK, inputs), jnp.float32))
    out_specs.append(pl.BlockSpec((BLOCK, inputs), lambda s: (0, 0)))
    macs = 2 * SUBBAND_COUNT * frames * inputs * 2 * SUBBAND_COUNT
    result = pl.pallas_call(
        functools.partial(front_kernel, splits, owners),
        grid=(steps,),
        out_shape=outs,
        in_specs=[
            pl.BlockSpec(memory_space=pltpu.SMEM),
            pl.BlockSpec((2, 1, inputs, span), lambda s: (0, 0, 0, hist_block)),
            pl.BlockSpec((2, 1, inputs, span), lambda s: (0, 0, 0, first + s)),
            pl.BlockSpec(window.shape, lambda s: (0, 0, 0)),
            pl.BlockSpec(table.shape, lambda s: (0, 0)),
        ],
        out_specs=out_specs,
        scratch_shapes=[
            pltpu.VMEM((2, 2, span, inputs), jnp.bfloat16),
            pltpu.VMEM((BLOCK, 2 * SUBBAND_COUNT, inputs), jnp.bfloat16),
            pltpu.VMEM((inputs // 128, 2 * SUBBAND_COUNT * SPREAD, 128), jnp.float32),
        ],
        compiler_params=pltpu.CompilerParams(vmem_limit_bytes=VMEM),
        cost_estimate=pl.CostEstimate(
            flops=2 * macs * 4, bytes_accessed=2 * frames * SUBBAND_COUNT * inputs * 8, transcendentals=0
        ),
        name="front",
    )(keep, hist, volts, window, table)
    return result[:-1], result[-1]


def after_kernel(value_ref, other_ref, out_ref):
    pass


def after(value, other):
    anywhere = pl.BlockSpec(memory_space=pl.ANY)
    return pl.pallas_call(
        after_kernel,
        out_shape=jax.ShapeDtypeStruct(value.shape, value.dtype),
        in_specs=[anywhere, anywhere],
        out_specs=anywhere,
        input_output_aliases={0: 0},
        cost_estimate=pl.CostEstimate(flops=0, bytes_accessed=0, transcendentals=0),
        name="after",
    )(value, other)


def correlate_kernel(owners, group, place_ref, *rest):
    early, late = rest[:owners], rest[owners : 2 * owners]
    out_ref, held, turned, sems = rest[2 * owners :]
    me, half = place_ref[0], place_ref[1]
    column = pl.program_id(0)
    per_half = turned.shape[0]
    lead = early[0].shape[2]

    @pl.when(column == 0)
    def _():
        copies = []
        for d in range(owners):
            source = lax.rem(me - d + owners, owners)
            copies.append(
                pltpu.make_async_copy(
                    early[d].at[group], held.at[source, :, pl.ds(0, lead)], sems.at[0, d]
                )
            )
            copies.append(
                pltpu.make_async_copy(
                    late[d].at[0],
                    held.at[source, :, pl.ds(lead, late[d].shape[2])],
                    sems.at[1, d],
                )
            )
        for copy in copies:
            copy.start()
        for copy in copies:
            copy.wait()
        for r in range(per_half):
            for part in range(2):
                turned[r, part] = held[half * per_half + r, part].T

    real, imag = held[column, 0], held[column, 1]
    width = real.shape[1]
    dot = functools.partial(jnp.dot, preferred_element_type=jnp.float32)
    for r in range(per_half):
        rows = slice(r * width, (r + 1) * width)
        out_ref[0, rows, :] = (dot(turned[r, 0], real) + dot(turned[r, 1], imag)).astype(out_ref.dtype)
        out_ref[1, rows, :] = (dot(turned[r, 1], real) - dot(turned[r, 0], imag)).astype(out_ref.dtype)


def correlate(place, early, late, group, dtype):
    owners = len(early)
    inputs = late[0].shape[-1]
    depth = early[0].shape[2] + late[0].shape[2]
    rows = owners // 2 * inputs
    anywhere = pl.BlockSpec(memory_space=pl.ANY)
    return pl.pallas_call(
        functools.partial(correlate_kernel, owners, group),
        grid=(owners,),
        out_shape=jax.ShapeDtypeStruct((2, rows, owners * inputs), dtype),
        in_specs=[pl.BlockSpec(memory_space=pltpu.SMEM)] + [anywhere] * (2 * owners),
        out_specs=pl.BlockSpec((2, rows, inputs), lambda b: (0, 0, b)),
        scratch_shapes=[
            pltpu.VMEM((owners, 2, depth, inputs), jnp.bfloat16),
            pltpu.VMEM((owners // 2, 2, inputs, depth), jnp.bfloat16),
            pltpu.SemaphoreType.DMA((2, owners)),
        ],
        compiler_params=pltpu.CompilerParams(vmem_limit_bytes=VMEM),
        cost_estimate=pl.CostEstimate(
            flops=8 * rows * owners * inputs * depth,
            bytes_accessed=owners * 4 * depth * inputs + 8 * rows * owners * inputs,
            transcendentals=0,
        ),
        name="correlate",
    )(place, *early, *late)


def equalize_kernel(rows_ref, columns_ref, mine_ref, theirs_ref, *rest):
    out_ref = rest[-1]
    scale = rows_ref[...] * columns_ref[...]
    for part in range(2):
        total = mine_ref[part] + theirs_ref[part].astype(jnp.float32)
        out_ref[0, part] = total * scale


def equalize(row_scales, column_scales, mine, theirs, out, group, groups):
    rows, columns = mine.shape[1:]
    block = rows // 4
    specs = [
        pl.BlockSpec((block, 1), lambda r: (r, 0)),
        pl.BlockSpec((1, columns), lambda r: (0, 0)),
        pl.BlockSpec((2, block, columns), lambda r: (0, r, 0)),
        pl.BlockSpec((2, block, columns), lambda r: (0, r, 0)),
    ]
    operands = [row_scales, column_scales, mine, theirs]
    aliases = {}
    if out is not None:
        specs.append(pl.BlockSpec(memory_space=pl.ANY))
        operands.append(out)
        aliases = {4: 0}
    return pl.pallas_call(
        equalize_kernel,
        grid=(rows // block,),
        out_shape=jax.ShapeDtypeStruct((groups, 2, rows, columns), jnp.float32),
        in_specs=specs,
        out_specs=pl.BlockSpec((1, 2, block, columns), lambda r: (group, 0, r, 0)),
        input_output_aliases=aliases,
        compiler_params=pltpu.CompilerParams(vmem_limit_bytes=VMEM),
        cost_estimate=pl.CostEstimate(
            flops=6 * rows * columns, bytes_accessed=20 * rows * columns, transcendentals=0
        ),
        name="equalize",
    )(*operands)


def shift(value, d):
    count = lax.axis_size("station")
    return lax.ppermute(value, "station", [(s, (s + d) % count) for s in range(count)])


def passed_on(value):
    count = lax.axis_size("tm")
    return lax.ppermute(value, "tm", [(s, s + 1) for s in range(count - 1)])


def keep_table(flagged):
    fine = jnp.arange(SUBBAND_COUNT, dtype=jnp.int32)
    return jnp.all(flagged[:, :, None] != fine[None, None, :], axis=1).astype(jnp.float32)


def pipelined(volts, flagged):
    owners = lax.axis_size("station")
    me = lax.axis_index("station")
    half = lax.axis_index("tm")
    inputs = volts.shape[2]
    frames = volts.shape[3] // SUBBAND_COUNT
    frames_all = frames * lax.axis_size("tm")
    fine = SUBBAND_COUNT // owners
    groups = fine // GROUP
    blocks = frames // BLOCK
    span = BLOCK * SUBBAND_COUNT

    keep_all = keep_table(flagged)
    keep_mine = lax.dynamic_index_in_dim(keep_all, lax.axis_index("band"), 0, keepdims=False)
    twice = jnp.concatenate([keep_mine, keep_mine])
    keep_ahead = lax.dynamic_slice_in_dim(twice, me * fine, SUBBAND_COUNT, 0)

    rows = twiddle_values().reshape(owners, groups, GROUP, 2, 2 * SUBBAND_COUNT)
    rows = rows.transpose(0, 1, 3, 2, 4).reshape(2 * SUBBAND_COUNT, 2 * SUBBAND_COUNT)
    rows = jnp.asarray(np.concatenate([rows, rows], 0)).astype(jnp.bfloat16)
    table = lax.dynamic_slice_in_dim(rows, me * 2 * fine, 2 * SUBBAND_COUNT, 0)
    window = jnp.broadcast_to(
        jnp.asarray(window_values())[:, :, None], (TAPS, SUBBAND_COUNT, 128)
    )

    halo = passed_on(volts[:, :, :, (blocks - 1) * span :])
    rest = blocks - FIRST
    early, power_a = front(volts, volts, rest - 1, rest, FIRST, 1, owners, keep_ahead, window, table)
    late, power_b = front(volts, halo, 0, 0, rest, groups, owners, keep_ahead, window, table)

    early = [x.reshape(groups, 2, GROUP * FIRST * BLOCK, inputs) for x in early]
    late = [x.reshape(1, 2, GROUP * rest * BLOCK, inputs) for x in late]
    late = [[late[d * groups + j] for d in range(owners)] for j in range(groups)]

    sent = [early[0]] + [shift(early[d], d) for d in range(1, owners)]
    arrived = []
    for j in range(groups):
        gate = sent if j == 1 else arrived[j - 2] if j > 1 else None
        got = [late[j][0]]
        for d in range(1, owners):
            value = late[j][d]
            if gate is not None:
                value = after(value, gate[d])
            got.append(shift(value, d))
        arrived.append(got)

    local = jnp.sum(power_a + power_b, axis=0)
    total = lax.psum(local, ("band", "tm"))
    scale = lax.rsqrt(total / (frames_all * jnp.sum(keep_all)) + 1e-06)
    scales = lax.all_gather(scale, "station", axis=0, tiled=True)
    kept = lax.dynamic_slice_in_dim(keep_mine, me * fine, fine, 0)
    counts = kept.reshape(groups, GROUP).sum(-1)
    denom = frames_all * jnp.maximum(counts, 1.0)
    per_half = scales.shape[0] // 2
    row_scales = lax.dynamic_slice_in_dim(scales, half * per_half, per_half, 0)

    other = [(0, 1), (1, 0)]
    send_place = jnp.stack([me, 1 - half]).astype(jnp.int32)
    mine_place = jnp.stack([me, half]).astype(jnp.int32)
    out = None
    for j in range(groups):
        theirs = correlate(send_place, sent, arrived[j], j, jnp.bfloat16)
        theirs = lax.ppermute(theirs, "tm", other)
        mine = correlate(mine_place, sent, arrived[j], j, jnp.float32)
        out = equalize(
            (row_scales / denom[j])[:, None], scales[None, :], mine, theirs, out, j, groups
        )
    return out[None]


def twiddle_table():
    values = twiddle_values().transpose(2, 1, 0)
    return jnp.asarray(values).astype(jnp.bfloat16)


def pair_products(left, right):
    swapped = jnp.stack([left[..., 1, :], -left[..., 0, :]], 4)
    real = jnp.einsum("cgfird,cgfjrd->icgj", left, right, preferred_element_type=jnp.float32)
    imag = jnp.einsum("cgfird,cgfjrd->icgj", swapped, right, preferred_element_type=jnp.float32)
    return jnp.stack([real, imag], 3)


def plain(volts, flagged):
    coarse_dev = volts.shape[1]
    inputs_dev = volts.shape[2]
    spec_count = volts.shape[3] // SUBBAND_COUNT
    frames_all = spec_count * lax.axis_size("tm")
    frames = volts.reshape(2, coarse_dev, inputs_dev, spec_count, SUBBAND_COUNT)
    history = passed_on(frames[:, :, :, spec_count - (TAPS - 1) :, :])
    padded = jnp.concatenate([history, frames], 3)
    window = jnp.asarray(window_values())
    filtered = jnp.zeros((2, coarse_dev, inputs_dev, spec_count, SUBBAND_COUNT), jnp.float32)
    for tap in range(TAPS):
        filtered = filtered + window[tap] * padded[:, :, :, tap : tap + spec_count, :].astype(
            jnp.float32
        )
    filtered = filtered.astype(jnp.bfloat16)
    joined = jnp.concatenate([filtered[0], filtered[1]], -1)
    spectra = jnp.einsum(
        "nqvx,xdl->nlqdv", joined, twiddle_table(), preferred_element_type=jnp.float32
    ).astype(jnp.bfloat16)
    keep_all = keep_table(flagged)
    keep_mine = lax.dynamic_slice_in_dim(
        keep_all, lax.axis_index("band") * coarse_dev, coarse_dev, 0
    )
    values = spectra.astype(jnp.float32)
    local = jnp.sum(values * values * keep_mine[:, :, None, None, None], axis=(0, 1, 3, 4))
    total = lax.psum(local, ("band", "tm"))
    scale = lax.rsqrt(total / (frames_all * jnp.sum(keep_all)) + 1e-06)
    scales = lax.all_gather(scale, "station", axis=0, tiled=True)
    received = lax.all_to_all(spectra, "station", split_axis=1, concat_axis=2, tiled=True)
    fine_dev = received.shape[1]
    inputs_all = received.shape[2]
    kept = lax.dynamic_slice_in_dim(keep_mine, lax.axis_index("station") * fine_dev, fine_dev, 1)
    groups_dev = fine_dev // GROUP
    masked = received * kept[:, :, None, None, None].astype(jnp.bfloat16)
    blocks = masked.reshape(coarse_dev, groups_dev, GROUP, inputs_all, 2, spec_count)
    rows = inputs_all // lax.axis_size("tm")
    summed = lax.psum_scatter(pair_products(blocks, blocks), "tm", scatter_dimension=0, tiled=True)
    counts = kept.reshape(coarse_dev, groups_dev, GROUP).sum(-1)
    denom = frames_all * jnp.maximum(counts, 1.0)
    row_scales = lax.dynamic_slice_in_dim(scales, lax.axis_index("tm") * rows, rows, 0)
    pairs = row_scales[:, None] * scales[None, :]
    ordered = jnp.transpose(summed, (1, 2, 3, 0, 4))
    return ordered * pairs[None, None, None, :, :] / denom[:, :, None, None, None]


def shards(volts, flagged):
    owners = lax.axis_size("station")
    frames = volts.shape[3] // SUBBAND_COUNT
    fits = (
        volts.shape[1] == 1
        and volts.shape[2] % 128 == 0
        and owners % 2 == 0
        and (SUBBAND_COUNT // owners) % GROUP == 0
        and lax.axis_size("tm") == 2
        and frames % BLOCK == 0
        and frames // BLOCK > FIRST
    )
    return (pipelined if fits else plain)(volts, flagged)


def solution(mesh):
    placed = (P(None, "band", "station", "tm"), P())
    return jax.shard_map(
        shards,
        mesh=mesh,
        in_specs=placed,
        out_specs=P("band", "station", None, "tm", None),
        check_vma=False,
    )
```

```python
import functools
import math

import jax
import jax.numpy as jnp
import numpy as np
from jax import lax
from jax.experimental import pallas as pl
from jax.experimental.pallas import tpu as pltpu
from jax.sharding import PartitionSpec as P

SUBBAND_COUNT = 144
TAPS = 12
GROUP = 9
BLOCK = 16
PARTS = (1, 3)
SPREAD = BLOCK + 1
VMEM = 60 * 1024 * 1024


def window_values():
    total = TAPS * SUBBAND_COUNT
    place = np.arange(total, dtype=np.float64)
    shape = np.sinc((place - total / 2.0 + 0.5) / SUBBAND_COUNT)
    taper = 0.5 - 0.5 * np.cos(2.0 * math.pi * (place + 0.5) / total)
    return (shape * taper).reshape(TAPS, SUBBAND_COUNT).astype(np.float32)


def twiddle_values():
    f = np.arange(SUBBAND_COUNT, dtype=np.int64)[:, None]
    n = np.arange(SUBBAND_COUNT, dtype=np.int64)[None, :]
    angle = 2.0 * math.pi * (f * n % SUBBAND_COUNT) / SUBBAND_COUNT
    cosines, sines = np.cos(angle), np.sin(angle)
    real = np.concatenate([cosines, sines], 1)
    imag = np.concatenate([-sines, cosines], 1)
    return np.stack([real, imag], 1).astype(np.float32)


def front_kernel(
    splits, owners, turned, tail, keep_ref, hist_ref, volts_ref, window_ref, table_ref, *rest
):
    outs, power_ref = rest[: owners * splits], rest[owners * splits]
    tail_ref = rest[owners * splits + 1] if tail else None
    ring, filt, spread = rest[-3:]
    step = pl.program_id(0)
    now = lax.rem(step, 2)
    before = 1 - now
    inputs = ring.shape[-1]
    tiles = inputs // 128
    span = BLOCK * SUBBAND_COUNT
    skipped = (BLOCK + 1 - TAPS) * SUBBAND_COUNT

    def turn(ref, slot, begin):
        def columns(c, _):
            at = pl.multiple_of(c * 128, 128)
            for part in range(2):
                ring[slot, part, pl.ds(at, 128), :] = ref[part, 0, :, pl.ds(at, 128)].T
            return 0

        lax.fori_loop(begin, span // 128, columns, 0, unroll=6 if begin == 0 else 1)

    @pl.when(step == 0)
    def _():
        if turned:
            for part in range(2):
                ring[1, part, pl.ds(skipped, span - skipped), :] = hist_ref[part]
        else:
            turn(hist_ref, 1, skipped // 128)
        power_ref[...] = jnp.zeros_like(power_ref)

    turn(volts_ref, now, 0)
    if tail:
        for part in range(2):
            tail_ref[part] = ring[now, part, pl.ds(skipped, span - skipped), :]

    def filter_rows(j, _):
        base = pl.multiple_of(j * 16, 16)
        for tile in range(tiles):
            lanes = pl.ds(tile * 128, 128)
            weights = [window_ref[k, pl.ds(base, 16), :] for k in range(TAPS)]
            for part in range(2):
                samples = []
                for t in range(1 - TAPS, BLOCK):
                    slot, frame = (now, t) if t >= 0 else (before, BLOCK + t)
                    at = pl.multiple_of(frame * SUBBAND_COUNT + base, 16)
                    samples.append(ring[slot, part, pl.ds(at, 16), lanes].astype(jnp.float32))
                for t in range(BLOCK):
                    total = weights[0] * samples[t]
                    for k in range(1, TAPS):
                        total = total + weights[k] * samples[t + k]
                    at = pl.multiple_of(part * SUBBAND_COUNT + base, 16)
                    filt[t, pl.ds(at, 16), lanes] = total.astype(jnp.bfloat16)
        return 0

    lax.fori_loop(0, SUBBAND_COUNT // 16, filter_rows, 0)

    def transform(t, _):
        result = jnp.dot(table_ref[...], filt[t], preferred_element_type=jnp.float32)
        for tile in range(tiles):
            spread[tile, pl.ds(t, 2 * SUBBAND_COUNT, stride=SPREAD), :] = result[
                :, tile * 128 : (tile + 1) * 128
            ]
        return 0

    lax.fori_loop(0, BLOCK, transform, 0, unroll=4)

    groups = SUBBAND_COUNT // owners // GROUP
    power = [jnp.zeros((BLOCK, 128), jnp.float32) for _ in range(tiles)]
    for d in range(owners):
        for j in range(groups):
            out = outs[d * splits + j] if splits > 1 else outs[d]
            place = 0 if splits > 1 else j

            def channel(f, power, d=d, j=j, out=out, place=place):
                keep = keep_ref[(d * groups + j) * GROUP + f]
                power = list(power)
                for part in range(2):
                    row = ((d * groups + j) * 2 + part) * GROUP + f
                    for tile in range(tiles):
                        value = spread[tile, pl.ds(row * SPREAD, BLOCK), :] * keep
                        value = value.astype(jnp.bfloat16)
                        out[place, part, f, :, tile * 128 : (tile + 1) * 128] = value
                        value = value.astype(jnp.float32)
                        power[tile] = power[tile] + value * value
                return tuple(power)

            power = lax.fori_loop(0, GROUP, channel, tuple(power), unroll=3)
    for tile in range(tiles):
        power_ref[:, tile * 128 : (tile + 1) * 128] += power[tile]


def front(volts, hist, first, steps, splits, owners, keep, window, table, tail):
    inputs = volts.shape[2]
    span = BLOCK * SUBBAND_COUNT
    groups = SUBBAND_COUNT // owners // GROUP
    each = groups // splits
    frames = steps * BLOCK
    outs = [
        jax.ShapeDtypeStruct((each, 2, GROUP, frames, inputs), jnp.bfloat16)
        for _ in range(owners * splits)
    ]
    out_specs = [
        pl.BlockSpec((each, 2, GROUP, BLOCK, inputs), lambda s: (0, 0, 0, s, 0))
        for _ in range(owners * splits)
    ]
    outs.append(jax.ShapeDtypeStruct((BLOCK, inputs), jnp.float32))
    out_specs.append(pl.BlockSpec((BLOCK, inputs), lambda s: (0, 0)))
    kept = (TAPS - 1) * SUBBAND_COUNT
    if tail:
        outs.append(jax.ShapeDtypeStruct((2, kept, inputs), jnp.bfloat16))
        out_specs.append(pl.BlockSpec((2, kept, inputs), lambda s: (0, 0, 0)))
    if hist is None:
        hist, hist_spec = volts, pl.BlockSpec((2, 1, inputs, span), lambda s: (0, 0, 0, first - 1))
        turned = False
    else:
        hist_spec, turned = pl.BlockSpec((2, kept, inputs), lambda s: (0, 0, 0)), True
    macs = 2 * SUBBAND_COUNT * frames * inputs * 2 * SUBBAND_COUNT
    result = pl.pallas_call(
        functools.partial(front_kernel, splits, owners, turned, tail),
        grid=(steps,),
        out_shape=outs,
        in_specs=[
            pl.BlockSpec(memory_space=pltpu.SMEM),
            hist_spec,
            pl.BlockSpec((2, 1, inputs, span), lambda s: (0, 0, 0, first + s)),
            pl.BlockSpec(window.shape, lambda s: (0, 0, 0)),
            pl.BlockSpec(table.shape, lambda s: (0, 0)),
        ],
        out_specs=out_specs,
        scratch_shapes=[
            pltpu.VMEM((2, 2, span, inputs), jnp.bfloat16),
            pltpu.VMEM((BLOCK, 2 * SUBBAND_COUNT, inputs), jnp.bfloat16),
            pltpu.VMEM((inputs // 128, 2 * SUBBAND_COUNT * SPREAD, 128), jnp.float32),
        ],
        compiler_params=pltpu.CompilerParams(vmem_limit_bytes=VMEM),
        cost_estimate=pl.CostEstimate(
            flops=2 * macs * 4, bytes_accessed=2 * frames * SUBBAND_COUNT * inputs * 8, transcendentals=0
        ),
        name="front",
    )(keep, hist, volts, window, table)
    count = owners * splits
    return result[:count], result[count], result[count + 1] if tail else None


def after_kernel(value_ref, other_ref, out_ref):
    pass


def after(value, other):
    anywhere = pl.BlockSpec(memory_space=pl.ANY)
    return pl.pallas_call(
        after_kernel,
        out_shape=jax.ShapeDtypeStruct(value.shape, value.dtype),
        in_specs=[anywhere, anywhere],
        out_specs=anywhere,
        input_output_aliases={0: 0},
        cost_estimate=pl.CostEstimate(flops=0, bytes_accessed=0, transcendentals=0),
        name="after",
    )(value, other)


def correlate_kernel(owners, picks, place_ref, *rest):
    count = len(picks)
    pieces = [rest[n * owners : (n + 1) * owners] for n in range(count)]
    out_ref, held, turned, sems = rest[-4:]
    me, half = place_ref[0], place_ref[1]
    column = pl.program_id(0)
    per_half = owners // 2
    inputs, depth = turned.shape[2], held.shape[2]

    @pl.when(column == 0)
    def _():
        copies = []
        for d in range(owners):
            source = lax.rem(me - d + owners, owners)
            at = 0
            for n in range(count):
                size = pieces[n][d].shape[2]
                copies.append(
                    pltpu.make_async_copy(
                        pieces[n][d].at[picks[n]], held.at[source, :, pl.ds(at, size)], sems.at[n, d]
                    )
                )
                at += size
        for copy in copies:
            copy.start()
        for copy in copies:
            copy.wait()
        for r in range(per_half):
            real = held[half * per_half + r, 0].T
            imag = held[half * per_half + r, 1].T
            turned[0, r, :, pl.ds(0, depth)] = real
            turned[0, r, :, pl.ds(depth, depth)] = imag
            turned[1, r, :, pl.ds(0, depth)] = imag
            turned[1, r, :, pl.ds(depth, depth)] = -real

    left = turned[...].reshape(2 * per_half * inputs, 2 * depth)
    right = held[column].reshape(2 * depth, inputs)
    both = jnp.dot(left, right, preferred_element_type=jnp.float32)
    out_ref[...] = both.reshape(2, per_half * inputs, inputs).astype(out_ref.dtype)


def correlate(place, pieces, picks, dtype, earlier):
    owners = len(pieces[0])
    inputs = pieces[0][0].shape[-1]
    depth = sum(piece[0].shape[2] for piece in pieces)
    rows = owners // 2 * inputs
    operands = [value for piece in pieces for value in piece]
    if earlier is not None:
        operands.append(earlier)
    anywhere = pl.BlockSpec(memory_space=pl.ANY)
    return pl.pallas_call(
        functools.partial(correlate_kernel, owners, picks),
        grid=(owners,),
        out_shape=jax.ShapeDtypeStruct((2, rows, owners * inputs), dtype),
        in_specs=[pl.BlockSpec(memory_space=pltpu.SMEM)] + [anywhere] * len(operands),
        out_specs=pl.BlockSpec((2, rows, inputs), lambda b: (0, 0, b)),
        scratch_shapes=[
            pltpu.VMEM((owners, 2, depth, inputs), jnp.bfloat16),
            pltpu.VMEM((2, owners // 2, inputs, 2 * depth), jnp.bfloat16),
            pltpu.SemaphoreType.DMA((len(pieces), owners)),
        ],
        compiler_params=pltpu.CompilerParams(vmem_limit_bytes=VMEM),
        cost_estimate=pl.CostEstimate(
            flops=8 * rows * owners * inputs * depth,
            bytes_accessed=owners * 4 * depth * inputs + 8 * rows * owners * inputs,
            transcendentals=0,
        ),
        name="correlate",
    )(place, *operands)


def equalize_kernel(rows_ref, columns_ref, mine_ref, theirs_ref, *rest):
    out_ref = rest[-1]
    scale = rows_ref[...] * columns_ref[...]
    for part in range(2):
        total = mine_ref[part] + theirs_ref[part].astype(jnp.float32)
        out_ref[0, part] = total * scale


def equalize(row_scales, column_scales, mine, theirs, out, group, groups):
    rows, columns = mine.shape[1:]
    block = rows // 4
    specs = [
        pl.BlockSpec((block, 1), lambda r: (r, 0)),
        pl.BlockSpec((1, columns), lambda r: (0, 0)),
        pl.BlockSpec((2, block, columns), lambda r: (0, r, 0)),
        pl.BlockSpec((2, block, columns), lambda r: (0, r, 0)),
    ]
    operands = [row_scales, column_scales, mine, theirs]
    aliases = {}
    if out is not None:
        specs.append(pl.BlockSpec(memory_space=pl.ANY))
        operands.append(out)
        aliases = {4: 0}
    return pl.pallas_call(
        equalize_kernel,
        grid=(rows // block,),
        out_shape=jax.ShapeDtypeStruct((groups, 2, rows, columns), jnp.float32),
        in_specs=specs,
        out_specs=pl.BlockSpec((1, 2, block, columns), lambda r: (group, 0, r, 0)),
        input_output_aliases=aliases,
        compiler_params=pltpu.CompilerParams(vmem_limit_bytes=VMEM),
        cost_estimate=pl.CostEstimate(
            flops=6 * rows * columns, bytes_accessed=20 * rows * columns, transcendentals=0
        ),
        name="equalize",
    )(*operands)


def shift(value, d):
    count = lax.axis_size("station")
    return lax.ppermute(value, "station", [(s, (s + d) % count) for s in range(count)])


def passed_on(value):
    count = lax.axis_size("tm")
    return lax.ppermute(value, "tm", [(s, s + 1) for s in range(count - 1)])


def keep_table(flagged):
    fine = jnp.arange(SUBBAND_COUNT, dtype=jnp.int32)
    return jnp.all(flagged[:, :, None] != fine[None, None, :], axis=1).astype(jnp.float32)


def pipelined(volts, flagged):
    owners = lax.axis_size("station")
    me = lax.axis_index("station")
    half = lax.axis_index("tm")
    inputs = volts.shape[2]
    frames = volts.shape[3] // SUBBAND_COUNT
    frames_all = frames * lax.axis_size("tm")
    fine = SUBBAND_COUNT // owners
    groups = fine // GROUP
    blocks = frames // BLOCK

    keep_all = keep_table(flagged)
    keep_mine = lax.dynamic_index_in_dim(keep_all, lax.axis_index("band"), 0, keepdims=False)
    twice = jnp.concatenate([keep_mine, keep_mine])
    keep_ahead = lax.dynamic_slice_in_dim(twice, me * fine, SUBBAND_COUNT, 0)

    rows = twiddle_values().reshape(owners, groups, GROUP, 2, 2 * SUBBAND_COUNT)
    rows = rows.transpose(0, 1, 3, 2, 4).reshape(2 * SUBBAND_COUNT, 2 * SUBBAND_COUNT)
    rows = jnp.asarray(np.concatenate([rows, rows], 0)).astype(jnp.bfloat16)
    table = lax.dynamic_slice_in_dim(rows, me * 2 * fine, 2 * SUBBAND_COUNT, 0)
    window = jnp.broadcast_to(
        jnp.asarray(window_values())[:, :, None], (TAPS, SUBBAND_COUNT, 128)
    )

    parts, power, halo, end = [], [], None, blocks
    for size in PARTS:
        end -= size
        spectra, part_power, tail = front(
            volts, None, end, size, 1, owners, keep_ahead, window, table, halo is None
        )
        if tail is not None:
            halo = passed_on(tail)
        parts.append([x.reshape(groups, 2, GROUP * size * BLOCK, inputs) for x in spectra])
        power.append(part_power)
    spectra, part_power, _ = front(
        volts, halo, 0, end, groups, owners, keep_ahead, window, table, False
    )
    power.append(part_power)
    spectra = [x.reshape(1, 2, GROUP * end * BLOCK, inputs) for x in spectra]
    for j in range(groups):
        parts.append([spectra[d * groups + j] for d in range(owners)])

    arrived = []
    for n, part in enumerate(parts):
        got = [part[0]]
        for d in range(1, owners):
            value = part[d] if n < 2 else after(part[d], arrived[n - 2][d])
            got.append(shift(value, d))
        arrived.append(got)

    local = jnp.sum(sum(power), axis=0)
    total = lax.psum(local, ("band", "tm"))
    scale = lax.rsqrt(total / (frames_all * jnp.sum(keep_all)) + 1e-06)
    scales = lax.all_gather(scale, "station", axis=0, tiled=True)
    kept = lax.dynamic_slice_in_dim(keep_mine, me * fine, fine, 0)
    counts = kept.reshape(groups, GROUP).sum(-1)
    denom = frames_all * jnp.maximum(counts, 1.0)
    per_half = scales.shape[0] // 2
    row_scales = lax.dynamic_slice_in_dim(scales, half * per_half, per_half, 0)

    other = [(0, 1), (1, 0)]
    send_place = jnp.stack([me, 1 - half]).astype(jnp.int32)
    mine_place = jnp.stack([me, half]).astype(jnp.int32)
    out = None
    shared = len(PARTS)
    for j in range(groups):
        pieces = arrived[:shared] + [arrived[shared + j]]
        picks = (j,) * shared + (0,)
        theirs = correlate(send_place, pieces, picks, jnp.bfloat16, out)
        theirs = lax.ppermute(theirs, "tm", other)
        mine = correlate(mine_place, pieces, picks, jnp.float32, None)
        out = equalize(
            (row_scales / denom[j])[:, None], scales[None, :], mine, theirs, out, j, groups
        )
    return out[None]


def twiddle_table():
    values = twiddle_values().transpose(2, 1, 0)
    return jnp.asarray(values).astype(jnp.bfloat16)


def pair_products(left, right):
    swapped = jnp.stack([left[..., 1, :], -left[..., 0, :]], 4)
    real = jnp.einsum("cgfird,cgfjrd->icgj", left, right, preferred_element_type=jnp.float32)
    imag = jnp.einsum("cgfird,cgfjrd->icgj", swapped, right, preferred_element_type=jnp.float32)
    return jnp.stack([real, imag], 3)


def plain(volts, flagged):
    coarse_dev = volts.shape[1]
    inputs_dev = volts.shape[2]
    spec_count = volts.shape[3] // SUBBAND_COUNT
    frames_all = spec_count * lax.axis_size("tm")
    frames = volts.reshape(2, coarse_dev, inputs_dev, spec_count, SUBBAND_COUNT)
    history = passed_on(frames[:, :, :, spec_count - (TAPS - 1) :, :])
    padded = jnp.concatenate([history, frames], 3)
    window = jnp.asarray(window_values())
    filtered = jnp.zeros((2, coarse_dev, inputs_dev, spec_count, SUBBAND_COUNT), jnp.float32)
    for tap in range(TAPS):
        filtered = filtered + window[tap] * padded[:, :, :, tap : tap + spec_count, :].astype(
            jnp.float32
        )
    filtered = filtered.astype(jnp.bfloat16)
    joined = jnp.concatenate([filtered[0], filtered[1]], -1)
    spectra = jnp.einsum(
        "nqvx,xdl->nlqdv", joined, twiddle_table(), preferred_element_type=jnp.float32
    ).astype(jnp.bfloat16)
    keep_all = keep_table(flagged)
    keep_mine = lax.dynamic_slice_in_dim(
        keep_all, lax.axis_index("band") * coarse_dev, coarse_dev, 0
    )
    values = spectra.astype(jnp.float32)
    local = jnp.sum(values * values * keep_mine[:, :, None, None, None], axis=(0, 1, 3, 4))
    total = lax.psum(local, ("band", "tm"))
    scale = lax.rsqrt(total / (frames_all * jnp.sum(keep_all)) + 1e-06)
    scales = lax.all_gather(scale, "station", axis=0, tiled=True)
    received = lax.all_to_all(spectra, "station", split_axis=1, concat_axis=2, tiled=True)
    fine_dev = received.shape[1]
    inputs_all = received.shape[2]
    kept = lax.dynamic_slice_in_dim(keep_mine, lax.axis_index("station") * fine_dev, fine_dev, 1)
    groups_dev = fine_dev // GROUP
    masked = received * kept[:, :, None, None, None].astype(jnp.bfloat16)
    blocks = masked.reshape(coarse_dev, groups_dev, GROUP, inputs_all, 2, spec_count)
    rows = inputs_all // lax.axis_size("tm")
    summed = lax.psum_scatter(pair_products(blocks, blocks), "tm", scatter_dimension=0, tiled=True)
    counts = kept.reshape(coarse_dev, groups_dev, GROUP).sum(-1)
    denom = frames_all * jnp.maximum(counts, 1.0)
    row_scales = lax.dynamic_slice_in_dim(scales, lax.axis_index("tm") * rows, rows, 0)
    pairs = row_scales[:, None] * scales[None, :]
    ordered = jnp.transpose(summed, (1, 2, 3, 0, 4))
    return ordered * pairs[None, None, None, :, :] / denom[:, :, None, None, None]


def shards(volts, flagged):
    owners = lax.axis_size("station")
    frames = volts.shape[3] // SUBBAND_COUNT
    fits = (
        volts.shape[1] == 1
        and volts.shape[2] % 128 == 0
        and owners % 2 == 0
        and (SUBBAND_COUNT // owners) % GROUP == 0
        and lax.axis_size("tm") == 2
        and frames % BLOCK == 0
        and frames // BLOCK > sum(PARTS)
    )
    return (pipelined if fits else plain)(volts, flagged)


def solution(mesh):
    placed = (P(None, "band", "station", "tm"), P())
    return jax.shard_map(
        shards,
        mesh=mesh,
        in_specs=placed,
        out_specs=P("band", "station", None, "tm", None),
        check_vma=False,
    )
```

```python
import functools
import math

import jax
import jax.numpy as jnp
import numpy as np
from jax import lax
from jax.experimental import pallas as pl
from jax.experimental.pallas import tpu as pltpu
from jax.sharding import PartitionSpec as P

SUBBAND_COUNT = 144
TAPS = 12
GROUP = 9
BLOCK = 16
PARTS = (1, 3)
SPREAD = BLOCK + 1
VMEM = 60 * 1024 * 1024
COST = pl.CostEstimate(flops=1024, bytes_accessed=1024, transcendentals=0)
IN_FLIGHT = 3


def window_values():
    total = TAPS * SUBBAND_COUNT
    place = np.arange(total, dtype=np.float64)
    shape = np.sinc((place - total / 2.0 + 0.5) / SUBBAND_COUNT)
    taper = 0.5 - 0.5 * np.cos(2.0 * math.pi * (place + 0.5) / total)
    return (shape * taper).reshape(TAPS, SUBBAND_COUNT).astype(np.float32)


def twiddle_values():
    f = np.arange(SUBBAND_COUNT, dtype=np.int64)[:, None]
    n = np.arange(SUBBAND_COUNT, dtype=np.int64)[None, :]
    angle = 2.0 * math.pi * (f * n % SUBBAND_COUNT) / SUBBAND_COUNT
    cosines, sines = np.cos(angle), np.sin(angle)
    real = np.concatenate([cosines, sines], 1)
    imag = np.concatenate([-sines, cosines], 1)
    return np.stack([real, imag], 1).astype(np.float32)


def front_kernel(
    splits, owners, turned, tail, keep_ref, hist_ref, volts_ref, window_ref, table_ref, *rest
):
    outs, power_ref = rest[: owners * splits], rest[owners * splits]
    tail_ref = rest[owners * splits + 1] if tail else None
    ring, filt, spread = rest[-3:]
    step = pl.program_id(0)
    now = lax.rem(step, 2)
    before = 1 - now
    inputs = ring.shape[-1]
    tiles = inputs // 128
    span = BLOCK * SUBBAND_COUNT
    skipped = (BLOCK + 1 - TAPS) * SUBBAND_COUNT

    def turn(ref, slot, begin):
        def columns(c, _):
            at = pl.multiple_of(c * 128, 128)
            for part in range(2):
                ring[slot, part, pl.ds(at, 128), :] = ref[part, 0, :, pl.ds(at, 128)].T
            return 0

        lax.fori_loop(begin, span // 128, columns, 0, unroll=6 if begin == 0 else 1)

    @pl.when(step == 0)
    def _():
        if turned:
            for part in range(2):
                ring[1, part, pl.ds(skipped, span - skipped), :] = hist_ref[part]
        else:
            turn(hist_ref, 1, skipped // 128)
        power_ref[...] = jnp.zeros_like(power_ref)

    turn(volts_ref, now, 0)
    if tail:
        for part in range(2):
            tail_ref[part] = ring[now, part, pl.ds(skipped, span - skipped), :]

    def filter_rows(j, _):
        base = pl.multiple_of(j * 16, 16)
        for tile in range(tiles):
            lanes = pl.ds(tile * 128, 128)
            weights = [window_ref[k, pl.ds(base, 16), :] for k in range(TAPS)]
            for part in range(2):
                samples = []
                for t in range(1 - TAPS, BLOCK):
                    slot, frame = (now, t) if t >= 0 else (before, BLOCK + t)
                    at = pl.multiple_of(frame * SUBBAND_COUNT + base, 16)
                    samples.append(ring[slot, part, pl.ds(at, 16), lanes].astype(jnp.float32))
                for t in range(BLOCK):
                    total = weights[0] * samples[t]
                    for k in range(1, TAPS):
                        total = total + weights[k] * samples[t + k]
                    at = pl.multiple_of(part * SUBBAND_COUNT + base, 16)
                    filt[t, pl.ds(at, 16), lanes] = total.astype(jnp.bfloat16)
        return 0

    lax.fori_loop(0, SUBBAND_COUNT // 16, filter_rows, 0)

    def transform(t, _):
        result = jnp.dot(table_ref[...], filt[t], preferred_element_type=jnp.float32)
        for tile in range(tiles):
            spread[tile, pl.ds(t, 2 * SUBBAND_COUNT, stride=SPREAD), :] = result[
                :, tile * 128 : (tile + 1) * 128
            ]
        return 0

    lax.fori_loop(0, BLOCK, transform, 0, unroll=4)

    groups = SUBBAND_COUNT // owners // GROUP
    power = [jnp.zeros((BLOCK, 128), jnp.float32) for _ in range(tiles)]
    for d in range(owners):
        for j in range(groups):
            out = outs[d * splits + j] if splits > 1 else outs[d]
            place = 0 if splits > 1 else j

            def channel(f, power, d=d, j=j, out=out, place=place):
                keep = keep_ref[(d * groups + j) * GROUP + f]
                power = list(power)
                for part in range(2):
                    row = ((d * groups + j) * 2 + part) * GROUP + f
                    for tile in range(tiles):
                        value = spread[tile, pl.ds(row * SPREAD, BLOCK), :] * keep
                        value = value.astype(jnp.bfloat16)
                        out[place, part, f, :, tile * 128 : (tile + 1) * 128] = value
                        value = value.astype(jnp.float32)
                        power[tile] = power[tile] + value * value
                return tuple(power)

            power = lax.fori_loop(0, GROUP, channel, tuple(power), unroll=3)
    for tile in range(tiles):
        power_ref[:, tile * 128 : (tile + 1) * 128] += power[tile]


def front(volts, hist, first, steps, splits, owners, keep, window, table, tail):
    inputs = volts.shape[2]
    span = BLOCK * SUBBAND_COUNT
    groups = SUBBAND_COUNT // owners // GROUP
    each = groups // splits
    frames = steps * BLOCK
    outs = [
        jax.ShapeDtypeStruct((each, 2, GROUP, frames, inputs), jnp.bfloat16)
        for _ in range(owners * splits)
    ]
    out_specs = [
        pl.BlockSpec((each, 2, GROUP, BLOCK, inputs), lambda s: (0, 0, 0, s, 0))
        for _ in range(owners * splits)
    ]
    outs.append(jax.ShapeDtypeStruct((BLOCK, inputs), jnp.float32))
    out_specs.append(pl.BlockSpec((BLOCK, inputs), lambda s: (0, 0)))
    kept = (TAPS - 1) * SUBBAND_COUNT
    if tail:
        outs.append(jax.ShapeDtypeStruct((2, kept, inputs), jnp.bfloat16))
        out_specs.append(pl.BlockSpec((2, kept, inputs), lambda s: (0, 0, 0)))
    if hist is None:
        hist, hist_spec = volts, pl.BlockSpec((2, 1, inputs, span), lambda s: (0, 0, 0, first - 1))
        turned = False
    else:
        hist_spec, turned = pl.BlockSpec((2, kept, inputs), lambda s: (0, 0, 0)), True
    result = pl.pallas_call(
        functools.partial(front_kernel, splits, owners, turned, tail),
        grid=(steps,),
        out_shape=outs,
        in_specs=[
            pl.BlockSpec(memory_space=pltpu.SMEM),
            hist_spec,
            pl.BlockSpec((2, 1, inputs, span), lambda s: (0, 0, 0, first + s)),
            pl.BlockSpec(window.shape, lambda s: (0, 0, 0)),
            pl.BlockSpec(table.shape, lambda s: (0, 0)),
        ],
        out_specs=out_specs,
        scratch_shapes=[
            pltpu.VMEM((2, 2, span, inputs), jnp.bfloat16),
            pltpu.VMEM((BLOCK, 2 * SUBBAND_COUNT, inputs), jnp.bfloat16),
            pltpu.VMEM((inputs // 128, 2 * SUBBAND_COUNT * SPREAD, 128), jnp.float32),
        ],
        compiler_params=pltpu.CompilerParams(vmem_limit_bytes=VMEM),
        cost_estimate=COST,
        name="front",
    )(keep, hist, volts, window, table)
    count = owners * splits
    return result[:count], result[count], result[count + 1] if tail else None


def after_kernel(*refs):
    pass


def after(value, *others):
    anywhere = pl.BlockSpec(memory_space=pl.ANY)
    return pl.pallas_call(
        after_kernel,
        out_shape=jax.ShapeDtypeStruct(value.shape, value.dtype),
        in_specs=[anywhere] * (1 + len(others)),
        out_specs=anywhere,
        input_output_aliases={0: 0},
        cost_estimate=COST,
        name="after",
    )(value, *others)


def correlate_kernel(owners, picks, outs, place_ref, *rest):
    count = len(picks)
    pieces = [rest[n * owners : (n + 1) * owners] for n in range(count)]
    out_refs, (held, turned, sems) = rest[-3 - outs : -3], rest[-3:]
    me = place_ref[0]
    column = pl.program_id(0)
    per_half = owners // 2
    inputs, depth = turned.shape[3], held.shape[2]

    @pl.when(column == 0)
    def _():
        copies = []
        for d in range(owners):
            source = lax.rem(me - d + owners, owners)
            at = 0
            for n in range(count):
                size = pieces[n][d].shape[2]
                copies.append(
                    pltpu.make_async_copy(
                        pieces[n][d].at[picks[n]], held.at[source, :, pl.ds(at, size)], sems.at[n, d]
                    )
                )
                at += size
        for copy in copies:
            copy.start()
        for copy in copies:
            copy.wait()
        for h in range(outs):
            for r in range(per_half):
                source = place_ref[1 + h] * per_half + r
                real, imag = held[source, 0].T, held[source, 1].T
                turned[h, 0, r, :, pl.ds(0, depth)] = real
                turned[h, 0, r, :, pl.ds(depth, depth)] = imag
                turned[h, 1, r, :, pl.ds(0, depth)] = imag
                turned[h, 1, r, :, pl.ds(depth, depth)] = -real

    right = held[column].reshape(2 * depth, inputs)
    for h in range(outs):
        left = turned[h].reshape(2 * per_half * inputs, 2 * depth)
        both = jnp.dot(left, right, preferred_element_type=jnp.float32)
        both = both.reshape(2, per_half * inputs, inputs)
        out_refs[h][...] = both.astype(out_refs[h].dtype)


def correlate(place, pieces, picks, dtypes, earlier):
    owners = len(pieces[0])
    inputs = pieces[0][0].shape[-1]
    depth = sum(piece[0].shape[2] for piece in pieces)
    rows = owners // 2 * inputs
    operands = [value for piece in pieces for value in piece] + list(earlier)
    anywhere = pl.BlockSpec(memory_space=pl.ANY)
    outs = len(dtypes)
    return pl.pallas_call(
        functools.partial(correlate_kernel, owners, picks, outs),
        grid=(owners,),
        out_shape=[jax.ShapeDtypeStruct((2, rows, owners * inputs), dtype) for dtype in dtypes],
        in_specs=[pl.BlockSpec(memory_space=pltpu.SMEM)] + [anywhere] * len(operands),
        out_specs=[pl.BlockSpec((2, rows, inputs), lambda b: (0, 0, b))] * outs,
        scratch_shapes=[
            pltpu.VMEM((owners, 2, depth, inputs), jnp.bfloat16),
            pltpu.VMEM((outs, 2, owners // 2, inputs, 2 * depth), jnp.bfloat16),
            pltpu.SemaphoreType.DMA((len(pieces), owners)),
        ],
        compiler_params=pltpu.CompilerParams(vmem_limit_bytes=VMEM),
        cost_estimate=COST,
        name="correlate",
    )(place, *operands)


def equalize_kernel(rows_ref, columns_ref, mine_ref, theirs_ref, *rest):
    out_ref = rest[-1]
    scale = rows_ref[...] * columns_ref[...]
    for part in range(2):
        total = mine_ref[part] + theirs_ref[part].astype(jnp.float32)
        out_ref[0, part] = total * scale


def equalize(row_scales, column_scales, mine, theirs, out, group, groups, waits):
    rows, columns = mine.shape[1:]
    block = rows // 4
    specs = [
        pl.BlockSpec((block, 1), lambda r: (r, 0)),
        pl.BlockSpec((1, columns), lambda r: (0, 0)),
        pl.BlockSpec((2, block, columns), lambda r: (0, r, 0)),
        pl.BlockSpec((2, block, columns), lambda r: (0, r, 0)),
    ]
    operands = [row_scales, column_scales, mine, theirs]
    aliases = {}
    if out is not None:
        specs.append(pl.BlockSpec(memory_space=pl.ANY))
        operands.append(out)
        aliases = {4: 0}
    specs += [pl.BlockSpec(memory_space=pl.ANY)] * len(waits)
    operands += waits
    return pl.pallas_call(
        equalize_kernel,
        grid=(rows // block,),
        out_shape=jax.ShapeDtypeStruct((groups, 2, rows, columns), jnp.float32),
        in_specs=specs,
        out_specs=pl.BlockSpec((1, 2, block, columns), lambda r: (group, 0, r, 0)),
        input_output_aliases=aliases,
        compiler_params=pltpu.CompilerParams(vmem_limit_bytes=VMEM),
        cost_estimate=COST,
        name="equalize",
    )(*operands)


def shift(value, d):
    count = lax.axis_size("station")
    return lax.ppermute(value, "station", [(s, (s + d) % count) for s in range(count)])


def passed_on(value):
    count = lax.axis_size("tm")
    return lax.ppermute(value, "tm", [(s, s + 1) for s in range(count - 1)])


def keep_table(flagged):
    fine = jnp.arange(SUBBAND_COUNT, dtype=jnp.int32)
    return jnp.all(flagged[:, :, None] != fine[None, None, :], axis=1).astype(jnp.float32)


def pipelined(volts, flagged):
    owners = lax.axis_size("station")
    me = lax.axis_index("station")
    half = lax.axis_index("tm")
    inputs = volts.shape[2]
    frames = volts.shape[3] // SUBBAND_COUNT
    frames_all = frames * lax.axis_size("tm")
    fine = SUBBAND_COUNT // owners
    groups = fine // GROUP
    blocks = frames // BLOCK

    keep_all = keep_table(flagged)
    keep_mine = lax.dynamic_index_in_dim(keep_all, lax.axis_index("band"), 0, keepdims=False)
    twice = jnp.concatenate([keep_mine, keep_mine])
    keep_ahead = lax.dynamic_slice_in_dim(twice, me * fine, SUBBAND_COUNT, 0)

    rows = twiddle_values().reshape(owners, groups, GROUP, 2, 2 * SUBBAND_COUNT)
    rows = rows.transpose(0, 1, 3, 2, 4).reshape(2 * SUBBAND_COUNT, 2 * SUBBAND_COUNT)
    rows = jnp.asarray(np.concatenate([rows, rows], 0)).astype(jnp.bfloat16)
    table = lax.dynamic_slice_in_dim(rows, me * 2 * fine, 2 * SUBBAND_COUNT, 0)
    window = jnp.broadcast_to(
        jnp.asarray(window_values())[:, :, None], (TAPS, SUBBAND_COUNT, 128)
    )

    parts, power, halo, end = [], [], None, blocks
    for size in PARTS:
        end -= size
        spectra, part_power, tail = front(
            volts, None, end, size, 1, owners, keep_ahead, window, table, halo is None
        )
        if tail is not None:
            with jax.named_scope("halo"):
                halo = passed_on(tail)
        parts.append([x.reshape(groups, 2, GROUP * size * BLOCK, inputs) for x in spectra])
        power.append(part_power)
    spectra, part_power, _ = front(
        volts, halo, 0, end, groups, owners, keep_ahead, window, table, False
    )
    power.append(part_power)
    spectra = [x.reshape(1, 2, GROUP * end * BLOCK, inputs) for x in spectra]
    for j in range(groups):
        parts.append([spectra[d * groups + j] for d in range(owners)])

    local = jnp.sum(sum(power), axis=0)
    total = lax.psum(local, ("band", "tm"))
    scale = lax.rsqrt(total / (frames_all * jnp.sum(keep_all)) + 1e-06)
    scales = lax.all_gather(scale, "station", axis=0, tiled=True)
    kept = lax.dynamic_slice_in_dim(keep_mine, me * fine, fine, 0)
    counts = kept.reshape(groups, GROUP).sum(-1)
    denom = frames_all * jnp.maximum(counts, 1.0)
    per_half = scales.shape[0] // 2
    row_scales = lax.dynamic_slice_in_dim(scales, half * per_half, per_half, 0)

    column_scales = scales[None, :]
    row_scales = [(row_scales / denom[j])[:, None] for j in range(groups)]

    place = jnp.stack([me, 1 - half, half]).astype(jnp.int32)
    shared = len(PARTS)
    arrived, flat, out = [], [], None

    def send(n, waits):
        got = [parts[n][0]]
        for d in range(1, owners):
            gates = list(waits.get(d, ()))
            if len(flat) >= IN_FLIGHT:
                gates.append(flat[len(flat) - IN_FLIGHT])
            value = after(parts[n][d], *gates) if gates else parts[n][d]
            with jax.named_scope(f"part{n}_shift{d}"):
                got.append(shift(value, d))
            flat.append(got[-1])
        arrived.append(got)

    def to_other(j, theirs):
        with jax.named_scope(f"rows{j}"):
            return lax.ppermute(theirs, "tm", [(0, 1), (1, 0)])

    def multiply(j, place, dtypes, earlier):
        pieces = arrived[:shared] + [arrived[shared + j]]
        return correlate(place, pieces, (j,) * shared + (0,), dtypes, earlier)

    for n in range(shared):
        send(n, {})
    send(shared, {owners - 1: [column_scales]})
    waiting = None
    for j in range(groups):
        final = j + 1 == groups
        if not final:
            send(shared + j + 1, {})
            theirs, mine = multiply(j, place, [jnp.bfloat16, jnp.float32], [])
        else:
            (theirs,) = multiply(j, place[:2], [jnp.bfloat16], [])
        if waiting is not None:
            out = equalize(*waiting, out, j - 1, groups, [theirs])
        if final:
            theirs = to_other(j, theirs)
            (mine,) = multiply(j, place[::2], [jnp.float32], [])
        else:
            theirs = to_other(j, after(theirs, *arrived[shared + j + 1][1:]))
        waiting = (row_scales[j], column_scales, mine, theirs)
    out = equalize(*waiting, out, groups - 1, groups, [])
    return out[None]


def twiddle_table():
    values = twiddle_values().transpose(2, 1, 0)
    return jnp.asarray(values).astype(jnp.bfloat16)


def pair_products(left, right):
    swapped = jnp.stack([left[..., 1, :], -left[..., 0, :]], 4)
    real = jnp.einsum("cgfird,cgfjrd->icgj", left, right, preferred_element_type=jnp.float32)
    imag = jnp.einsum("cgfird,cgfjrd->icgj", swapped, right, preferred_element_type=jnp.float32)
    return jnp.stack([real, imag], 3)


def plain(volts, flagged):
    coarse_dev = volts.shape[1]
    inputs_dev = volts.shape[2]
    spec_count = volts.shape[3] // SUBBAND_COUNT
    frames_all = spec_count * lax.axis_size("tm")
    frames = volts.reshape(2, coarse_dev, inputs_dev, spec_count, SUBBAND_COUNT)
    history = passed_on(frames[:, :, :, spec_count - (TAPS - 1) :, :])
    padded = jnp.concatenate([history, frames], 3)
    window = jnp.asarray(window_values())
    filtered = jnp.zeros((2, coarse_dev, inputs_dev, spec_count, SUBBAND_COUNT), jnp.float32)
    for tap in range(TAPS):
        filtered = filtered + window[tap] * padded[:, :, :, tap : tap + spec_count, :].astype(
            jnp.float32
        )
    filtered = filtered.astype(jnp.bfloat16)
    joined = jnp.concatenate([filtered[0], filtered[1]], -1)
    spectra = jnp.einsum(
        "nqvx,xdl->nlqdv", joined, twiddle_table(), preferred_element_type=jnp.float32
    ).astype(jnp.bfloat16)
    keep_all = keep_table(flagged)
    keep_mine = lax.dynamic_slice_in_dim(
        keep_all, lax.axis_index("band") * coarse_dev, coarse_dev, 0
    )
    values = spectra.astype(jnp.float32)
    local = jnp.sum(values * values * keep_mine[:, :, None, None, None], axis=(0, 1, 3, 4))
    total = lax.psum(local, ("band", "tm"))
    scale = lax.rsqrt(total / (frames_all * jnp.sum(keep_all)) + 1e-06)
    scales = lax.all_gather(scale, "station", axis=0, tiled=True)
    received = lax.all_to_all(spectra, "station", split_axis=1, concat_axis=2, tiled=True)
    fine_dev = received.shape[1]
    inputs_all = received.shape[2]
    kept = lax.dynamic_slice_in_dim(keep_mine, lax.axis_index("station") * fine_dev, fine_dev, 1)
    groups_dev = fine_dev // GROUP
    masked = received * kept[:, :, None, None, None].astype(jnp.bfloat16)
    blocks = masked.reshape(coarse_dev, groups_dev, GROUP, inputs_all, 2, spec_count)
    rows = inputs_all // lax.axis_size("tm")
    summed = lax.psum_scatter(pair_products(blocks, blocks), "tm", scatter_dimension=0, tiled=True)
    counts = kept.reshape(coarse_dev, groups_dev, GROUP).sum(-1)
    denom = frames_all * jnp.maximum(counts, 1.0)
    row_scales = lax.dynamic_slice_in_dim(scales, lax.axis_index("tm") * rows, rows, 0)
    pairs = row_scales[:, None] * scales[None, :]
    ordered = jnp.transpose(summed, (1, 2, 3, 0, 4))
    return ordered * pairs[None, None, None, :, :] / denom[:, :, None, None, None]


def shards(volts, flagged):
    owners = lax.axis_size("station")
    frames = volts.shape[3] // SUBBAND_COUNT
    fits = (
        volts.shape[1] == 1
        and volts.shape[2] % 128 == 0
        and owners % 2 == 0
        and (SUBBAND_COUNT // owners) % GROUP == 0
        and lax.axis_size("tm") == 2
        and frames % BLOCK == 0
        and frames // BLOCK > sum(PARTS)
    )
    return (pipelined if fits else plain)(volts, flagged)


def solution(mesh):
    placed = (P(None, "band", "station", "tm"), P())
    return jax.shard_map(
        shards,
        mesh=mesh,
        in_specs=placed,
        out_specs=P("band", "station", None, "tm", None),
        check_vma=False,
    )
```

```python
import functools
import math

import jax
import jax.numpy as jnp
import numpy as np
from jax import lax
from jax.experimental import pallas as pl
from jax.experimental.pallas import tpu as pltpu
from jax.sharding import PartitionSpec as P

SUBBAND_COUNT = 144
TAPS = 12
GROUP = 9
BLOCK = 16
PARTS = (1, 3)
SPREAD = BLOCK + 1
VMEM = 60 * 1024 * 1024
COST = pl.CostEstimate(flops=1024, bytes_accessed=1024, transcendentals=0)
IN_FLIGHT = 3


def window_values():
    total = TAPS * SUBBAND_COUNT
    place = np.arange(total, dtype=np.float64)
    shape = np.sinc((place - total / 2.0 + 0.5) / SUBBAND_COUNT)
    taper = 0.5 - 0.5 * np.cos(2.0 * math.pi * (place + 0.5) / total)
    return (shape * taper).reshape(TAPS, SUBBAND_COUNT).astype(np.float32)


def twiddle_values():
    f = np.arange(SUBBAND_COUNT, dtype=np.int64)[:, None]
    n = np.arange(SUBBAND_COUNT, dtype=np.int64)[None, :]
    angle = 2.0 * math.pi * (f * n % SUBBAND_COUNT) / SUBBAND_COUNT
    cosines, sines = np.cos(angle), np.sin(angle)
    real = np.concatenate([cosines, sines], 1)
    imag = np.concatenate([-sines, cosines], 1)
    return np.stack([real, imag], 1).astype(np.float32)


def front_kernel(
    splits, owners, turned, tail, me_ref, keep_ref, hist_ref, volts_ref, window_ref, table_ref, *rest
):
    outs, power_ref = rest[: owners * splits], rest[owners * splits]
    tail_ref = rest[owners * splits + 1] if tail else None
    ring, filt, spread = rest[-3:]
    step = pl.program_id(0)
    now = lax.rem(step, 2)
    before = 1 - now
    inputs = ring.shape[-1]
    tiles = inputs // 128
    span = BLOCK * SUBBAND_COUNT
    skipped = (BLOCK + 1 - TAPS) * SUBBAND_COUNT

    def turn(ref, slot, begin):
        def columns(c, _):
            at = pl.multiple_of(c * 128, 128)
            for part in range(2):
                ring[slot, part, pl.ds(at, 128), :] = ref[part, 0, :, pl.ds(at, 128)].T
            return 0

        lax.fori_loop(begin, span // 128, columns, 0, unroll=6 if begin == 0 else 5)

    @pl.when(step == 0)
    def _():
        if turned:
            for part in range(2):
                ring[1, part, pl.ds(skipped, span - skipped), :] = hist_ref[part]
        else:
            turn(hist_ref, 1, 3)
        power_ref[...] = jnp.zeros_like(power_ref)

    turn(volts_ref, now, 0)
    if tail:
        for part in range(2):
            tail_ref[part] = ring[now, part, pl.ds(skipped, span - skipped), :]

    def filter_rows(j, _):
        base = pl.multiple_of(j * 16, 16)
        for tile in range(tiles):
            lanes = pl.ds(tile * 128, 128)
            weights = [window_ref[k, pl.ds(base, 16), :] for k in range(TAPS)]
            for part in range(2):
                samples = []
                for t in range(1 - TAPS, BLOCK):
                    slot, frame = (now, t) if t >= 0 else (before, BLOCK + t)
                    at = pl.multiple_of(frame * SUBBAND_COUNT + base, 16)
                    samples.append(ring[slot, part, pl.ds(at, 16), lanes].astype(jnp.float32))
                for t in range(BLOCK):
                    total = weights[0] * samples[t]
                    for k in range(1, TAPS):
                        total = total + weights[k] * samples[t + k]
                    at = pl.multiple_of(part * SUBBAND_COUNT + base, 16)
                    filt[t, pl.ds(at, 16), lanes] = total.astype(jnp.bfloat16)
        return 0

    lax.fori_loop(0, SUBBAND_COUNT // 16, filter_rows, 0)

    def transform(t, _):
        result = jnp.dot(table_ref[0], filt[t], preferred_element_type=jnp.float32)
        for tile in range(tiles):
            spread[tile, pl.ds(t, 2 * SUBBAND_COUNT, stride=SPREAD), :] = result[
                :, tile * 128 : (tile + 1) * 128
            ]
        return 0

    lax.fori_loop(0, BLOCK, transform, 0, unroll=4)

    groups = SUBBAND_COUNT // owners // GROUP
    power = [jnp.zeros((BLOCK, 128), jnp.float32) for _ in range(tiles)]
    for d in range(owners):
        for j in range(groups):
            out = outs[d * splits + j] if splits > 1 else outs[d]
            place = 0 if splits > 1 else j

            def channel(f, power, d=d, j=j, out=out, place=place):
                keep = keep_ref[(d * groups + j) * GROUP + f]
                power = list(power)
                for part in range(2):
                    row = ((d * groups + j) * 2 + part) * GROUP + f
                    for tile in range(tiles):
                        value = spread[tile, pl.ds(row * SPREAD, BLOCK), :] * keep
                        value = value.astype(jnp.bfloat16)
                        out[place, part, f, :, tile * 128 : (tile + 1) * 128] = value
                        value = value.astype(jnp.float32)
                        power[tile] = power[tile] + value * value
                return tuple(power)

            power = lax.fori_loop(0, GROUP, channel, tuple(power), unroll=3)
    for tile in range(tiles):
        power_ref[:, tile * 128 : (tile + 1) * 128] += power[tile]


def front(volts, hist, first, steps, splits, owners, keep, me, window, table, tail):
    inputs = volts.shape[2]
    span = BLOCK * SUBBAND_COUNT
    groups = SUBBAND_COUNT // owners // GROUP
    each = groups // splits
    frames = steps * BLOCK
    outs = [
        jax.ShapeDtypeStruct((each, 2, GROUP, frames, inputs), jnp.bfloat16)
        for _ in range(owners * splits)
    ]
    out_specs = [
        pl.BlockSpec((each, 2, GROUP, BLOCK, inputs), lambda s, me: (0, 0, 0, s, 0))
        for _ in range(owners * splits)
    ]
    outs.append(jax.ShapeDtypeStruct((BLOCK, inputs), jnp.float32))
    out_specs.append(pl.BlockSpec((BLOCK, inputs), lambda s, me: (0, 0)))
    kept = (TAPS - 1) * SUBBAND_COUNT
    if tail:
        outs.append(jax.ShapeDtypeStruct((2, kept, inputs), jnp.bfloat16))
        out_specs.append(pl.BlockSpec((2, kept, inputs), lambda s, me: (0, 0, 0)))
    if hist is None:
        hist, hist_spec = volts, pl.BlockSpec((2, 1, inputs, span), lambda s, me: (0, 0, 0, first - 1))
        turned = False
    else:
        hist_spec, turned = pl.BlockSpec((2, kept, inputs), lambda s, me: (0, 0, 0)), True
    result = pl.pallas_call(
        functools.partial(front_kernel, splits, owners, turned, tail),
        grid_spec=pltpu.PrefetchScalarGridSpec(
            num_scalar_prefetch=1,
            grid=(steps,),
            in_specs=[
                pl.BlockSpec(memory_space=pltpu.SMEM),
                hist_spec,
                pl.BlockSpec((2, 1, inputs, span), lambda s, me: (0, 0, 0, first + s)),
                pl.BlockSpec(window.shape, lambda s, me: (0, 0, 0)),
                pl.BlockSpec((1, *table.shape[1:]), lambda s, me: (me[0], 0, 0)),
            ],
            out_specs=out_specs,
            scratch_shapes=[
                pltpu.VMEM((2, 2, span, inputs), jnp.bfloat16),
                pltpu.VMEM((BLOCK, 2 * SUBBAND_COUNT, inputs), jnp.bfloat16),
                pltpu.VMEM((inputs // 128, 2 * SUBBAND_COUNT * SPREAD, 128), jnp.float32),
            ],
        ),
        out_shape=outs,
        compiler_params=pltpu.CompilerParams(vmem_limit_bytes=VMEM),
        cost_estimate=COST,
        name="front",
    )(me, keep, hist, volts, window, table)
    count = owners * splits
    return result[:count], result[count], result[count + 1] if tail else None


def after_kernel(*refs):
    pass


def after(value, *others):
    anywhere = pl.BlockSpec(memory_space=pl.ANY)
    return pl.pallas_call(
        after_kernel,
        out_shape=jax.ShapeDtypeStruct(value.shape, value.dtype),
        in_specs=[anywhere] * (1 + len(others)),
        out_specs=anywhere,
        input_output_aliases={0: 0},
        cost_estimate=COST,
        name="after",
    )(value, *others)


def correlate_kernel(owners, picks, outs, sums, place_ref, *rest):
    count = len(picks)
    sum_refs, rest = rest[:sums], rest[sums:]
    pieces = [rest[n * owners : (n + 1) * owners] for n in range(count)]
    out_refs, (held, turned, sems) = rest[-3 - outs : -3], rest[-3:]
    me = place_ref[0]
    column = pl.program_id(0)
    per_half = owners // 2
    inputs, depth = turned.shape[3], held.shape[2]

    @pl.when(column == 0)
    def _():
        copies = []
        for d in range(owners):
            source = lax.rem(me - d + owners, owners)
            at = 0
            for n in range(count):
                size = pieces[n][d].shape[2]
                copies.append(
                    pltpu.make_async_copy(
                        pieces[n][d].at[picks[n]], held.at[source, :, pl.ds(at, size)], sems.at[n, d]
                    )
                )
                at += size
        for copy in copies:
            copy.start()
        for copy in copies:
            copy.wait()
        for h in range(outs):
            for r in range(per_half):
                source = place_ref[1 + h] * per_half + r
                real, imag = held[source, 0].T, held[source, 1].T
                turned[h, 0, r, :, pl.ds(0, depth)] = real
                turned[h, 0, r, :, pl.ds(depth, depth)] = imag
                turned[h, 1, r, :, pl.ds(0, depth)] = imag
                turned[h, 1, r, :, pl.ds(depth, depth)] = -real

    right = held[column].reshape(2 * depth, inputs)
    for h in range(outs):
        left = turned[h].reshape(2 * per_half * inputs, 2 * depth)
        both = jnp.dot(left, right, preferred_element_type=jnp.float32)
        both = both.reshape(2, per_half * inputs, inputs)
        if sums:
            both = both + sum_refs[h][...]
        out_refs[h][...] = both.astype(out_refs[h].dtype)


def correlate(place, pieces, picks, dtypes, sums, earlier):
    owners = len(pieces[0])
    inputs = pieces[0][0].shape[-1]
    depth = sum(piece[0].shape[2] for piece in pieces)
    rows = owners // 2 * inputs
    operands = [value for piece in pieces for value in piece] + list(earlier)
    columns = pl.BlockSpec((2, rows, inputs), lambda b: (0, 0, b))
    anywhere = pl.BlockSpec(memory_space=pl.ANY)
    outs = len(dtypes)
    return pl.pallas_call(
        functools.partial(correlate_kernel, owners, picks, outs, len(sums)),
        grid=(owners,),
        out_shape=[jax.ShapeDtypeStruct((2, rows, owners * inputs), dtype) for dtype in dtypes],
        in_specs=[pl.BlockSpec(memory_space=pltpu.SMEM)]
        + [columns] * len(sums)
        + [anywhere] * len(operands),
        out_specs=[columns] * outs,
        scratch_shapes=[
            pltpu.VMEM((owners, 2, depth, inputs), jnp.bfloat16),
            pltpu.VMEM((outs, 2, owners // 2, inputs, 2 * depth), jnp.bfloat16),
            pltpu.SemaphoreType.DMA((len(pieces), owners)),
        ],
        compiler_params=pltpu.CompilerParams(vmem_limit_bytes=VMEM),
        cost_estimate=COST,
        name="correlate",
    )(place, *sums, *operands)


def equalize_kernel(rows_ref, columns_ref, mine_ref, theirs_ref, *rest):
    out_ref = rest[-1]
    scale = rows_ref[...] * columns_ref[...]
    for part in range(2):
        total = mine_ref[part] + theirs_ref[part].astype(jnp.float32)
        out_ref[0, part] = total * scale


def equalize(row_scales, column_scales, mine, theirs, out, group, groups, waits):
    rows, columns = mine.shape[1:]
    block = rows // 8
    specs = [
        pl.BlockSpec((block, 1), lambda r: (r, 0)),
        pl.BlockSpec((1, columns), lambda r: (0, 0)),
        pl.BlockSpec((2, block, columns), lambda r: (0, r, 0)),
        pl.BlockSpec((2, block, columns), lambda r: (0, r, 0)),
    ]
    operands = [row_scales, column_scales, mine, theirs]
    aliases = {}
    if out is not None:
        specs.append(pl.BlockSpec(memory_space=pl.ANY))
        operands.append(out)
        aliases = {4: 0}
    specs += [pl.BlockSpec(memory_space=pl.ANY)] * len(waits)
    operands += waits
    return pl.pallas_call(
        equalize_kernel,
        grid=(rows // block,),
        out_shape=jax.ShapeDtypeStruct((groups, 2, rows, columns), jnp.float32),
        in_specs=specs,
        out_specs=pl.BlockSpec((1, 2, block, columns), lambda r: (group, 0, r, 0)),
        input_output_aliases=aliases,
        compiler_params=pltpu.CompilerParams(vmem_limit_bytes=VMEM),
        cost_estimate=COST,
        name="equalize",
    )(*operands)


def shift(value, d):
    count = lax.axis_size("station")
    return lax.ppermute(value, "station", [(s, (s + d) % count) for s in range(count)])


def passed_on(value):
    count = lax.axis_size("tm")
    return lax.ppermute(value, "tm", [(s, s + 1) for s in range(count - 1)])


def keep_table(flagged):
    fine = jnp.arange(SUBBAND_COUNT, dtype=jnp.int32)
    return jnp.all(flagged[:, :, None] != fine[None, None, :], axis=1).astype(jnp.float32)


def pipelined(volts, flagged):
    owners = lax.axis_size("station")
    me = lax.axis_index("station")
    half = lax.axis_index("tm")
    inputs = volts.shape[2]
    frames = volts.shape[3] // SUBBAND_COUNT
    frames_all = frames * lax.axis_size("tm")
    fine = SUBBAND_COUNT // owners
    groups = fine // GROUP
    blocks = frames // BLOCK

    keep_all = keep_table(flagged)
    keep_mine = lax.dynamic_index_in_dim(keep_all, lax.axis_index("band"), 0, keepdims=False)
    twice = jnp.concatenate([keep_mine, keep_mine])
    keep_ahead = lax.dynamic_slice_in_dim(twice, me * fine, SUBBAND_COUNT, 0)

    rows = twiddle_values().reshape(owners, groups, GROUP, 2, 2 * SUBBAND_COUNT)
    rows = rows.transpose(0, 1, 3, 2, 4)
    turns = [np.roll(rows, -z, 0).reshape(2 * SUBBAND_COUNT, -1) for z in range(owners)]
    table = jnp.asarray(np.stack(turns).astype(jnp.bfloat16))
    window = np.broadcast_to(window_values()[:, :, None], (TAPS, SUBBAND_COUNT, 128))
    window = jnp.asarray(np.ascontiguousarray(window))
    spot = jnp.reshape(me, (1,)).astype(jnp.int32)

    parts, power, halo, end = [], [], None, blocks
    for size in PARTS:
        end -= size
        spectra, part_power, tail = front(
            volts, None, end, size, 1, owners, keep_ahead, spot, window, table, halo is None
        )
        if tail is not None:
            with jax.named_scope("halo"):
                halo = passed_on(tail)
        parts.append([x.reshape(groups, 2, GROUP * size * BLOCK, inputs) for x in spectra])
        power.append(part_power)
    spectra, part_power, _ = front(
        volts, halo, 0, end, groups, owners, keep_ahead, spot, window, table, False
    )
    power.append(part_power)
    spectra = [x.reshape(1, 2, GROUP * end * BLOCK, inputs) for x in spectra]
    for j in range(groups):
        parts.append([spectra[d * groups + j] for d in range(owners)])

    local = jnp.sum(sum(power), axis=0)
    total = lax.psum(local, ("band", "tm"))
    scale = lax.rsqrt(total / (frames_all * jnp.sum(keep_all)) + 1e-06)
    scales = lax.all_gather(scale, "station", axis=0, tiled=True)
    kept = lax.dynamic_slice_in_dim(keep_mine, me * fine, fine, 0)
    counts = kept.reshape(groups, GROUP).sum(-1)
    denom = frames_all * jnp.maximum(counts, 1.0)
    per_half = scales.shape[0] // 2
    row_scales = lax.dynamic_slice_in_dim(scales, half * per_half, per_half, 0)

    column_scales = scales[None, :]
    row_scales = [(row_scales / denom[j])[:, None] for j in range(groups)]

    place = jnp.stack([me, 1 - half, half]).astype(jnp.int32)
    shared = len(PARTS)
    arrived, flat, out = [], [], None

    def send(n, waits):
        got = [parts[n][0]]
        for d in range(1, owners):
            gates = list(waits.get(d, ()))
            if len(flat) >= IN_FLIGHT and not (n == 1 and d == 2):
                gates.append(flat[len(flat) - IN_FLIGHT])
            value = after(parts[n][d], *gates) if gates else parts[n][d]
            with jax.named_scope(f"part{n}_shift{d}"):
                got.append(shift(value, d))
            flat.append(got[-1])
        arrived.append(got)

    def to_other(j, theirs):
        with jax.named_scope(f"rows{j}"):
            return lax.ppermute(theirs, "tm", [(0, 1), (1, 0)])

    def multiply(j, place, dtypes, sums=(), earlier=(), begin=0, end=shared + 1):
        pieces = arrived[:shared] + arrived[shared + j : shared + j + 1]
        picks = (j,) * shared + (0,)
        return correlate(place, pieces[begin:end], picks[begin:end], dtypes, sums, earlier)

    both = [jnp.bfloat16, jnp.float32]
    last_spectra = parts[shared][0]
    for n in range(shared):
        waits = {} if n == 0 else {d: [last_spectra, arrived[0][2]] for d in range(1, owners) if d != 2}
        send(n, waits)
    send(shared, {owners - 1: [column_scales]})
    waiting = None
    for j in range(groups - 1):
        waits = {}
        if j == 0:
            partial = multiply(groups - 1, place, [jnp.float32] * 2, end=shared)
            waits = {owners - 1: partial}
        send(shared + j + 1, waits)
        theirs, mine = multiply(j, place, both)
        if waiting is not None:
            out = equalize(*waiting, out, j - 1, groups, [theirs])
        if j + 2 < groups:
            theirs = after(theirs, *arrived[shared + j + 1][1:])
        theirs = to_other(j, theirs)
        waiting = (row_scales[j], column_scales, mine, theirs)
    j = groups - 1
    (theirs,) = multiply(j, place[:2], both[:1], partial[:1], [out], begin=shared)
    out = equalize(*waiting, out, groups - 2, groups, [theirs])
    theirs = to_other(j, theirs)
    (mine,) = multiply(j, place[::2], both[1:], partial[1:], begin=shared)
    out = equalize(row_scales[j], column_scales, mine, theirs, out, j, groups, [])
    return out[None]


def twiddle_table():
    values = twiddle_values().transpose(2, 1, 0)
    return jnp.asarray(values).astype(jnp.bfloat16)


def pair_products(left, right):
    swapped = jnp.stack([left[..., 1, :], -left[..., 0, :]], 4)
    real = jnp.einsum("cgfird,cgfjrd->icgj", left, right, preferred_element_type=jnp.float32)
    imag = jnp.einsum("cgfird,cgfjrd->icgj", swapped, right, preferred_element_type=jnp.float32)
    return jnp.stack([real, imag], 3)


def plain(volts, flagged):
    coarse_dev = volts.shape[1]
    inputs_dev = volts.shape[2]
    spec_count = volts.shape[3] // SUBBAND_COUNT
    frames_all = spec_count * lax.axis_size("tm")
    frames = volts.reshape(2, coarse_dev, inputs_dev, spec_count, SUBBAND_COUNT)
    history = passed_on(frames[:, :, :, spec_count - (TAPS - 1) :, :])
    padded = jnp.concatenate([history, frames], 3)
    window = jnp.asarray(window_values())
    filtered = jnp.zeros((2, coarse_dev, inputs_dev, spec_count, SUBBAND_COUNT), jnp.float32)
    for tap in range(TAPS):
        filtered = filtered + window[tap] * padded[:, :, :, tap : tap + spec_count, :].astype(
            jnp.float32
        )
    filtered = filtered.astype(jnp.bfloat16)
    joined = jnp.concatenate([filtered[0], filtered[1]], -1)
    spectra = jnp.einsum(
        "nqvx,xdl->nlqdv", joined, twiddle_table(), preferred_element_type=jnp.float32
    ).astype(jnp.bfloat16)
    keep_all = keep_table(flagged)
    keep_mine = lax.dynamic_slice_in_dim(
        keep_all, lax.axis_index("band") * coarse_dev, coarse_dev, 0
    )
    values = spectra.astype(jnp.float32)
    local = jnp.sum(values * values * keep_mine[:, :, None, None, None], axis=(0, 1, 3, 4))
    total = lax.psum(local, ("band", "tm"))
    scale = lax.rsqrt(total / (frames_all * jnp.sum(keep_all)) + 1e-06)
    scales = lax.all_gather(scale, "station", axis=0, tiled=True)
    received = lax.all_to_all(spectra, "station", split_axis=1, concat_axis=2, tiled=True)
    fine_dev = received.shape[1]
    inputs_all = received.shape[2]
    kept = lax.dynamic_slice_in_dim(keep_mine, lax.axis_index("station") * fine_dev, fine_dev, 1)
    groups_dev = fine_dev // GROUP
    masked = received * kept[:, :, None, None, None].astype(jnp.bfloat16)
    blocks = masked.reshape(coarse_dev, groups_dev, GROUP, inputs_all, 2, spec_count)
    rows = inputs_all // lax.axis_size("tm")
    summed = lax.psum_scatter(pair_products(blocks, blocks), "tm", scatter_dimension=0, tiled=True)
    counts = kept.reshape(coarse_dev, groups_dev, GROUP).sum(-1)
    denom = frames_all * jnp.maximum(counts, 1.0)
    row_scales = lax.dynamic_slice_in_dim(scales, lax.axis_index("tm") * rows, rows, 0)
    pairs = row_scales[:, None] * scales[None, :]
    ordered = jnp.transpose(summed, (1, 2, 3, 0, 4))
    return ordered * pairs[None, None, None, :, :] / denom[:, :, None, None, None]


def shards(volts, flagged):
    owners = lax.axis_size("station")
    frames = volts.shape[3] // SUBBAND_COUNT
    fits = (
        volts.shape[1] == 1
        and volts.shape[2] % 128 == 0
        and owners % 2 == 0
        and (SUBBAND_COUNT // owners) % GROUP == 0
        and lax.axis_size("tm") == 2
        and frames % BLOCK == 0
        and SUBBAND_COUNT // owners // GROUP > 1
        and frames // BLOCK > sum(PARTS)
    )
    return (pipelined if fits else plain)(volts, flagged)


def solution(mesh):
    placed = (P(None, "band", "station", "tm"), P())
    return jax.shard_map(
        shards,
        mesh=mesh,
        in_specs=placed,
        out_specs=P("band", "station", None, "tm", None),
        check_vma=False,
    )
```

```python
import functools
import math

import jax
import jax.numpy as jnp
import numpy as np
from jax import lax
from jax.experimental import pallas as pl
from jax.experimental.pallas import tpu as pltpu
from jax.sharding import PartitionSpec as P

SUBBAND_COUNT = 144
TAPS = 12
GROUP = 9
BLOCK = 16
PARTS = (1, 3)
SPREAD = BLOCK + 1
VMEM = 60 * 1024 * 1024
COST = pl.CostEstimate(flops=1024, bytes_accessed=1024, transcendentals=0)
IN_FLIGHT = 3


def window_values():
    total = TAPS * SUBBAND_COUNT
    place = np.arange(total, dtype=np.float64)
    shape = np.sinc((place - total / 2.0 + 0.5) / SUBBAND_COUNT)
    taper = 0.5 - 0.5 * np.cos(2.0 * math.pi * (place + 0.5) / total)
    return (shape * taper).reshape(TAPS, SUBBAND_COUNT).astype(np.float32)


def twiddle_values():
    f = np.arange(SUBBAND_COUNT, dtype=np.int64)[:, None]
    n = np.arange(SUBBAND_COUNT, dtype=np.int64)[None, :]
    angle = 2.0 * math.pi * (f * n % SUBBAND_COUNT) / SUBBAND_COUNT
    cosines, sines = np.cos(angle), np.sin(angle)
    real = np.concatenate([cosines, sines], 1)
    imag = np.concatenate([-sines, cosines], 1)
    return np.stack([real, imag], 1).astype(np.float32)


def front_kernel(
    splits, owners, turned, tail, me_ref, keep_ref, hist_ref, volts_ref, window_ref, table_ref, *rest
):
    outs, power_ref = rest[: owners * splits], rest[owners * splits]
    tail_ref = rest[owners * splits + 1] if tail else None
    ring, filt, spread = rest[-3:]
    step = pl.program_id(0)
    now = lax.rem(step, 2)
    before = 1 - now
    inputs = ring.shape[-1]
    tiles = inputs // 128
    span = BLOCK * SUBBAND_COUNT
    skipped = (BLOCK + 1 - TAPS) * SUBBAND_COUNT

    def turn(ref, slot, begin):
        def columns(c, _):
            at = pl.multiple_of(c * 128, 128)
            for part in range(2):
                ring[slot, part, pl.ds(at, 128), :] = ref[part, 0, :, pl.ds(at, 128)].T
            return 0

        lax.fori_loop(begin, span // 128, columns, 0, unroll=6 if begin == 0 else 5)

    @pl.when(step == 0)
    def _():
        if turned:
            for part in range(2):
                ring[1, part, pl.ds(skipped, span - skipped), :] = hist_ref[part]
        else:
            turn(hist_ref, 1, 3)
        power_ref[...] = jnp.zeros_like(power_ref)

    turn(volts_ref, now, 0)
    if tail:
        for part in range(2):
            tail_ref[part] = ring[now, part, pl.ds(skipped, span - skipped), :]

    def filter_rows(j, _):
        base = pl.multiple_of(j * 16, 16)
        for tile in range(tiles):
            lanes = pl.ds(tile * 128, 128)
            weights = [window_ref[k, pl.ds(base, 16), :] for k in range(TAPS)]
            for part in range(2):
                samples = []
                for t in range(1 - TAPS, BLOCK):
                    slot, frame = (now, t) if t >= 0 else (before, BLOCK + t)
                    at = pl.multiple_of(frame * SUBBAND_COUNT + base, 16)
                    samples.append(ring[slot, part, pl.ds(at, 16), lanes].astype(jnp.float32))
                for t in range(BLOCK):
                    total = weights[0] * samples[t]
                    for k in range(1, TAPS):
                        total = total + weights[k] * samples[t + k]
                    at = pl.multiple_of(part * SUBBAND_COUNT + base, 16)
                    filt[t, pl.ds(at, 16), lanes] = total.astype(jnp.bfloat16)
        return 0

    lax.fori_loop(0, SUBBAND_COUNT // 16, filter_rows, 0)

    def transform(t, _):
        result = jnp.dot(table_ref[0], filt[t], preferred_element_type=jnp.float32)
        for tile in range(tiles):
            spread[tile, pl.ds(t, 2 * SUBBAND_COUNT, stride=SPREAD), :] = result[
                :, tile * 128 : (tile + 1) * 128
            ]
        return 0

    lax.fori_loop(0, BLOCK, transform, 0, unroll=4)

    groups = SUBBAND_COUNT // owners // GROUP
    power = [jnp.zeros((BLOCK, 128), jnp.float32) for _ in range(tiles)]
    for d in range(owners):
        for j in range(groups):
            out = outs[d * splits + j] if splits > 1 else outs[d]
            place = 0 if splits > 1 else j

            def channel(f, power, d=d, j=j, out=out, place=place):
                keep = keep_ref[(d * groups + j) * GROUP + f]
                power = list(power)
                for part in range(2):
                    row = ((d * groups + j) * 2 + part) * GROUP + f
                    for tile in range(tiles):
                        value = spread[tile, pl.ds(row * SPREAD, BLOCK), :] * keep
                        value = value.astype(jnp.bfloat16)
                        out[place, part, f, :, tile * 128 : (tile + 1) * 128] = value
                        value = value.astype(jnp.float32)
                        power[tile] = power[tile] + value * value
                return tuple(power)

            power = lax.fori_loop(0, GROUP, channel, tuple(power), unroll=3)
    for tile in range(tiles):
        power_ref[:, tile * 128 : (tile + 1) * 128] += power[tile]


def front(volts, hist, first, steps, splits, owners, keep, me, window, table, tail):
    inputs = volts.shape[2]
    span = BLOCK * SUBBAND_COUNT
    groups = SUBBAND_COUNT // owners // GROUP
    each = groups // splits
    frames = steps * BLOCK
    outs = [
        jax.ShapeDtypeStruct((each, 2, GROUP, frames, inputs), jnp.bfloat16)
        for _ in range(owners * splits)
    ]
    out_specs = [
        pl.BlockSpec((each, 2, GROUP, BLOCK, inputs), lambda s, me: (0, 0, 0, s, 0))
        for _ in range(owners * splits)
    ]
    outs.append(jax.ShapeDtypeStruct((BLOCK, inputs), jnp.float32))
    out_specs.append(pl.BlockSpec((BLOCK, inputs), lambda s, me: (0, 0)))
    kept = (TAPS - 1) * SUBBAND_COUNT
    if tail:
        outs.append(jax.ShapeDtypeStruct((2, kept, inputs), jnp.bfloat16))
        out_specs.append(pl.BlockSpec((2, kept, inputs), lambda s, me: (0, 0, 0)))
    if hist is None:
        hist, hist_spec = volts, pl.BlockSpec((2, 1, inputs, span), lambda s, me: (0, 0, 0, first - 1))
        turned = False
    else:
        hist_spec, turned = pl.BlockSpec((2, kept, inputs), lambda s, me: (0, 0, 0)), True
    result = pl.pallas_call(
        functools.partial(front_kernel, splits, owners, turned, tail),
        grid_spec=pltpu.PrefetchScalarGridSpec(
            num_scalar_prefetch=1,
            grid=(steps,),
            in_specs=[
                pl.BlockSpec(memory_space=pltpu.SMEM),
                hist_spec,
                pl.BlockSpec((2, 1, inputs, span), lambda s, me: (0, 0, 0, first + s)),
                pl.BlockSpec(window.shape, lambda s, me: (0, 0, 0)),
                pl.BlockSpec((1, *table.shape[1:]), lambda s, me: (me[0], 0, 0)),
            ],
            out_specs=out_specs,
            scratch_shapes=[
                pltpu.VMEM((2, 2, span, inputs), jnp.bfloat16),
                pltpu.VMEM((BLOCK, 2 * SUBBAND_COUNT, inputs), jnp.bfloat16),
                pltpu.VMEM((inputs // 128, 2 * SUBBAND_COUNT * SPREAD, 128), jnp.float32),
            ],
        ),
        out_shape=outs,
        compiler_params=pltpu.CompilerParams(vmem_limit_bytes=VMEM),
        cost_estimate=COST,
        name="front",
    )(me, keep, hist, volts, window, table)
    count = owners * splits
    return result[:count], result[count], result[count + 1] if tail else None


def after_kernel(*refs):
    pass


def after(value, *others):
    anywhere = pl.BlockSpec(memory_space=pl.ANY)
    return pl.pallas_call(
        after_kernel,
        out_shape=jax.ShapeDtypeStruct(value.shape, value.dtype),
        in_specs=[anywhere] * (1 + len(others)),
        out_specs=anywhere,
        input_output_aliases={0: 0},
        cost_estimate=COST,
        name="after",
    )(value, *others)


def correlate_kernel(owners, picks, outs, sums, place_ref, *rest):
    count = len(picks)
    sum_refs, rest = rest[:sums], rest[sums:]
    pieces = [rest[n * owners : (n + 1) * owners] for n in range(count)]
    out_refs, (held, turned, sems) = rest[-3 - outs : -3], rest[-3:]
    me = place_ref[0]
    column = pl.program_id(0)
    per_half = owners // 2
    inputs, depth = turned.shape[3], held.shape[2]

    @pl.when(column == 0)
    def _():
        copies = []
        for d in range(owners):
            source = lax.rem(me - d + owners, owners)
            at = 0
            for n in range(count):
                size = pieces[n][d].shape[2]
                copies.append(
                    pltpu.make_async_copy(
                        pieces[n][d].at[picks[n]], held.at[source, :, pl.ds(at, size)], sems.at[n, d]
                    )
                )
                at += size
        for copy in copies:
            copy.start()
        for copy in copies:
            copy.wait()
        for h in range(outs):
            for r in range(per_half):
                source = place_ref[1 + h] * per_half + r
                real, imag = held[source, 0].T, held[source, 1].T
                turned[h, 0, r, :, pl.ds(0, depth)] = real
                turned[h, 0, r, :, pl.ds(depth, depth)] = imag
                turned[h, 1, r, :, pl.ds(0, depth)] = imag
                turned[h, 1, r, :, pl.ds(depth, depth)] = -real

    right = held[column].reshape(2 * depth, inputs)
    for h in range(outs):
        left = turned[h].reshape(2 * per_half * inputs, 2 * depth)
        both = jnp.dot(left, right, preferred_element_type=jnp.float32)
        both = both.reshape(2, per_half * inputs, inputs)
        if sums:
            both = both + sum_refs[h][...]
        out_refs[h][...] = both.astype(out_refs[h].dtype)


def correlate(place, pieces, picks, dtypes, sums, earlier):
    owners = len(pieces[0])
    inputs = pieces[0][0].shape[-1]
    depth = sum(piece[0].shape[2] for piece in pieces)
    rows = owners // 2 * inputs
    operands = [value for piece in pieces for value in piece] + list(earlier)
    columns = pl.BlockSpec((2, rows, inputs), lambda b: (0, 0, b))
    anywhere = pl.BlockSpec(memory_space=pl.ANY)
    outs = len(dtypes)
    return pl.pallas_call(
        functools.partial(correlate_kernel, owners, picks, outs, len(sums)),
        grid=(owners,),
        out_shape=[jax.ShapeDtypeStruct((2, rows, owners * inputs), dtype) for dtype in dtypes],
        in_specs=[pl.BlockSpec(memory_space=pltpu.SMEM)]
        + [columns] * len(sums)
        + [anywhere] * len(operands),
        out_specs=[columns] * outs,
        scratch_shapes=[
            pltpu.VMEM((owners, 2, depth, inputs), jnp.bfloat16),
            pltpu.VMEM((outs, 2, owners // 2, inputs, 2 * depth), jnp.bfloat16),
            pltpu.SemaphoreType.DMA((len(pieces), owners)),
        ],
        compiler_params=pltpu.CompilerParams(vmem_limit_bytes=VMEM),
        cost_estimate=COST,
        name="correlate",
    )(place, *sums, *operands)


def equalize_kernel(rows_ref, columns_ref, mine_ref, theirs_ref, *rest):
    out_ref = rest[-1]
    scale = rows_ref[...] * columns_ref[...]
    for part in range(2):
        total = mine_ref[part] + theirs_ref[part].astype(jnp.float32)
        out_ref[0, part] = total * scale


def equalize(row_scales, column_scales, mine, theirs, out, group, groups, waits):
    rows, columns = mine.shape[1:]
    block = rows // 4
    specs = [
        pl.BlockSpec((block, 1), lambda r: (r, 0)),
        pl.BlockSpec((1, columns), lambda r: (0, 0)),
        pl.BlockSpec((2, block, columns), lambda r: (0, r, 0)),
        pl.BlockSpec((2, block, columns), lambda r: (0, r, 0)),
    ]
    operands = [row_scales, column_scales, mine, theirs]
    aliases = {}
    if out is not None:
        specs.append(pl.BlockSpec(memory_space=pl.ANY))
        operands.append(out)
        aliases = {4: 0}
    specs += [pl.BlockSpec(memory_space=pl.ANY)] * len(waits)
    operands += waits
    return pl.pallas_call(
        equalize_kernel,
        grid=(rows // block,),
        out_shape=jax.ShapeDtypeStruct((groups, 2, rows, columns), jnp.float32),
        in_specs=specs,
        out_specs=pl.BlockSpec((1, 2, block, columns), lambda r: (group, 0, r, 0)),
        input_output_aliases=aliases,
        compiler_params=pltpu.CompilerParams(vmem_limit_bytes=VMEM),
        cost_estimate=COST,
        name="equalize",
    )(*operands)


def shift(value, d):
    count = lax.axis_size("station")
    return lax.ppermute(value, "station", [(s, (s + d) % count) for s in range(count)])


def passed_on(value):
    count = lax.axis_size("tm")
    return lax.ppermute(value, "tm", [(s, s + 1) for s in range(count - 1)])


def keep_table(flagged):
    fine = jnp.arange(SUBBAND_COUNT, dtype=jnp.int32)
    return jnp.all(flagged[:, :, None] != fine[None, None, :], axis=1).astype(jnp.float32)


def pipelined(volts, flagged):
    owners = lax.axis_size("station")
    me = lax.axis_index("station")
    half = lax.axis_index("tm")
    inputs = volts.shape[2]
    frames = volts.shape[3] // SUBBAND_COUNT
    frames_all = frames * lax.axis_size("tm")
    fine = SUBBAND_COUNT // owners
    groups = fine // GROUP
    blocks = frames // BLOCK

    keep_all = keep_table(flagged)
    keep_mine = lax.dynamic_index_in_dim(keep_all, lax.axis_index("band"), 0, keepdims=False)
    twice = jnp.concatenate([keep_mine, keep_mine])
    keep_ahead = lax.dynamic_slice_in_dim(twice, me * fine, SUBBAND_COUNT, 0)

    rows = twiddle_values().reshape(owners, groups, GROUP, 2, 2 * SUBBAND_COUNT)
    rows = rows.transpose(0, 1, 3, 2, 4)
    turns = [np.roll(rows, -z, 0).reshape(2 * SUBBAND_COUNT, -1) for z in range(owners)]
    table = jnp.asarray(np.stack(turns).astype(jnp.bfloat16))
    window = np.broadcast_to(window_values()[:, :, None], (TAPS, SUBBAND_COUNT, 128))
    window = jnp.asarray(np.ascontiguousarray(window))
    spot = jnp.reshape(me, (1,)).astype(jnp.int32)

    parts, arrived, flat, out = [], [], [], None

    def send(n, waits):
        got = [parts[n][0]]
        for d in range(1, owners):
            gates = list(waits.get(d, ()))
            if len(flat) >= IN_FLIGHT and not (n == 1 and d == 2):
                gates.append(flat[len(flat) - IN_FLIGHT])
            value = after(parts[n][d], *gates) if gates else parts[n][d]
            with jax.named_scope(f"part{n}_shift{d}"):
                got.append(shift(value, d))
            flat.append(got[-1])
        arrived.append(got)

    power, halo, end = [], None, blocks
    for size in PARTS:
        end -= size
        spectra, part_power, tail = front(
            volts, None, end, size, 1, owners, keep_ahead, spot, window, table, halo is None
        )
        if tail is not None:
            halo = tail
        parts.append([x.reshape(groups, 2, GROUP * size * BLOCK, inputs) for x in spectra])
        power.append(part_power)
        if len(parts) == 1:
            send(0, {})
    with jax.named_scope("halo"):
        halo = passed_on(halo)
    spectra, part_power, _ = front(
        volts, halo, 0, end, groups, owners, keep_ahead, spot, window, table, False
    )
    power.append(part_power)
    spectra = [x.reshape(1, 2, GROUP * end * BLOCK, inputs) for x in spectra]
    for j in range(groups):
        parts.append([spectra[d * groups + j] for d in range(owners)])

    local = jnp.sum(sum(power), axis=0)
    total = lax.psum(local, ("band", "tm"))
    scale = lax.rsqrt(total / (frames_all * jnp.sum(keep_all)) + 1e-06)
    scales = lax.all_gather(scale, "station", axis=0, tiled=True)
    kept = lax.dynamic_slice_in_dim(keep_mine, me * fine, fine, 0)
    counts = kept.reshape(groups, GROUP).sum(-1)
    denom = frames_all * jnp.maximum(counts, 1.0)
    per_half = scales.shape[0] // 2
    row_scales = lax.dynamic_slice_in_dim(scales, half * per_half, per_half, 0)

    column_scales = scales[None, :]
    row_scales = [(row_scales / denom[j])[:, None] for j in range(groups)]

    place = jnp.stack([me, 1 - half, half]).astype(jnp.int32)
    shared = len(PARTS)
    def to_other(j, theirs):
        with jax.named_scope(f"rows{j}"):
            return lax.ppermute(theirs, "tm", [(0, 1), (1, 0)])

    def multiply(j, place, dtypes, sums=(), earlier=(), begin=0, end=shared + 1):
        pieces = arrived[:shared] + arrived[shared + j : shared + j + 1]
        picks = (j,) * shared + (0,)
        return correlate(place, pieces[begin:end], picks[begin:end], dtypes, sums, earlier)

    both = [jnp.bfloat16, jnp.float32]
    last_spectra = parts[shared][0]
    for n in range(1, shared):
        send(n, {d: [last_spectra, arrived[0][2]] for d in range(1, owners) if d != 2})
    send(shared, {owners - 1: [column_scales]})
    waiting = None
    for j in range(groups - 1):
        waits = {}
        if j == 0:
            partial = multiply(groups - 1, place, [jnp.float32] * 2, end=shared)
            waits = {owners - 1: partial}
        send(shared + j + 1, waits)
        theirs, mine = multiply(j, place, both)
        if waiting is not None:
            out = equalize(*waiting, out, j - 1, groups, [theirs])
        if j + 2 < groups:
            theirs = after(theirs, *arrived[shared + j + 1][1:])
        theirs = to_other(j, theirs)
        waiting = (row_scales[j], column_scales, mine, theirs)
    j = groups - 1
    theirs, mine = multiply(j, place, both, partial, [out], begin=shared)
    out = equalize(*waiting, out, groups - 2, groups, [theirs])
    theirs = to_other(j, theirs)
    out = equalize(row_scales[j], column_scales, mine, theirs, out, j, groups, [])
    return out[None]


def twiddle_table():
    values = twiddle_values().transpose(2, 1, 0)
    return jnp.asarray(values).astype(jnp.bfloat16)


def pair_products(left, right):
    swapped = jnp.stack([left[..., 1, :], -left[..., 0, :]], 4)
    real = jnp.einsum("cgfird,cgfjrd->icgj", left, right, preferred_element_type=jnp.float32)
    imag = jnp.einsum("cgfird,cgfjrd->icgj", swapped, right, preferred_element_type=jnp.float32)
    return jnp.stack([real, imag], 3)


def plain(volts, flagged):
    coarse_dev = volts.shape[1]
    inputs_dev = volts.shape[2]
    spec_count = volts.shape[3] // SUBBAND_COUNT
    frames_all = spec_count * lax.axis_size("tm")
    frames = volts.reshape(2, coarse_dev, inputs_dev, spec_count, SUBBAND_COUNT)
    history = passed_on(frames[:, :, :, spec_count - (TAPS - 1) :, :])
    padded = jnp.concatenate([history, frames], 3)
    window = jnp.asarray(window_values())
    filtered = jnp.zeros((2, coarse_dev, inputs_dev, spec_count, SUBBAND_COUNT), jnp.float32)
    for tap in range(TAPS):
        filtered = filtered + window[tap] * padded[:, :, :, tap : tap + spec_count, :].astype(
            jnp.float32
        )
    filtered = filtered.astype(jnp.bfloat16)
    joined = jnp.concatenate([filtered[0], filtered[1]], -1)
    spectra = jnp.einsum(
        "nqvx,xdl->nlqdv", joined, twiddle_table(), preferred_element_type=jnp.float32
    ).astype(jnp.bfloat16)
    keep_all = keep_table(flagged)
    keep_mine = lax.dynamic_slice_in_dim(
        keep_all, lax.axis_index("band") * coarse_dev, coarse_dev, 0
    )
    values = spectra.astype(jnp.float32)
    local = jnp.sum(values * values * keep_mine[:, :, None, None, None], axis=(0, 1, 3, 4))
    total = lax.psum(local, ("band", "tm"))
    scale = lax.rsqrt(total / (frames_all * jnp.sum(keep_all)) + 1e-06)
    scales = lax.all_gather(scale, "station", axis=0, tiled=True)
    received = lax.all_to_all(spectra, "station", split_axis=1, concat_axis=2, tiled=True)
    fine_dev = received.shape[1]
    inputs_all = received.shape[2]
    kept = lax.dynamic_slice_in_dim(keep_mine, lax.axis_index("station") * fine_dev, fine_dev, 1)
    groups_dev = fine_dev // GROUP
    masked = received * kept[:, :, None, None, None].astype(jnp.bfloat16)
    blocks = masked.reshape(coarse_dev, groups_dev, GROUP, inputs_all, 2, spec_count)
    rows = inputs_all // lax.axis_size("tm")
    summed = lax.psum_scatter(pair_products(blocks, blocks), "tm", scatter_dimension=0, tiled=True)
    counts = kept.reshape(coarse_dev, groups_dev, GROUP).sum(-1)
    denom = frames_all * jnp.maximum(counts, 1.0)
    row_scales = lax.dynamic_slice_in_dim(scales, lax.axis_index("tm") * rows, rows, 0)
    pairs = row_scales[:, None] * scales[None, :]
    ordered = jnp.transpose(summed, (1, 2, 3, 0, 4))
    return ordered * pairs[None, None, None, :, :] / denom[:, :, None, None, None]


def shards(volts, flagged):
    owners = lax.axis_size("station")
    frames = volts.shape[3] // SUBBAND_COUNT
    fits = (
        volts.shape[1] == 1
        and volts.shape[2] % 128 == 0
        and owners % 2 == 0
        and (SUBBAND_COUNT // owners) % GROUP == 0
        and lax.axis_size("tm") == 2
        and frames % BLOCK == 0
        and SUBBAND_COUNT // owners // GROUP > 1
        and frames // BLOCK > sum(PARTS)
    )
    return (pipelined if fits else plain)(volts, flagged)


def solution(mesh):
    placed = (P(None, "band", "station", "tm"), P())
    return jax.shard_map(
        shards,
        mesh=mesh,
        in_specs=placed,
        out_specs=P("band", "station", None, "tm", None),
        check_vma=False,
    )
```

```python
import functools
import math

import jax
import jax.numpy as jnp
import numpy as np
from jax import lax
from jax.experimental import pallas as pl
from jax.experimental.pallas import tpu as pltpu
from jax.sharding import PartitionSpec as P

SUBBAND_COUNT = 144
TAPS = 12
GROUP = 9
BLOCK = 16
PARTS = (1, 3)
SPREAD = BLOCK + 1
VMEM = 60 * 1024 * 1024
COST = pl.CostEstimate(flops=1024, bytes_accessed=1024, transcendentals=0)
DROPPED = 3
IN_FLIGHT = 3


def window_values():
    total = TAPS * SUBBAND_COUNT
    place = np.arange(total, dtype=np.float64)
    shape = np.sinc((place - total / 2.0 + 0.5) / SUBBAND_COUNT)
    taper = 0.5 - 0.5 * np.cos(2.0 * math.pi * (place + 0.5) / total)
    return (shape * taper).reshape(TAPS, SUBBAND_COUNT).astype(np.float32)


def twiddle_values():
    f = np.arange(SUBBAND_COUNT, dtype=np.int64)[:, None]
    n = np.arange(SUBBAND_COUNT, dtype=np.int64)[None, :]
    angle = 2.0 * math.pi * (f * n % SUBBAND_COUNT) / SUBBAND_COUNT
    cosines, sines = np.cos(angle), np.sin(angle)
    real = np.concatenate([cosines, sines], 1)
    imag = np.concatenate([-sines, cosines], 1)
    return np.stack([real, imag], 1).astype(np.float32)


def unrolled(count):
    return max(n for n in range(1, 7) if count % n == 0)


def front_kernel(
    sizes, owners, turned, tail, me_ref, keep_ref, hist_ref, volts_ref, window_ref, table_ref, pick_ref, *rest
):
    splits, slots = len(sizes), sum(sizes)
    outs, power_ref = rest[: owners * splits], rest[owners * splits]
    tail_ref = rest[owners * splits + 1] if tail else None
    ring, filt, spread, picked = rest[-4:]
    step = pl.program_id(0)
    now = lax.rem(step, 2)
    before = 1 - now
    inputs = ring.shape[-1]
    tiles = inputs // 128
    span = BLOCK * SUBBAND_COUNT
    skipped = (BLOCK + 1 - TAPS) * SUBBAND_COUNT

    def turn(ref, slot, begin):
        def columns(c, _):
            at = pl.multiple_of(c * 128, 128)
            for part in range(2):
                ring[slot, part, pl.ds(at, 128), :] = ref[part, 0, :, pl.ds(at, 128)].T
            return 0

        lax.fori_loop(begin, span // 128, columns, 0, unroll=6 if begin == 0 else 5)

    @pl.when(step == 0)
    def _():
        if turned:
            for part in range(2):
                ring[1, part, pl.ds(skipped, span - skipped), :] = hist_ref[part]
        else:
            turn(hist_ref, 1, 3)
        power_ref[...] = jnp.zeros_like(power_ref)
        chosen = jnp.dot(pick_ref[...], table_ref[0], preferred_element_type=jnp.float32)
        picked[...] = chosen.astype(jnp.bfloat16)

    turn(volts_ref, now, 0)
    if tail:
        for part in range(2):
            tail_ref[part] = ring[now, part, pl.ds(skipped, span - skipped), :]

    def filter_rows(j, _):
        base = pl.multiple_of(j * 16, 16)
        for tile in range(tiles):
            lanes = pl.ds(tile * 128, 128)
            weights = [window_ref[k, pl.ds(base, 16), :] for k in range(TAPS)]
            for part in range(2):
                samples = []
                for t in range(1 - TAPS, BLOCK):
                    slot, frame = (now, t) if t >= 0 else (before, BLOCK + t)
                    at = pl.multiple_of(frame * SUBBAND_COUNT + base, 16)
                    samples.append(ring[slot, part, pl.ds(at, 16), lanes].astype(jnp.float32))
                for t in range(BLOCK):
                    total = weights[0] * samples[t]
                    for k in range(1, TAPS):
                        total = total + weights[k] * samples[t + k]
                    at = pl.multiple_of(part * SUBBAND_COUNT + base, 16)
                    filt[t, pl.ds(at, 16), lanes] = total.astype(jnp.bfloat16)
        return 0

    lax.fori_loop(0, SUBBAND_COUNT // 16, filter_rows, 0)

    def transform(t, _):
        result = jnp.dot(picked[...], filt[t], preferred_element_type=jnp.float32)
        for tile in range(tiles):
            spread[tile, pl.ds(t, 2 * owners * slots, stride=SPREAD), :] = result[
                :, tile * 128 : (tile + 1) * 128
            ]
        return 0

    lax.fori_loop(0, BLOCK, transform, 0, unroll=4)

    power = [jnp.zeros((BLOCK, 128), jnp.float32) for _ in range(tiles)]
    for d in range(owners):
        for q in range(splits):
            out = outs[d * splits + q]
            begin = d * slots + sum(sizes[:q])

            def channel(f, power, out=out, begin=begin):
                keep = keep_ref[begin + f]
                power = list(power)
                for part in range(2):
                    row = (begin + f) * 2 + part
                    for tile in range(tiles):
                        value = spread[tile, pl.ds(row * SPREAD, BLOCK), :] * keep
                        value = value.astype(jnp.bfloat16)
                        out[part, f, :, tile * 128 : (tile + 1) * 128] = value
                        value = value.astype(jnp.float32)
                        power[tile] = power[tile] + value * value
                return tuple(power)

            power = lax.fori_loop(0, sizes[q], channel, tuple(power), unroll=unrolled(sizes[q]))
    for tile in range(tiles):
        power_ref[:, tile * 128 : (tile + 1) * 128] += power[tile]


def front(volts, hist, first, steps, sizes, owners, keep, me, window, table, pick, tail):
    inputs = volts.shape[2]
    span = BLOCK * SUBBAND_COUNT
    frames = steps * BLOCK
    outs, out_specs = [], []
    for _ in range(owners):
        for size in sizes:
            outs.append(jax.ShapeDtypeStruct((2, size, frames, inputs), jnp.bfloat16))
            out_specs.append(pl.BlockSpec((2, size, BLOCK, inputs), lambda s, me: (0, 0, s, 0)))
    outs.append(jax.ShapeDtypeStruct((BLOCK, inputs), jnp.float32))
    out_specs.append(pl.BlockSpec((BLOCK, inputs), lambda s, me: (0, 0)))
    kept = (TAPS - 1) * SUBBAND_COUNT
    if tail:
        outs.append(jax.ShapeDtypeStruct((2, kept, inputs), jnp.bfloat16))
        out_specs.append(pl.BlockSpec((2, kept, inputs), lambda s, me: (0, 0, 0)))
    if hist is None:
        hist, hist_spec = volts, pl.BlockSpec((2, 1, inputs, span), lambda s, me: (0, 0, 0, first - 1))
        turned = False
    else:
        hist_spec, turned = pl.BlockSpec((2, kept, inputs), lambda s, me: (0, 0, 0)), True
    result = pl.pallas_call(
        functools.partial(front_kernel, sizes, owners, turned, tail),
        grid_spec=pltpu.PrefetchScalarGridSpec(
            num_scalar_prefetch=1,
            grid=(steps,),
            in_specs=[
                pl.BlockSpec(memory_space=pltpu.SMEM),
                hist_spec,
                pl.BlockSpec((2, 1, inputs, span), lambda s, me: (0, 0, 0, first + s)),
                pl.BlockSpec(window.shape, lambda s, me: (0, 0, 0)),
                pl.BlockSpec((1, *table.shape[1:]), lambda s, me: (me[0], 0, 0)),
                pl.BlockSpec(pick.shape, lambda s, me: (0, 0)),
            ],
            out_specs=out_specs,
            scratch_shapes=[
                pltpu.VMEM((2, 2, span, inputs), jnp.bfloat16),
                pltpu.VMEM((BLOCK, 2 * SUBBAND_COUNT, inputs), jnp.bfloat16),
                pltpu.VMEM((inputs // 128, pick.shape[0] * SPREAD, 128), jnp.float32),
                pltpu.VMEM((pick.shape[0], 2 * SUBBAND_COUNT), jnp.bfloat16),
            ],
        ),
        out_shape=outs,
        compiler_params=pltpu.CompilerParams(vmem_limit_bytes=VMEM),
        cost_estimate=COST,
        name="front",
    )(me, keep, hist, volts, window, table, pick)
    count = owners * len(sizes)
    return result[:count], result[count], result[count + 1] if tail else None


def after_kernel(*refs):
    pass


def after(value, *others):
    anywhere = pl.BlockSpec(memory_space=pl.ANY)
    return pl.pallas_call(
        after_kernel,
        out_shape=jax.ShapeDtypeStruct(value.shape, value.dtype),
        in_specs=[anywhere] * (1 + len(others)),
        out_specs=anywhere,
        input_output_aliases={0: 0},
        cost_estimate=COST,
        name="after",
    )(value, *others)


def correlate_kernel(owners, picks, outs, sums, place_ref, mask_ref, *rest):
    count = len(picks)
    sum_refs, rest = rest[:sums], rest[sums:]
    pieces = [rest[n * owners : (n + 1) * owners] for n in range(count)]
    out_refs, (held, turned, sems) = rest[-3 - outs : -3], rest[-3:]
    me = place_ref[0]
    column = pl.program_id(0)
    per_half = owners // 2
    inputs, depth = turned.shape[3], held.shape[2]

    @pl.when(column == 0)
    def _():
        copies = []
        for d in range(owners):
            source = lax.rem(me - d + owners, owners)
            at = 0
            for n in range(count):
                begin, size = picks[n]
                copies.append(
                    pltpu.make_async_copy(
                        pieces[n][d].at[:, pl.ds(begin, size)],
                        held.at[source, :, pl.ds(at, size)],
                        sems.at[n, d],
                    )
                )
                at += size
        for copy in copies:
            copy.start()
        for copy in copies:
            copy.wait()
        for h in range(outs):
            for r in range(per_half):
                source = place_ref[1 + h] * per_half + r
                real = held[source, 0].T * mask_ref[...]
                imag = held[source, 1].T * mask_ref[...]
                turned[h, 0, r, :, pl.ds(0, depth)] = real
                turned[h, 0, r, :, pl.ds(depth, depth)] = imag
                turned[h, 1, r, :, pl.ds(0, depth)] = imag
                turned[h, 1, r, :, pl.ds(depth, depth)] = -real

    right = held[column].reshape(2 * depth, inputs)
    for h in range(outs):
        left = turned[h].reshape(2 * per_half * inputs, 2 * depth)
        both = jnp.dot(left, right, preferred_element_type=jnp.float32)
        both = both.reshape(2, per_half * inputs, inputs)
        if sums:
            both = both + sum_refs[h][...]
        out_refs[h][...] = both.astype(out_refs[h].dtype)


def correlate(place, mask, pieces, picks, dtypes, sums, earlier):
    owners = len(pieces[0])
    inputs = pieces[0][0].shape[-1]
    depth = sum(size for _, size in picks)
    rows = owners // 2 * inputs
    operands = [value for piece in pieces for value in piece] + list(earlier)
    columns = pl.BlockSpec((2, rows, inputs), lambda b: (0, 0, b))
    anywhere = pl.BlockSpec(memory_space=pl.ANY)
    outs = len(dtypes)
    return pl.pallas_call(
        functools.partial(correlate_kernel, owners, picks, outs, len(sums)),
        grid=(owners,),
        out_shape=[jax.ShapeDtypeStruct((2, rows, owners * inputs), dtype) for dtype in dtypes],
        in_specs=[pl.BlockSpec(memory_space=pltpu.SMEM), pl.BlockSpec((1, depth), lambda b: (0, 0))]
        + [columns] * len(sums)
        + [anywhere] * len(operands),
        out_specs=[columns] * outs,
        scratch_shapes=[
            pltpu.VMEM((owners, 2, depth, inputs), jnp.bfloat16),
            pltpu.VMEM((outs, 2, owners // 2, inputs, 2 * depth), jnp.bfloat16),
            pltpu.SemaphoreType.DMA((len(pieces), owners)),
        ],
        compiler_params=pltpu.CompilerParams(vmem_limit_bytes=VMEM),
        cost_estimate=COST,
        name="correlate",
    )(place, mask, *sums, *operands)


def equalize_kernel(rows_ref, columns_ref, mine_ref, theirs_ref, *rest):
    out_ref = rest[-1]
    scale = rows_ref[...] * columns_ref[...]
    for part in range(2):
        total = mine_ref[part] + theirs_ref[part].astype(jnp.float32)
        out_ref[0, part] = total * scale


def equalize(row_scales, column_scales, mine, theirs, out, group, groups, waits):
    rows, columns = mine.shape[1:]
    block = rows // 4
    specs = [
        pl.BlockSpec((block, 1), lambda r: (r, 0)),
        pl.BlockSpec((1, columns), lambda r: (0, 0)),
        pl.BlockSpec((2, block, columns), lambda r: (0, r, 0)),
        pl.BlockSpec((2, block, columns), lambda r: (0, r, 0)),
    ]
    operands = [row_scales, column_scales, mine, theirs]
    aliases = {}
    if out is not None:
        specs.append(pl.BlockSpec(memory_space=pl.ANY))
        operands.append(out)
        aliases = {4: 0}
    specs += [pl.BlockSpec(memory_space=pl.ANY)] * len(waits)
    operands += waits
    return pl.pallas_call(
        equalize_kernel,
        grid=(rows // block,),
        out_shape=jax.ShapeDtypeStruct((groups, 2, rows, columns), jnp.float32),
        in_specs=specs,
        out_specs=pl.BlockSpec((1, 2, block, columns), lambda r: (group, 0, r, 0)),
        input_output_aliases=aliases,
        compiler_params=pltpu.CompilerParams(vmem_limit_bytes=VMEM),
        cost_estimate=COST,
        name="equalize",
    )(*operands)


def shift(value, d):
    count = lax.axis_size("station")
    return lax.ppermute(value, "station", [(s, (s + d) % count) for s in range(count)])


def passed_on(value):
    count = lax.axis_size("tm")
    return lax.ppermute(value, "tm", [(s, s + 1) for s in range(count - 1)])


def keep_table(flagged):
    fine = jnp.arange(SUBBAND_COUNT, dtype=jnp.int32)
    return jnp.all(flagged[:, :, None] != fine[None, None, :], axis=1).astype(jnp.float32)


def pipelined(volts, flagged):
    owners = lax.axis_size("station")
    keep_all = keep_table(flagged)
    kept = keep_all.reshape(-1, SUBBAND_COUNT // owners).sum(-1)
    spare = (SUBBAND_COUNT // owners - jnp.max(kept)).astype(jnp.int32)
    branches = [functools.partial(slotted, dropped) for dropped in range(DROPPED + 1)]
    return lax.switch(jnp.minimum(spare, DROPPED), branches, volts, keep_all)


def slotted(dropped, volts, keep_all):
    owners = lax.axis_size("station")
    me = lax.axis_index("station")
    half = lax.axis_index("tm")
    inputs = volts.shape[2]
    frames = volts.shape[3] // SUBBAND_COUNT
    frames_all = frames * lax.axis_size("tm")
    fine = SUBBAND_COUNT // owners
    groups = fine // GROUP
    blocks = frames // BLOCK
    slots = fine - dropped

    keep_mine = lax.dynamic_index_in_dim(keep_all, lax.axis_index("band"), 0, keepdims=False)
    twice = jnp.concatenate([keep_mine, keep_mine])
    keep_ahead = lax.dynamic_slice_in_dim(twice, me * fine, SUBBAND_COUNT, 0).reshape(owners, fine)

    earlier = np.tril(np.ones((fine, fine), np.float32), -1)
    flags = 1.0 - keep_ahead
    before = jnp.sum(flags[:, None, :] * earlier, -1)
    out_of = flags * (before < dropped)
    gone = jnp.minimum(before, float(dropped))
    place_of = jnp.where(out_of > 0, -1.0, np.arange(fine, dtype=np.float32) - gone)
    holds = place_of[:, None, :] == np.arange(slots, dtype=np.float32)[None, :, None]
    holds = holds.astype(jnp.float32)
    keep_slots = jnp.sum(holds * keep_ahead[:, None, :], -1).reshape(-1)
    channel_of = jnp.sum(holds * np.arange(fine, dtype=np.float32), -1)
    member = jnp.sum(holds[0].reshape(slots, groups, GROUP), -1)
    row_of = (channel_of + fine * np.arange(owners, dtype=np.float32)[:, None]).reshape(-1)
    row_of = (2.0 * row_of[:, None] + np.arange(2, dtype=np.float32)).reshape(-1)
    pick = row_of[:, None] == np.arange(2 * SUBBAND_COUNT, dtype=np.float32)[None, :]
    pick = pick.astype(jnp.bfloat16)

    rows = twiddle_values().reshape(owners, 2 * fine, 2 * SUBBAND_COUNT)
    turns = [np.roll(rows, -z, 0).reshape(2 * SUBBAND_COUNT, -1) for z in range(owners)]
    table = jnp.asarray(np.stack(turns).astype(jnp.bfloat16))
    window = np.broadcast_to(window_values()[:, :, None], (TAPS, SUBBAND_COUNT, 128))
    window = jnp.asarray(np.ascontiguousarray(window))
    spot = jnp.reshape(me, (1,)).astype(jnp.int32)

    parts, arrived, flat, out = [], [], [], None

    def send(n, waits):
        got = [parts[n][0]]
        for d in range(1, owners):
            gates = list(waits.get(d, ()))
            if len(flat) >= IN_FLIGHT and not (n == 1 and d == 2):
                gates.append(flat[len(flat) - IN_FLIGHT])
            value = after(parts[n][d], *gates) if gates else parts[n][d]
            with jax.named_scope(f"part{n}_shift{d}"):
                got.append(shift(value, d))
            flat.append(got[-1])
        arrived.append(got)

    power, halo, end = [], None, blocks
    for size in PARTS:
        end -= size
        spectra, part_power, tail = front(
            volts, None, end, size, (slots,), owners, keep_slots, spot, window, table, pick, halo is None
        )
        if tail is not None:
            halo = tail
        parts.append([x.reshape(2, slots * size * BLOCK, inputs) for x in spectra])
        power.append(part_power)
        if len(parts) == 1:
            send(0, {})
    with jax.named_scope("halo"):
        halo = passed_on(halo)
    sizes = (GROUP,) * (groups - 1) + (GROUP - dropped,)
    spectra, part_power, _ = front(
        volts, halo, 0, end, sizes, owners, keep_slots, spot, window, table, pick, False
    )
    power.append(part_power)
    for j in range(groups):
        parts.append(
            [spectra[d * groups + j].reshape(2, -1, inputs) for d in range(owners)]
        )

    local = jnp.sum(sum(power), axis=0)
    total = lax.psum(local, ("band", "tm"))
    scale = lax.rsqrt(total / (frames_all * jnp.sum(keep_all)) + 1e-06)
    scales = lax.all_gather(scale, "station", axis=0, tiled=True)
    kept = lax.dynamic_slice_in_dim(keep_mine, me * fine, fine, 0)
    counts = kept.reshape(groups, GROUP).sum(-1)
    denom = frames_all * jnp.maximum(counts, 1.0)
    per_half = scales.shape[0] // 2
    row_scales = lax.dynamic_slice_in_dim(scales, half * per_half, per_half, 0)

    column_scales = scales[None, :]
    row_scales = [(row_scales / denom[j])[:, None] for j in range(groups)]

    place = jnp.stack([me, 1 - half, half]).astype(jnp.int32)
    shared = len(PARTS)
    def to_other(j, theirs):
        with jax.named_scope(f"rows{j}"):
            return lax.ppermute(theirs, "tm", [(0, 1), (1, 0)])

    end_frames = end * BLOCK

    def multiply(j, place, dtypes, sums=(), earlier=(), begin=0, end=None):
        low, high = max(0, j * GROUP - dropped), min(slots, (j + 1) * GROUP)
        pieces = [(arrived[n], low, high, 0, PARTS[n] * BLOCK) for n in range(shared)]
        if end is None:
            pieces.append((arrived[shared + j], j * GROUP, high, j * GROUP, end_frames))
        if end is None and low < j * GROUP:
            pieces.append(
                (arrived[shared + j - 1], low, j * GROUP, (j - 1) * GROUP, end_frames)
            )
        pieces = pieces[begin:end]
        picks = tuple(((a - first) * size, (b - a) * size) for _, a, b, first, size in pieces)
        mask = jnp.concatenate([jnp.repeat(member[a:b, j], size) for _, a, b, _, size in pieces])
        mask = mask.astype(jnp.bfloat16)[None, :]
        return correlate(place, mask, [x[0] for x in pieces], picks, dtypes, sums, earlier)

    both = [jnp.bfloat16, jnp.float32]
    last_spectra = parts[shared][0]
    for n in range(1, shared):
        send(n, {d: [last_spectra, arrived[0][2]] for d in range(1, owners) if d != 2})
    send(shared, {owners - 1: [column_scales]})
    waiting = None
    for j in range(groups - 1):
        waits = {}
        if j == 0:
            partial = multiply(groups - 1, place, [jnp.float32] * 2, end=shared)
            waits = {owners - 1: partial}
        send(shared + j + 1, waits)
        theirs, mine = multiply(j, place, both)
        if waiting is not None:
            out = equalize(*waiting, out, j - 1, groups, [theirs])
        if j + 2 < groups:
            theirs = after(theirs, *arrived[shared + j + 1][1:])
        theirs = to_other(j, theirs)
        waiting = (row_scales[j], column_scales, mine, theirs)
    j = groups - 1
    theirs, mine = multiply(j, place, both, partial, [out], begin=shared)
    out = equalize(*waiting, out, groups - 2, groups, [theirs])
    theirs = to_other(j, theirs)
    out = equalize(row_scales[j], column_scales, mine, theirs, out, j, groups, [])
    return out[None]


def twiddle_table():
    values = twiddle_values().transpose(2, 1, 0)
    return jnp.asarray(values).astype(jnp.bfloat16)


def pair_products(left, right):
    swapped = jnp.stack([left[..., 1, :], -left[..., 0, :]], 4)
    real = jnp.einsum("cgfird,cgfjrd->icgj", left, right, preferred_element_type=jnp.float32)
    imag = jnp.einsum("cgfird,cgfjrd->icgj", swapped, right, preferred_element_type=jnp.float32)
    return jnp.stack([real, imag], 3)


def plain(volts, flagged):
    coarse_dev = volts.shape[1]
    inputs_dev = volts.shape[2]
    spec_count = volts.shape[3] // SUBBAND_COUNT
    frames_all = spec_count * lax.axis_size("tm")
    frames = volts.reshape(2, coarse_dev, inputs_dev, spec_count, SUBBAND_COUNT)
    history = passed_on(frames[:, :, :, spec_count - (TAPS - 1) :, :])
    padded = jnp.concatenate([history, frames], 3)
    window = jnp.asarray(window_values())
    filtered = jnp.zeros((2, coarse_dev, inputs_dev, spec_count, SUBBAND_COUNT), jnp.float32)
    for tap in range(TAPS):
        filtered = filtered + window[tap] * padded[:, :, :, tap : tap + spec_count, :].astype(
            jnp.float32
        )
    filtered = filtered.astype(jnp.bfloat16)
    joined = jnp.concatenate([filtered[0], filtered[1]], -1)
    spectra = jnp.einsum(
        "nqvx,xdl->nlqdv", joined, twiddle_table(), preferred_element_type=jnp.float32
    ).astype(jnp.bfloat16)
    keep_all = keep_table(flagged)
    keep_mine = lax.dynamic_slice_in_dim(
        keep_all, lax.axis_index("band") * coarse_dev, coarse_dev, 0
    )
    values = spectra.astype(jnp.float32)
    local = jnp.sum(values * values * keep_mine[:, :, None, None, None], axis=(0, 1, 3, 4))
    total = lax.psum(local, ("band", "tm"))
    scale = lax.rsqrt(total / (frames_all * jnp.sum(keep_all)) + 1e-06)
    scales = lax.all_gather(scale, "station", axis=0, tiled=True)
    received = lax.all_to_all(spectra, "station", split_axis=1, concat_axis=2, tiled=True)
    fine_dev = received.shape[1]
    inputs_all = received.shape[2]
    kept = lax.dynamic_slice_in_dim(keep_mine, lax.axis_index("station") * fine_dev, fine_dev, 1)
    groups_dev = fine_dev // GROUP
    masked = received * kept[:, :, None, None, None].astype(jnp.bfloat16)
    blocks = masked.reshape(coarse_dev, groups_dev, GROUP, inputs_all, 2, spec_count)
    rows = inputs_all // lax.axis_size("tm")
    summed = lax.psum_scatter(pair_products(blocks, blocks), "tm", scatter_dimension=0, tiled=True)
    counts = kept.reshape(coarse_dev, groups_dev, GROUP).sum(-1)
    denom = frames_all * jnp.maximum(counts, 1.0)
    row_scales = lax.dynamic_slice_in_dim(scales, lax.axis_index("tm") * rows, rows, 0)
    pairs = row_scales[:, None] * scales[None, :]
    ordered = jnp.transpose(summed, (1, 2, 3, 0, 4))
    return ordered * pairs[None, None, None, :, :] / denom[:, :, None, None, None]


def shards(volts, flagged):
    owners = lax.axis_size("station")
    frames = volts.shape[3] // SUBBAND_COUNT
    fits = (
        volts.shape[1] == 1
        and volts.shape[2] % 128 == 0
        and owners % 2 == 0
        and (SUBBAND_COUNT // owners) % GROUP == 0
        and lax.axis_size("tm") == 2
        and frames % BLOCK == 0
        and SUBBAND_COUNT // owners // GROUP > 1
        and frames // BLOCK > sum(PARTS)
    )
    return (pipelined if fits else plain)(volts, flagged)


def solution(mesh):
    placed = (P(None, "band", "station", "tm"), P())
    return jax.shard_map(
        shards,
        mesh=mesh,
        in_specs=placed,
        out_specs=P("band", "station", None, "tm", None),
        check_vma=False,
    )
```

```python
import functools
import math

import jax
import jax.numpy as jnp
import numpy as np
from jax import lax
from jax.experimental import pallas as pl
from jax.experimental.pallas import tpu as pltpu
from jax.sharding import PartitionSpec as P

SUBBAND_COUNT = 144
TAPS = 12
GROUP = 9
BLOCK = 16
PARTS = (1, 4)
RUNS = (1, 1, 1, 1)
SPREAD = BLOCK + 1
VMEM = 60 * 1024 * 1024
COST = pl.CostEstimate(flops=1024, bytes_accessed=1024, transcendentals=0)
IN_FLIGHT = 3


def window_values():
    total = TAPS * SUBBAND_COUNT
    place = np.arange(total, dtype=np.float64)
    shape = np.sinc((place - total / 2.0 + 0.5) / SUBBAND_COUNT)
    taper = 0.5 - 0.5 * np.cos(2.0 * math.pi * (place + 0.5) / total)
    return (shape * taper).reshape(TAPS, SUBBAND_COUNT).astype(np.float32)


def twiddle_values():
    f = np.arange(SUBBAND_COUNT, dtype=np.int64)[:, None]
    n = np.arange(SUBBAND_COUNT, dtype=np.int64)[None, :]
    angle = 2.0 * math.pi * (f * n % SUBBAND_COUNT) / SUBBAND_COUNT
    cosines, sines = np.cos(angle), np.sin(angle)
    real = np.concatenate([cosines, sines], 1)
    imag = np.concatenate([-sines, cosines], 1)
    return np.stack([real, imag], 1).astype(np.float32)


def front_kernel(
    runs, owners, turned, tail, me_ref, keep_ref, hist_ref, volts_ref, window_ref, table_ref, *rest
):
    splits = len(runs)
    outs, power_ref = rest[: owners * splits], rest[owners * splits]
    tail_ref = rest[owners * splits + 1] if tail else None
    homes = [(q, place) for q, run in enumerate(runs) for place in range(run)]
    ring, filt, spread = rest[-3:]
    step = pl.program_id(0)
    now = lax.rem(step, 2)
    before = 1 - now
    inputs = ring.shape[-1]
    tiles = inputs // 128
    span = BLOCK * SUBBAND_COUNT
    skipped = (BLOCK + 1 - TAPS) * SUBBAND_COUNT

    def turn(ref, slot, begin):
        def columns(c, _):
            at = pl.multiple_of(c * 128, 128)
            for part in range(2):
                ring[slot, part, pl.ds(at, 128), :] = ref[part, 0, :, pl.ds(at, 128)].T
            return 0

        lax.fori_loop(begin, span // 128, columns, 0, unroll=6 if begin == 0 else 5)

    @pl.when(step == 0)
    def _():
        if turned:
            for part in range(2):
                ring[1, part, pl.ds(skipped, span - skipped), :] = hist_ref[part]
        else:
            turn(hist_ref, 1, 3)
        power_ref[...] = jnp.zeros_like(power_ref)

    turn(volts_ref, now, 0)
    if tail:
        for part in range(2):
            tail_ref[part] = ring[now, part, pl.ds(skipped, span - skipped), :]

    def filter_rows(j, _):
        base = pl.multiple_of(j * 16, 16)
        for tile in range(tiles):
            lanes = pl.ds(tile * 128, 128)
            weights = [window_ref[k, pl.ds(base, 16), :] for k in range(TAPS)]
            for part in range(2):
                samples = []
                for t in range(1 - TAPS, BLOCK):
                    slot, frame = (now, t) if t >= 0 else (before, BLOCK + t)
                    at = pl.multiple_of(frame * SUBBAND_COUNT + base, 16)
                    samples.append(ring[slot, part, pl.ds(at, 16), lanes].astype(jnp.float32))
                for t in range(BLOCK):
                    total = weights[0] * samples[t]
                    for k in range(1, TAPS):
                        total = total + weights[k] * samples[t + k]
                    at = pl.multiple_of(part * SUBBAND_COUNT + base, 16)
                    filt[t, pl.ds(at, 16), lanes] = total.astype(jnp.bfloat16)
        return 0

    lax.fori_loop(0, SUBBAND_COUNT // 16, filter_rows, 0)

    def transform(t, _):
        result = jnp.dot(table_ref[0], filt[t], preferred_element_type=jnp.float32)
        for tile in range(tiles):
            spread[tile, pl.ds(t, 2 * SUBBAND_COUNT, stride=SPREAD), :] = result[
                :, tile * 128 : (tile + 1) * 128
            ]
        return 0

    lax.fori_loop(0, BLOCK, transform, 0, unroll=4)

    groups = SUBBAND_COUNT // owners // GROUP
    power = [jnp.zeros((BLOCK, 128), jnp.float32) for _ in range(tiles)]
    for d in range(owners):
        for j in range(groups):
            q, place = homes[j]
            out = outs[d * splits + q]

            def channel(f, power, d=d, j=j, out=out, place=place):
                keep = keep_ref[(d * groups + j) * GROUP + f]
                power = list(power)
                for part in range(2):
                    row = ((d * groups + j) * 2 + part) * GROUP + f
                    for tile in range(tiles):
                        value = spread[tile, pl.ds(row * SPREAD, BLOCK), :] * keep
                        value = value.astype(jnp.bfloat16)
                        out[place, part, f, :, tile * 128 : (tile + 1) * 128] = value
                        value = value.astype(jnp.float32)
                        power[tile] = power[tile] + value * value
                return tuple(power)

            power = lax.fori_loop(0, GROUP, channel, tuple(power), unroll=3)
    for tile in range(tiles):
        power_ref[:, tile * 128 : (tile + 1) * 128] += power[tile]


def front(volts, hist, first, steps, runs, owners, keep, me, window, table, tail):
    inputs = volts.shape[2]
    span = BLOCK * SUBBAND_COUNT
    frames = steps * BLOCK
    outs, out_specs = [], []
    for _ in range(owners):
        for run in runs:
            outs.append(jax.ShapeDtypeStruct((run, 2, GROUP, frames, inputs), jnp.bfloat16))
            out_specs.append(
                pl.BlockSpec((run, 2, GROUP, BLOCK, inputs), lambda s, me: (0, 0, 0, s, 0))
            )
    outs.append(jax.ShapeDtypeStruct((BLOCK, inputs), jnp.float32))
    out_specs.append(pl.BlockSpec((BLOCK, inputs), lambda s, me: (0, 0)))
    kept = (TAPS - 1) * SUBBAND_COUNT
    if tail:
        outs.append(jax.ShapeDtypeStruct((2, kept, inputs), jnp.bfloat16))
        out_specs.append(pl.BlockSpec((2, kept, inputs), lambda s, me: (0, 0, 0)))
    if hist is None:
        hist, hist_spec = volts, pl.BlockSpec((2, 1, inputs, span), lambda s, me: (0, 0, 0, first - 1))
        turned = False
    else:
        hist_spec, turned = pl.BlockSpec((2, kept, inputs), lambda s, me: (0, 0, 0)), True
    result = pl.pallas_call(
        functools.partial(front_kernel, runs, owners, turned, tail),
        grid_spec=pltpu.PrefetchScalarGridSpec(
            num_scalar_prefetch=1,
            grid=(steps,),
            in_specs=[
                pl.BlockSpec(memory_space=pltpu.SMEM),
                hist_spec,
                pl.BlockSpec((2, 1, inputs, span), lambda s, me: (0, 0, 0, first + s)),
                pl.BlockSpec(window.shape, lambda s, me: (0, 0, 0)),
                pl.BlockSpec((1, *table.shape[1:]), lambda s, me: (me[0], 0, 0)),
            ],
            out_specs=out_specs,
            scratch_shapes=[
                pltpu.VMEM((2, 2, span, inputs), jnp.bfloat16),
                pltpu.VMEM((BLOCK, 2 * SUBBAND_COUNT, inputs), jnp.bfloat16),
                pltpu.VMEM((inputs // 128, 2 * SUBBAND_COUNT * SPREAD, 128), jnp.float32),
            ],
        ),
        out_shape=outs,
        compiler_params=pltpu.CompilerParams(vmem_limit_bytes=VMEM),
        cost_estimate=COST,
        name="front",
    )(me, keep, hist, volts, window, table)
    count = owners * len(runs)
    return result[:count], result[count], result[count + 1] if tail else None


def after_kernel(*refs):
    pass


def after(value, *others):
    anywhere = pl.BlockSpec(memory_space=pl.ANY)
    return pl.pallas_call(
        after_kernel,
        out_shape=jax.ShapeDtypeStruct(value.shape, value.dtype),
        in_specs=[anywhere] * (1 + len(others)),
        out_specs=anywhere,
        input_output_aliases={0: 0},
        cost_estimate=COST,
        name="after",
    )(value, *others)


def correlate_kernel(owners, picks, outs, sums, place_ref, *rest):
    count = len(picks)
    sum_refs, rest = rest[:sums], rest[sums:]
    pieces = [rest[n * owners : (n + 1) * owners] for n in range(count)]
    out_refs, (held, turned, sems) = rest[-3 - outs : -3], rest[-3:]
    me = place_ref[0]
    column = pl.program_id(0)
    per_half = owners // 2
    inputs, depth = turned.shape[3], held.shape[2]

    @pl.when(column == 0)
    def _():
        copies = []
        for d in range(owners):
            source = lax.rem(me - d + owners, owners)
            at = 0
            for n in range(count):
                size = pieces[n][d].shape[2]
                copies.append(
                    pltpu.make_async_copy(
                        pieces[n][d].at[picks[n]], held.at[source, :, pl.ds(at, size)], sems.at[n, d]
                    )
                )
                at += size
        for copy in copies:
            copy.start()
        for copy in copies:
            copy.wait()
        for h in range(outs):
            for r in range(per_half):
                source = place_ref[1 + h] * per_half + r
                real, imag = held[source, 0].T, held[source, 1].T
                turned[h, 0, r, :, pl.ds(0, depth)] = real
                turned[h, 0, r, :, pl.ds(depth, depth)] = imag
                turned[h, 1, r, :, pl.ds(0, depth)] = imag
                turned[h, 1, r, :, pl.ds(depth, depth)] = -real

    right = held[column].reshape(2 * depth, inputs)
    for h in range(outs):
        left = turned[h].reshape(2 * per_half * inputs, 2 * depth)
        both = jnp.dot(left, right, preferred_element_type=jnp.float32)
        both = both.reshape(2, per_half * inputs, inputs)
        if sums:
            both = both + sum_refs[h][...]
        out_refs[h][...] = both.astype(out_refs[h].dtype)


def correlate(place, pieces, picks, dtypes, sums, earlier):
    owners = len(pieces[0])
    inputs = pieces[0][0].shape[-1]
    depth = sum(piece[0].shape[2] for piece in pieces)
    rows = owners // 2 * inputs
    operands = [value for piece in pieces for value in piece] + list(earlier)
    columns = pl.BlockSpec((2, rows, inputs), lambda b: (0, 0, b))
    anywhere = pl.BlockSpec(memory_space=pl.ANY)
    outs = len(dtypes)
    return pl.pallas_call(
        functools.partial(correlate_kernel, owners, picks, outs, len(sums)),
        grid=(owners,),
        out_shape=[jax.ShapeDtypeStruct((2, rows, owners * inputs), dtype) for dtype in dtypes],
        in_specs=[pl.BlockSpec(memory_space=pltpu.SMEM)]
        + [columns] * len(sums)
        + [anywhere] * len(operands),
        out_specs=[columns] * outs,
        scratch_shapes=[
            pltpu.VMEM((owners, 2, depth, inputs), jnp.bfloat16),
            pltpu.VMEM((outs, 2, owners // 2, inputs, 2 * depth), jnp.bfloat16),
            pltpu.SemaphoreType.DMA((len(pieces), owners)),
        ],
        compiler_params=pltpu.CompilerParams(vmem_limit_bytes=VMEM),
        cost_estimate=COST,
        name="correlate",
    )(place, *sums, *operands)


def equalize_kernel(rows_ref, columns_ref, mine_ref, theirs_ref, *rest):
    out_ref = rest[-1]
    rows = rows_ref.shape[1]
    by_row = jnp.broadcast_to(rows_ref[...], (rows, rows)).T
    for at in range(0, columns_ref.shape[1], rows):
        columns = slice(at, at + rows)
        scale = by_row * columns_ref[:, columns]
        for part in range(2):
            total = mine_ref[part, :, columns] + theirs_ref[part, :, columns].astype(jnp.float32)
            out_ref[0, part, :, columns] = total * scale


def equalize(row_scales, column_scales, mine, theirs, out, group, groups, waits):
    rows, columns = mine.shape[1:]
    block = 128
    specs = [
        pl.BlockSpec((1, block), lambda r: (0, r)),
        pl.BlockSpec((1, columns), lambda r: (0, 0)),
        pl.BlockSpec((2, block, columns), lambda r: (0, r, 0)),
        pl.BlockSpec((2, block, columns), lambda r: (0, r, 0)),
    ]
    operands = [row_scales, column_scales, mine, theirs]
    aliases = {}
    if out is not None:
        specs.append(pl.BlockSpec(memory_space=pl.ANY))
        operands.append(out)
        aliases = {4: 0}
    specs += [pl.BlockSpec(memory_space=pl.ANY)] * len(waits)
    operands += waits
    return pl.pallas_call(
        equalize_kernel,
        grid=(rows // block,),
        out_shape=jax.ShapeDtypeStruct((groups, 2, rows, columns), jnp.float32),
        in_specs=specs,
        out_specs=pl.BlockSpec((1, 2, block, columns), lambda r: (group, 0, r, 0)),
        input_output_aliases=aliases,
        compiler_params=pltpu.CompilerParams(vmem_limit_bytes=VMEM),
        cost_estimate=COST,
        name="equalize",
    )(*operands)


def shift(value, d):
    count = lax.axis_size("station")
    return lax.ppermute(value, "station", [(s, (s + d) % count) for s in range(count)])


def passed_on(value):
    count = lax.axis_size("tm")
    return lax.ppermute(value, "tm", [(s, s + 1) for s in range(count - 1)])


def keep_table(flagged):
    fine = jnp.arange(SUBBAND_COUNT, dtype=jnp.int32)
    return jnp.all(flagged[:, :, None] != fine[None, None, :], axis=1).astype(jnp.float32)


def pipelined(volts, flagged):
    owners = lax.axis_size("station")
    me = lax.axis_index("station")
    half = lax.axis_index("tm")
    inputs = volts.shape[2]
    frames = volts.shape[3] // SUBBAND_COUNT
    frames_all = frames * lax.axis_size("tm")
    fine = SUBBAND_COUNT // owners
    groups = fine // GROUP
    blocks = frames // BLOCK

    keep_all = keep_table(flagged)
    keep_mine = lax.dynamic_index_in_dim(keep_all, lax.axis_index("band"), 0, keepdims=False)
    twice = jnp.concatenate([keep_mine, keep_mine])
    keep_ahead = lax.dynamic_slice_in_dim(twice, me * fine, SUBBAND_COUNT, 0)

    rows = twiddle_values().reshape(owners, groups, GROUP, 2, 2 * SUBBAND_COUNT)
    rows = rows.transpose(0, 1, 3, 2, 4)
    turns = [np.roll(rows, -z, 0).reshape(2 * SUBBAND_COUNT, -1) for z in range(owners)]
    table = jnp.asarray(np.stack(turns).astype(jnp.bfloat16))
    window = np.broadcast_to(window_values()[:, :, None], (TAPS, SUBBAND_COUNT, 128))
    window = jnp.asarray(np.ascontiguousarray(window))
    spot = jnp.reshape(me, (1,)).astype(jnp.int32)

    if groups != sum(RUNS):
        runs = (1,) * groups
    else:
        runs = RUNS
    parts, arrived, flat, out = [], [], [], None

    def send(n, waits):
        got = [parts[n][0]]
        for d in range(1, owners):
            gates = list(waits.get(d, ()))
            if len(flat) >= IN_FLIGHT and not (n == 1 and d == 2):
                gates.append(flat[len(flat) - IN_FLIGHT])
            value = after(parts[n][d], *gates) if gates else parts[n][d]
            with jax.named_scope(f"part{n}_shift{d}"):
                got.append(shift(value, d))
            flat.append(got[-1])
        arrived.append(got)

    power, halo, end = [], None, blocks
    for size in PARTS:
        end -= size
        spectra, part_power, tail = front(
            volts, None, end, size, (groups,), owners, keep_ahead, spot, window, table, halo is None
        )
        if tail is not None:
            halo = tail
        parts.append([x.reshape(groups, 2, GROUP * size * BLOCK, inputs) for x in spectra])
        power.append(part_power)
        if len(parts) == 1:
            send(0, {})
    with jax.named_scope("halo"):
        halo = passed_on(halo)
    spectra, part_power, _ = front(
        volts, halo, 0, end, runs, owners, keep_ahead, spot, window, table, False
    )
    power.append(part_power)
    for q, run in enumerate(runs):
        parts.append(
            [
                spectra[d * len(runs) + q].reshape(run, 2, GROUP * end * BLOCK, inputs)
                for d in range(owners)
            ]
        )

    local = jnp.sum(sum(power), axis=0)
    total = lax.psum(local, ("band", "tm"))
    scale = lax.rsqrt(total / (frames_all * jnp.sum(keep_all)) + 1e-06)
    scales = lax.all_gather(scale, "station", axis=0, tiled=True)
    kept = lax.dynamic_slice_in_dim(keep_mine, me * fine, fine, 0)
    counts = kept.reshape(groups, GROUP).sum(-1)
    denom = frames_all * jnp.maximum(counts, 1.0)
    per_half = scales.shape[0] // 2
    row_scales = lax.dynamic_slice_in_dim(scales, half * per_half, per_half, 0)

    column_scales = scales[None, :]
    row_scales = [(row_scales / denom[j])[None, :] for j in range(groups)]

    place = jnp.stack([me, 1 - half, half]).astype(jnp.int32)
    shared = len(PARTS)
    def to_other(j, theirs):
        with jax.named_scope(f"rows{j}"):
            return lax.ppermute(theirs, "tm", [(0, 1), (1, 0)])

    homes = [(q, at) for q, run in enumerate(runs) for at in range(run)]

    def multiply(j, place, dtypes, sums=(), earlier=(), begin=0, end=shared + 1):
        q, at = homes[j]
        pieces = arrived[:shared] + arrived[shared + q : shared + q + 1]
        picks = (j,) * shared + (at,)
        return correlate(place, pieces[begin:end], picks[begin:end], dtypes, sums, earlier)

    both = [jnp.bfloat16, jnp.float32]
    last_spectra = parts[shared][0]
    for n in range(1, shared):
        send(n, {d: [last_spectra, arrived[0][2]] for d in range(1, owners) if d != 2})
    send(shared, {owners - 1: [column_scales]})
    partial = multiply(groups - 1, place, [jnp.float32] * 2, end=shared)
    waiting = []

    def settle(out, earlier):
        for j, mine, theirs in waiting:
            out = equalize(row_scales[j], column_scales, mine, theirs, out, j, groups, earlier)
        waiting.clear()
        return out

    done = 0
    for q, run in enumerate(runs[:-1]):
        send(shared + q + 1, {owners - 1: partial} if q == 0 else {})
        results = [multiply(j, place, both) for j in range(done, done + run)]
        if waiting:
            out = settle(out, [x[0] for x in results])
        for j, (theirs, mine) in enumerate(results, done):
            if q + 2 < len(runs):
                theirs = after(theirs, *arrived[shared + q + 1][1:])
            waiting.append((j, mine, to_other(j, theirs)))
        done += run
    j = groups - 1
    theirs, mine = multiply(j, place, both, partial, [] if out is None else [out], begin=shared)
    out = settle(out, [theirs])
    waiting.append((j, mine, to_other(j, theirs)))
    out = settle(out, [])
    return out[None]


def twiddle_table():
    values = twiddle_values().transpose(2, 1, 0)
    return jnp.asarray(values).astype(jnp.bfloat16)


def pair_products(left, right):
    swapped = jnp.stack([left[..., 1, :], -left[..., 0, :]], 4)
    real = jnp.einsum("cgfird,cgfjrd->icgj", left, right, preferred_element_type=jnp.float32)
    imag = jnp.einsum("cgfird,cgfjrd->icgj", swapped, right, preferred_element_type=jnp.float32)
    return jnp.stack([real, imag], 3)


def plain(volts, flagged):
    coarse_dev = volts.shape[1]
    inputs_dev = volts.shape[2]
    spec_count = volts.shape[3] // SUBBAND_COUNT
    frames_all = spec_count * lax.axis_size("tm")
    frames = volts.reshape(2, coarse_dev, inputs_dev, spec_count, SUBBAND_COUNT)
    history = passed_on(frames[:, :, :, spec_count - (TAPS - 1) :, :])
    padded = jnp.concatenate([history, frames], 3)
    window = jnp.asarray(window_values())
    filtered = jnp.zeros((2, coarse_dev, inputs_dev, spec_count, SUBBAND_COUNT), jnp.float32)
    for tap in range(TAPS):
        filtered = filtered + window[tap] * padded[:, :, :, tap : tap + spec_count, :].astype(
            jnp.float32
        )
    filtered = filtered.astype(jnp.bfloat16)
    joined = jnp.concatenate([filtered[0], filtered[1]], -1)
    spectra = jnp.einsum(
        "nqvx,xdl->nlqdv", joined, twiddle_table(), preferred_element_type=jnp.float32
    ).astype(jnp.bfloat16)
    keep_all = keep_table(flagged)
    keep_mine = lax.dynamic_slice_in_dim(
        keep_all, lax.axis_index("band") * coarse_dev, coarse_dev, 0
    )
    values = spectra.astype(jnp.float32)
    local = jnp.sum(values * values * keep_mine[:, :, None, None, None], axis=(0, 1, 3, 4))
    total = lax.psum(local, ("band", "tm"))
    scale = lax.rsqrt(total / (frames_all * jnp.sum(keep_all)) + 1e-06)
    scales = lax.all_gather(scale, "station", axis=0, tiled=True)
    received = lax.all_to_all(spectra, "station", split_axis=1, concat_axis=2, tiled=True)
    fine_dev = received.shape[1]
    inputs_all = received.shape[2]
    kept = lax.dynamic_slice_in_dim(keep_mine, lax.axis_index("station") * fine_dev, fine_dev, 1)
    groups_dev = fine_dev // GROUP
    masked = received * kept[:, :, None, None, None].astype(jnp.bfloat16)
    blocks = masked.reshape(coarse_dev, groups_dev, GROUP, inputs_all, 2, spec_count)
    rows = inputs_all // lax.axis_size("tm")
    summed = lax.psum_scatter(pair_products(blocks, blocks), "tm", scatter_dimension=0, tiled=True)
    counts = kept.reshape(coarse_dev, groups_dev, GROUP).sum(-1)
    denom = frames_all * jnp.maximum(counts, 1.0)
    row_scales = lax.dynamic_slice_in_dim(scales, lax.axis_index("tm") * rows, rows, 0)
    pairs = row_scales[:, None] * scales[None, :]
    ordered = jnp.transpose(summed, (1, 2, 3, 0, 4))
    return ordered * pairs[None, None, None, :, :] / denom[:, :, None, None, None]


def shards(volts, flagged):
    owners = lax.axis_size("station")
    frames = volts.shape[3] // SUBBAND_COUNT
    fits = (
        volts.shape[1] == 1
        and volts.shape[2] % 128 == 0
        and owners % 2 == 0
        and (SUBBAND_COUNT // owners) % GROUP == 0
        and lax.axis_size("tm") == 2
        and frames % BLOCK == 0
        and SUBBAND_COUNT // owners // GROUP > 1
        and owners * volts.shape[2] // 2 % 128 == 0
        and frames // BLOCK > sum(PARTS)
    )
    return (pipelined if fits else plain)(volts, flagged)


def solution(mesh):
    placed = (P(None, "band", "station", "tm"), P())
    return jax.shard_map(
        shards,
        mesh=mesh,
        in_specs=placed,
        out_specs=P("band", "station", None, "tm", None),
        check_vma=False,
    )
```

```python
import functools
import math

import jax
import jax.numpy as jnp
import numpy as np
from jax import lax
from jax.experimental import pallas as pl
from jax.experimental.pallas import tpu as pltpu
from jax.sharding import PartitionSpec as P

SUBBAND_COUNT = 144
TAPS = 12
GROUP = 9
BLOCK = 16
PARTS = (1, 4)
RUNS = (1, 1, 1, 1)
SPREAD = BLOCK + 1
VMEM = 62 * 1024 * 1024
COST = pl.CostEstimate(flops=1024, bytes_accessed=1024, transcendentals=0)
IN_FLIGHT = 3


def window_values():
    total = TAPS * SUBBAND_COUNT
    place = np.arange(total, dtype=np.float64)
    shape = np.sinc((place - total / 2.0 + 0.5) / SUBBAND_COUNT)
    taper = 0.5 - 0.5 * np.cos(2.0 * math.pi * (place + 0.5) / total)
    return (shape * taper).reshape(TAPS, SUBBAND_COUNT).astype(np.float32)


def twiddle_values():
    f = np.arange(SUBBAND_COUNT, dtype=np.int64)[:, None]
    n = np.arange(SUBBAND_COUNT, dtype=np.int64)[None, :]
    angle = 2.0 * math.pi * (f * n % SUBBAND_COUNT) / SUBBAND_COUNT
    cosines, sines = np.cos(angle), np.sin(angle)
    real = np.concatenate([cosines, sines], 1)
    imag = np.concatenate([-sines, cosines], 1)
    return np.stack([real, imag], 1).astype(np.float32)


def front_kernel(
    runs, owners, turned, tail, me_ref, keep_ref, hist_ref, volts_ref, window_ref, table_ref, *rest
):
    splits = len(runs)
    outs, power_ref = rest[: owners * splits], rest[owners * splits]
    tail_ref = rest[owners * splits + 1] if tail else None
    homes = [(q, place) for q, run in enumerate(runs) for place in range(run)]
    ring, filt, spread = rest[-3:]
    step = pl.program_id(0)
    now = lax.rem(step, 2)
    before = 1 - now
    inputs = ring.shape[-1]
    tiles = inputs // 128
    span = BLOCK * SUBBAND_COUNT
    skipped = (BLOCK + 1 - TAPS) * SUBBAND_COUNT

    def turn(ref, slot, begin):
        def columns(c, _):
            at = pl.multiple_of(c * 128, 128)
            for part in range(2):
                ring[slot, part, pl.ds(at, 128), :] = ref[part, 0, :, pl.ds(at, 128)].T
            return 0

        lax.fori_loop(begin, span // 128, columns, 0, unroll=6 if begin == 0 else 5)

    @pl.when(step == 0)
    def _():
        if turned:
            for part in range(2):
                ring[1, part, pl.ds(skipped, span - skipped), :] = hist_ref[part]
        else:
            turn(hist_ref, 1, 3)
        power_ref[...] = jnp.zeros_like(power_ref)

    turn(volts_ref, now, 0)
    if tail:
        for part in range(2):
            tail_ref[part] = ring[now, part, pl.ds(skipped, span - skipped), :]

    def filter_rows(j, _):
        base = pl.multiple_of(j * 16, 16)
        for tile in range(tiles):
            lanes = pl.ds(tile * 128, 128)
            weights = [window_ref[k, pl.ds(base, 16), :] for k in range(TAPS)]
            for part in range(2):
                samples = []
                for t in range(1 - TAPS, BLOCK):
                    slot, frame = (now, t) if t >= 0 else (before, BLOCK + t)
                    at = pl.multiple_of(frame * SUBBAND_COUNT + base, 16)
                    samples.append(ring[slot, part, pl.ds(at, 16), lanes].astype(jnp.float32))
                for t in range(BLOCK):
                    total = weights[0] * samples[t]
                    for k in range(1, TAPS):
                        total = total + weights[k] * samples[t + k]
                    at = pl.multiple_of(part * SUBBAND_COUNT + base, 16)
                    filt[t, pl.ds(at, 16), lanes] = total.astype(jnp.bfloat16)
        return 0

    lax.fori_loop(0, SUBBAND_COUNT // 16, filter_rows, 0)

    def transform(t, _):
        result = jnp.dot(table_ref[0], filt[t], preferred_element_type=jnp.float32)
        for tile in range(tiles):
            spread[tile, pl.ds(t, 2 * SUBBAND_COUNT, stride=SPREAD), :] = result[
                :, tile * 128 : (tile + 1) * 128
            ]
        return 0

    lax.fori_loop(0, BLOCK, transform, 0, unroll=4)

    groups = SUBBAND_COUNT // owners // GROUP
    power = [jnp.zeros((BLOCK, 128), jnp.float32) for _ in range(tiles)]
    for d in range(owners):
        for j in range(groups):
            q, place = homes[j]
            out = outs[d * splits + q]

            def channel(f, power, d=d, j=j, out=out, place=place):
                keep = keep_ref[(d * groups + j) * GROUP + f]
                power = list(power)
                for part in range(2):
                    row = ((d * groups + j) * 2 + part) * GROUP + f
                    for tile in range(tiles):
                        value = spread[tile, pl.ds(row * SPREAD, BLOCK), :] * keep
                        value = value.astype(jnp.bfloat16)
                        out[place, part, f, :, tile * 128 : (tile + 1) * 128] = value
                        value = value.astype(jnp.float32)
                        power[tile] = power[tile] + value * value
                return tuple(power)

            power = lax.fori_loop(0, GROUP, channel, tuple(power), unroll=3)
    for tile in range(tiles):
        power_ref[:, tile * 128 : (tile + 1) * 128] += power[tile]


def front(volts, hist, first, steps, runs, owners, keep, me, window, table, tail):
    inputs = volts.shape[2]
    span = BLOCK * SUBBAND_COUNT
    frames = steps * BLOCK
    outs, out_specs = [], []
    for _ in range(owners):
        for run in runs:
            outs.append(jax.ShapeDtypeStruct((run, 2, GROUP, frames, inputs), jnp.bfloat16))
            out_specs.append(
                pl.BlockSpec((run, 2, GROUP, BLOCK, inputs), lambda s, me: (0, 0, 0, s, 0))
            )
    outs.append(jax.ShapeDtypeStruct((BLOCK, inputs), jnp.float32))
    out_specs.append(pl.BlockSpec((BLOCK, inputs), lambda s, me: (0, 0)))
    kept = (TAPS - 1) * SUBBAND_COUNT
    if tail:
        outs.append(jax.ShapeDtypeStruct((2, kept, inputs), jnp.bfloat16))
        out_specs.append(pl.BlockSpec((2, kept, inputs), lambda s, me: (0, 0, 0)))
    if hist is None:
        hist, hist_spec = volts, pl.BlockSpec((2, 1, inputs, span), lambda s, me: (0, 0, 0, first - 1))
        turned = False
    else:
        hist_spec, turned = pl.BlockSpec((2, kept, inputs), lambda s, me: (0, 0, 0)), True
    result = pl.pallas_call(
        functools.partial(front_kernel, runs, owners, turned, tail),
        grid_spec=pltpu.PrefetchScalarGridSpec(
            num_scalar_prefetch=1,
            grid=(steps,),
            in_specs=[
                pl.BlockSpec(memory_space=pltpu.SMEM),
                hist_spec,
                pl.BlockSpec((2, 1, inputs, span), lambda s, me: (0, 0, 0, first + s)),
                pl.BlockSpec(window.shape, lambda s, me: (0, 0, 0)),
                pl.BlockSpec((1, *table.shape[1:]), lambda s, me: (me[0], 0, 0)),
            ],
            out_specs=out_specs,
            scratch_shapes=[
                pltpu.VMEM((2, 2, span, inputs), jnp.bfloat16),
                pltpu.VMEM((BLOCK, 2 * SUBBAND_COUNT, inputs), jnp.bfloat16),
                pltpu.VMEM((inputs // 128, 2 * SUBBAND_COUNT * SPREAD, 128), jnp.float32),
            ],
        ),
        out_shape=outs,
        compiler_params=pltpu.CompilerParams(vmem_limit_bytes=VMEM),
        cost_estimate=COST,
        name="front",
    )(me, keep, hist, volts, window, table)
    count = owners * len(runs)
    return result[:count], result[count], result[count + 1] if tail else None


def after_kernel(*refs):
    pass


def after(value, *others):
    anywhere = pl.BlockSpec(memory_space=pl.ANY)
    return pl.pallas_call(
        after_kernel,
        out_shape=jax.ShapeDtypeStruct(value.shape, value.dtype),
        in_specs=[anywhere] * (1 + len(others)),
        out_specs=anywhere,
        input_output_aliases={0: 0},
        cost_estimate=COST,
        name="after",
    )(value, *others)


def correlate_kernel(owners, picks, outs, sums, place_ref, *rest):
    count = len(picks)
    sum_refs, rest = rest[:sums], rest[sums:]
    pieces = [rest[n * owners : (n + 1) * owners] for n in range(count)]
    out_refs, (held, turned, sems) = rest[-3 - outs : -3], rest[-3:]
    me = place_ref[0]
    column = pl.program_id(0)
    per_half = owners // 2
    inputs, depth = turned.shape[3], held.shape[2]

    @pl.when(column == 0)
    def _():
        copies = []
        for d in range(owners):
            source = lax.rem(me - d + owners, owners)
            at = 0
            for n in range(count):
                size = pieces[n][d].shape[2]
                copies.append(
                    pltpu.make_async_copy(
                        pieces[n][d].at[picks[n]], held.at[source, :, pl.ds(at, size)], sems.at[n, d]
                    )
                )
                at += size
        for copy in copies:
            copy.start()
        for copy in copies:
            copy.wait()
        for h in range(outs):
            for r in range(per_half):
                source = place_ref[1 + h] * per_half + r
                real, imag = held[source, 0].T, held[source, 1].T
                turned[h, 0, r, :, pl.ds(0, depth)] = real
                turned[h, 0, r, :, pl.ds(depth, depth)] = imag
                turned[h, 1, r, :, pl.ds(0, depth)] = imag
                turned[h, 1, r, :, pl.ds(depth, depth)] = -real

    right = held[column].reshape(2 * depth, inputs)
    for h in range(outs):
        left = turned[h].reshape(2 * per_half * inputs, 2 * depth)
        both = jnp.dot(left, right, preferred_element_type=jnp.float32)
        both = both.reshape(2, per_half * inputs, inputs)
        if sums:
            both = both + sum_refs[h][...]
        out_refs[h][...] = both.astype(out_refs[h].dtype)


def correlate(place, pieces, picks, dtypes, sums, earlier):
    owners = len(pieces[0])
    inputs = pieces[0][0].shape[-1]
    depth = sum(piece[0].shape[2] for piece in pieces)
    rows = owners // 2 * inputs
    operands = [value for piece in pieces for value in piece] + list(earlier)
    columns = pl.BlockSpec((2, rows, inputs), lambda b: (0, 0, b))
    anywhere = pl.BlockSpec(memory_space=pl.ANY)
    outs = len(dtypes)
    return pl.pallas_call(
        functools.partial(correlate_kernel, owners, picks, outs, len(sums)),
        grid=(owners,),
        out_shape=[jax.ShapeDtypeStruct((2, rows, owners * inputs), dtype) for dtype in dtypes],
        in_specs=[pl.BlockSpec(memory_space=pltpu.SMEM)]
        + [columns] * len(sums)
        + [anywhere] * len(operands),
        out_specs=[columns] * outs,
        scratch_shapes=[
            pltpu.VMEM((owners, 2, depth, inputs), jnp.bfloat16),
            pltpu.VMEM((outs, 2, owners // 2, inputs, 2 * depth), jnp.bfloat16),
            pltpu.SemaphoreType.DMA((len(pieces), owners)),
        ],
        compiler_params=pltpu.CompilerParams(vmem_limit_bytes=VMEM),
        cost_estimate=COST,
        name="correlate",
    )(place, *sums, *operands)


def equalize_kernel(rows_ref, columns_ref, mine_ref, theirs_ref, *rest):
    out_ref = rest[-1]
    rows = rows_ref.shape[1]
    by_row = jnp.broadcast_to(rows_ref[...], (rows, rows)).T
    for at in range(0, columns_ref.shape[1], rows):
        columns = slice(at, at + rows)
        scale = by_row * columns_ref[:, columns]
        for part in range(2):
            total = mine_ref[part, :, columns] + theirs_ref[part, :, columns].astype(jnp.float32)
            out_ref[0, part, :, columns] = total * scale


def equalize(row_scales, column_scales, mine, theirs, out, group, groups, waits):
    rows, columns = mine.shape[1:]
    block = 128
    specs = [
        pl.BlockSpec((1, block), lambda r: (0, r)),
        pl.BlockSpec((1, columns), lambda r: (0, 0)),
        pl.BlockSpec((2, block, columns), lambda r: (0, r, 0)),
        pl.BlockSpec((2, block, columns), lambda r: (0, r, 0)),
    ]
    operands = [row_scales, column_scales, mine, theirs]
    aliases = {}
    if out is not None:
        specs.append(pl.BlockSpec(memory_space=pl.ANY))
        operands.append(out)
        aliases = {4: 0}
    specs += [pl.BlockSpec(memory_space=pl.ANY)] * len(waits)
    operands += waits
    return pl.pallas_call(
        equalize_kernel,
        grid=(rows // block,),
        out_shape=jax.ShapeDtypeStruct((groups, 2, rows, columns), jnp.float32),
        in_specs=specs,
        out_specs=pl.BlockSpec((1, 2, block, columns), lambda r: (group, 0, r, 0)),
        input_output_aliases=aliases,
        compiler_params=pltpu.CompilerParams(vmem_limit_bytes=VMEM),
        cost_estimate=COST,
        name="equalize",
    )(*operands)


def shift(value, d):
    count = lax.axis_size("station")
    return lax.ppermute(value, "station", [(s, (s + d) % count) for s in range(count)])


def passed_on(value):
    count = lax.axis_size("tm")
    return lax.ppermute(value, "tm", [(s, s + 1) for s in range(count - 1)])


def keep_table(flagged):
    fine = jnp.arange(SUBBAND_COUNT, dtype=jnp.int32)
    return jnp.all(flagged[:, :, None] != fine[None, None, :], axis=1).astype(jnp.float32)


def pipelined(volts, flagged):
    owners = lax.axis_size("station")
    me = lax.axis_index("station")
    half = lax.axis_index("tm")
    inputs = volts.shape[2]
    frames = volts.shape[3] // SUBBAND_COUNT
    frames_all = frames * lax.axis_size("tm")
    fine = SUBBAND_COUNT // owners
    groups = fine // GROUP
    blocks = frames // BLOCK

    keep_all = keep_table(flagged)
    keep_mine = lax.dynamic_index_in_dim(keep_all, lax.axis_index("band"), 0, keepdims=False)
    twice = jnp.concatenate([keep_mine, keep_mine])
    keep_ahead = lax.dynamic_slice_in_dim(twice, me * fine, SUBBAND_COUNT, 0)

    rows = twiddle_values().reshape(owners, groups, GROUP, 2, 2 * SUBBAND_COUNT)
    rows = rows.transpose(0, 1, 3, 2, 4)
    turns = [np.roll(rows, -z, 0).reshape(2 * SUBBAND_COUNT, -1) for z in range(owners)]
    table = jnp.asarray(np.stack(turns).astype(jnp.bfloat16))
    window = np.broadcast_to(window_values()[:, :, None], (TAPS, SUBBAND_COUNT, 128))
    window = jnp.asarray(np.ascontiguousarray(window))
    spot = jnp.reshape(me, (1,)).astype(jnp.int32)

    if groups != sum(RUNS):
        runs = (1,) * groups
    else:
        runs = RUNS
    parts, arrived, flat, out = [], [], [], None

    def send(n, waits):
        got = [parts[n][0]]
        for d in range(1, owners):
            gates = list(waits.get(d, ()))
            if len(flat) >= IN_FLIGHT and not (n == 1 and d == 2):
                gates.append(flat[len(flat) - IN_FLIGHT])
            value = after(parts[n][d], *gates) if gates else parts[n][d]
            with jax.named_scope(f"part{n}_shift{d}"):
                got.append(shift(value, d))
            flat.append(got[-1])
        arrived.append(got)

    power, halo, end = [], None, blocks
    for size in PARTS:
        end -= size
        spectra, part_power, tail = front(
            volts, None, end, size, (groups,), owners, keep_ahead, spot, window, table, halo is None
        )
        if tail is not None:
            halo = tail
        parts.append([x.reshape(groups, 2, GROUP * size * BLOCK, inputs) for x in spectra])
        power.append(part_power)
        if len(parts) == 1:
            send(0, {})
    with jax.named_scope("halo"):
        halo = passed_on(halo)
    spectra, part_power, _ = front(
        volts, halo, 0, end, runs, owners, keep_ahead, spot, window, table, False
    )
    power.append(part_power)
    for q, run in enumerate(runs):
        parts.append(
            [
                spectra[d * len(runs) + q].reshape(run, 2, GROUP * end * BLOCK, inputs)
                for d in range(owners)
            ]
        )

    local = jnp.sum(sum(power), axis=0)
    total = lax.psum(local, ("band", "tm"))
    scale = lax.rsqrt(total / (frames_all * jnp.sum(keep_all)) + 1e-06)
    scales = lax.all_gather(scale, "station", axis=0, tiled=True)
    kept = lax.dynamic_slice_in_dim(keep_mine, me * fine, fine, 0)
    counts = kept.reshape(groups, GROUP).sum(-1)
    denom = frames_all * jnp.maximum(counts, 1.0)
    per_half = scales.shape[0] // 2
    row_scales = lax.dynamic_slice_in_dim(scales, half * per_half, per_half, 0)

    column_scales = scales[None, :]
    row_scales = [(row_scales / denom[j])[None, :] for j in range(groups)]

    place = jnp.stack([me, 1 - half, half]).astype(jnp.int32)
    shared = len(PARTS)
    def to_other(j, theirs):
        with jax.named_scope(f"rows{j}"):
            return lax.ppermute(theirs, "tm", [(0, 1), (1, 0)])

    homes = [(q, at) for q, run in enumerate(runs) for at in range(run)]

    def multiply(j, place, dtypes, sums=(), earlier=(), begin=0, end=shared + 1):
        q, at = homes[j]
        pieces = arrived[:shared] + arrived[shared + q : shared + q + 1]
        picks = (j,) * shared + (at,)
        return correlate(place, pieces[begin:end], picks[begin:end], dtypes, sums, earlier)

    both = [jnp.bfloat16, jnp.float32]
    last_spectra = parts[shared][0]
    for n in range(1, shared):
        send(n, {d: [last_spectra, arrived[0][2]] for d in range(1, owners) if d != 2})
    send(shared, {min(2, owners - 1): [column_scales]})
    partial = multiply(groups - 1, place, [jnp.float32] * 2, end=shared)
    waiting = []

    def settle(out, earlier):
        for j, mine, theirs in waiting:
            out = equalize(row_scales[j], column_scales, mine, theirs, out, j, groups, earlier)
        waiting.clear()
        return out

    done = 0
    for q, run in enumerate(runs[:-1]):
        send(shared + q + 1, {owners - 1: partial} if q == 0 else {})
        results = [multiply(j, place, both) for j in range(done, done + run)]
        if waiting:
            out = settle(out, [x[0] for x in results])
        for j, (theirs, mine) in enumerate(results, done):
            if q + 2 < len(runs):
                theirs = after(theirs, *arrived[shared + q + 1][1:])
            waiting.append((j, mine, to_other(j, theirs)))
        done += run
    j = groups - 1
    theirs, mine = multiply(j, place, both, partial, [] if out is None else [out], begin=shared)
    out = settle(out, [theirs])
    waiting.append((j, mine, to_other(j, theirs)))
    out = settle(out, [])
    return out[None]


def twiddle_table():
    values = twiddle_values().transpose(2, 1, 0)
    return jnp.asarray(values).astype(jnp.bfloat16)


def pair_products(left, right):
    swapped = jnp.stack([left[..., 1, :], -left[..., 0, :]], 4)
    real = jnp.einsum("cgfird,cgfjrd->icgj", left, right, preferred_element_type=jnp.float32)
    imag = jnp.einsum("cgfird,cgfjrd->icgj", swapped, right, preferred_element_type=jnp.float32)
    return jnp.stack([real, imag], 3)


def plain(volts, flagged):
    coarse_dev = volts.shape[1]
    inputs_dev = volts.shape[2]
    spec_count = volts.shape[3] // SUBBAND_COUNT
    frames_all = spec_count * lax.axis_size("tm")
    frames = volts.reshape(2, coarse_dev, inputs_dev, spec_count, SUBBAND_COUNT)
    history = passed_on(frames[:, :, :, spec_count - (TAPS - 1) :, :])
    padded = jnp.concatenate([history, frames], 3)
    window = jnp.asarray(window_values())
    filtered = jnp.zeros((2, coarse_dev, inputs_dev, spec_count, SUBBAND_COUNT), jnp.float32)
    for tap in range(TAPS):
        filtered = filtered + window[tap] * padded[:, :, :, tap : tap + spec_count, :].astype(
            jnp.float32
        )
    filtered = filtered.astype(jnp.bfloat16)
    joined = jnp.concatenate([filtered[0], filtered[1]], -1)
    spectra = jnp.einsum(
        "nqvx,xdl->nlqdv", joined, twiddle_table(), preferred_element_type=jnp.float32
    ).astype(jnp.bfloat16)
    keep_all = keep_table(flagged)
    keep_mine = lax.dynamic_slice_in_dim(
        keep_all, lax.axis_index("band") * coarse_dev, coarse_dev, 0
    )
    values = spectra.astype(jnp.float32)
    local = jnp.sum(values * values * keep_mine[:, :, None, None, None], axis=(0, 1, 3, 4))
    total = lax.psum(local, ("band", "tm"))
    scale = lax.rsqrt(total / (frames_all * jnp.sum(keep_all)) + 1e-06)
    scales = lax.all_gather(scale, "station", axis=0, tiled=True)
    received = lax.all_to_all(spectra, "station", split_axis=1, concat_axis=2, tiled=True)
    fine_dev = received.shape[1]
    inputs_all = received.shape[2]
    kept = lax.dynamic_slice_in_dim(keep_mine, lax.axis_index("station") * fine_dev, fine_dev, 1)
    groups_dev = fine_dev // GROUP
    masked = received * kept[:, :, None, None, None].astype(jnp.bfloat16)
    blocks = masked.reshape(coarse_dev, groups_dev, GROUP, inputs_all, 2, spec_count)
    rows = inputs_all // lax.axis_size("tm")
    summed = lax.psum_scatter(pair_products(blocks, blocks), "tm", scatter_dimension=0, tiled=True)
    counts = kept.reshape(coarse_dev, groups_dev, GROUP).sum(-1)
    denom = frames_all * jnp.maximum(counts, 1.0)
    row_scales = lax.dynamic_slice_in_dim(scales, lax.axis_index("tm") * rows, rows, 0)
    pairs = row_scales[:, None] * scales[None, :]
    ordered = jnp.transpose(summed, (1, 2, 3, 0, 4))
    return ordered * pairs[None, None, None, :, :] / denom[:, :, None, None, None]


def shards(volts, flagged):
    owners = lax.axis_size("station")
    frames = volts.shape[3] // SUBBAND_COUNT
    fits = (
        volts.shape[1] == 1
        and volts.shape[2] % 128 == 0
        and owners % 2 == 0
        and (SUBBAND_COUNT // owners) % GROUP == 0
        and lax.axis_size("tm") == 2
        and frames % BLOCK == 0
        and SUBBAND_COUNT // owners // GROUP > 1
        and owners * volts.shape[2] // 2 % 128 == 0
        and frames // BLOCK > sum(PARTS)
    )
    return (pipelined if fits else plain)(volts, flagged)


def solution(mesh):
    placed = (P(None, "band", "station", "tm"), P())
    return jax.shard_map(
        shards,
        mesh=mesh,
        in_specs=placed,
        out_specs=P("band", "station", None, "tm", None),
        check_vma=False,
    )
```

```python
import functools
import math

import jax
import jax.numpy as jnp
import numpy as np
from jax import lax
from jax.experimental import pallas as pl
from jax.experimental.pallas import tpu as pltpu
from jax.sharding import PartitionSpec as P

SUBBAND_COUNT = 144
TAPS = 12
GROUP = 9
BLOCK = 16
PARTS = (1, 4)
RUNS = (1, 1, 1, 1)
SPREAD = BLOCK + 1
VMEM = 60 * 1024 * 1024
COST = pl.CostEstimate(flops=1024, bytes_accessed=1024, transcendentals=0)
IN_FLIGHT = 3


def window_values():
    total = TAPS * SUBBAND_COUNT
    place = np.arange(total, dtype=np.float64)
    shape = np.sinc((place - total / 2.0 + 0.5) / SUBBAND_COUNT)
    taper = 0.5 - 0.5 * np.cos(2.0 * math.pi * (place + 0.5) / total)
    return (shape * taper).reshape(TAPS, SUBBAND_COUNT).astype(np.float32)


def twiddle_values():
    f = np.arange(SUBBAND_COUNT, dtype=np.int64)[:, None]
    n = np.arange(SUBBAND_COUNT, dtype=np.int64)[None, :]
    angle = 2.0 * math.pi * (f * n % SUBBAND_COUNT) / SUBBAND_COUNT
    cosines, sines = np.cos(angle), np.sin(angle)
    real = np.concatenate([cosines, sines], 1)
    imag = np.concatenate([-sines, cosines], 1)
    return np.stack([real, imag], 1).astype(np.float32)


def front_kernel(
    runs, owners, turned, tail, me_ref, keep_ref, hist_ref, volts_ref, window_ref, table_ref, *rest
):
    splits = len(runs)
    outs, power_ref = rest[: owners * splits], rest[owners * splits]
    tail_ref = rest[owners * splits + 1] if tail else None
    homes = [(q, place) for q, run in enumerate(runs) for place in range(run)]
    ring, filt, spread = rest[-3:]
    step = pl.program_id(0)
    now = lax.rem(step, 2)
    before = 1 - now
    inputs = ring.shape[-1]
    tiles = inputs // 128
    span = BLOCK * SUBBAND_COUNT
    skipped = (BLOCK + 1 - TAPS) * SUBBAND_COUNT

    def turn(ref, slot, begin):
        def columns(c, _):
            at = pl.multiple_of(c * 128, 128)
            for part in range(2):
                ring[slot, part, pl.ds(at, 128), :] = ref[part, 0, :, pl.ds(at, 128)].T
            return 0

        lax.fori_loop(begin, span // 128, columns, 0, unroll=6 if begin == 0 else 5)

    @pl.when(step == 0)
    def _():
        if turned:
            for part in range(2):
                ring[1, part, pl.ds(skipped, span - skipped), :] = hist_ref[part]
        else:
            turn(hist_ref, 1, 3)
        power_ref[...] = jnp.zeros_like(power_ref)

    turn(volts_ref, now, 0)
    if tail:
        for part in range(2):
            tail_ref[part] = ring[now, part, pl.ds(skipped, span - skipped), :]

    def filter_rows(j, _):
        base = pl.multiple_of(j * 16, 16)
        for tile in range(tiles):
            lanes = pl.ds(tile * 128, 128)
            weights = [window_ref[k, pl.ds(base, 16), :] for k in range(TAPS)]
            for part in range(2):
                samples = []
                for t in range(1 - TAPS, BLOCK):
                    slot, frame = (now, t) if t >= 0 else (before, BLOCK + t)
                    at = pl.multiple_of(frame * SUBBAND_COUNT + base, 16)
                    samples.append(ring[slot, part, pl.ds(at, 16), lanes].astype(jnp.float32))
                for t in range(BLOCK):
                    total = weights[0] * samples[t]
                    for k in range(1, TAPS):
                        total = total + weights[k] * samples[t + k]
                    at = pl.multiple_of(part * SUBBAND_COUNT + base, 16)
                    filt[t, pl.ds(at, 16), lanes] = total.astype(jnp.bfloat16)
        return 0

    lax.fori_loop(0, SUBBAND_COUNT // 16, filter_rows, 0)

    def transform(t, _):
        result = jnp.dot(table_ref[0], filt[t], preferred_element_type=jnp.float32)
        for tile in range(tiles):
            spread[tile, pl.ds(t, 2 * SUBBAND_COUNT, stride=SPREAD), :] = result[
                :, tile * 128 : (tile + 1) * 128
            ]
        return 0

    lax.fori_loop(0, BLOCK, transform, 0, unroll=4)

    groups = SUBBAND_COUNT // owners // GROUP
    power = [jnp.zeros((BLOCK, 128), jnp.float32) for _ in range(tiles)]
    for d in range(owners):
        for j in range(groups):
            q, place = homes[j]
            out = outs[d * splits + q]

            def channel(f, power, d=d, j=j, out=out, place=place):
                keep = keep_ref[(d * groups + j) * GROUP + f]
                power = list(power)
                for part in range(2):
                    row = ((d * groups + j) * 2 + part) * GROUP + f
                    for tile in range(tiles):
                        value = spread[tile, pl.ds(row * SPREAD, BLOCK), :] * keep
                        value = value.astype(jnp.bfloat16)
                        out[place, part, f, :, tile * 128 : (tile + 1) * 128] = value
                        value = value.astype(jnp.float32)
                        power[tile] = power[tile] + value * value
                return tuple(power)

            power = lax.fori_loop(0, GROUP, channel, tuple(power), unroll=3)
    for tile in range(tiles):
        power_ref[:, tile * 128 : (tile + 1) * 128] += power[tile]


def front(volts, hist, first, steps, runs, owners, keep, me, window, table, tail):
    inputs = volts.shape[2]
    span = BLOCK * SUBBAND_COUNT
    frames = steps * BLOCK
    outs, out_specs = [], []
    for _ in range(owners):
        for run in runs:
            outs.append(jax.ShapeDtypeStruct((run, 2, GROUP, frames, inputs), jnp.bfloat16))
            out_specs.append(
                pl.BlockSpec((run, 2, GROUP, BLOCK, inputs), lambda s, me: (0, 0, 0, s, 0))
            )
    outs.append(jax.ShapeDtypeStruct((BLOCK, inputs), jnp.float32))
    out_specs.append(pl.BlockSpec((BLOCK, inputs), lambda s, me: (0, 0)))
    kept = (TAPS - 1) * SUBBAND_COUNT
    if tail:
        outs.append(jax.ShapeDtypeStruct((2, kept, inputs), jnp.bfloat16))
        out_specs.append(pl.BlockSpec((2, kept, inputs), lambda s, me: (0, 0, 0)))
    if hist is None:
        hist, hist_spec = volts, pl.BlockSpec((2, 1, inputs, span), lambda s, me: (0, 0, 0, first - 1))
        turned = False
    else:
        hist_spec, turned = pl.BlockSpec((2, kept, inputs), lambda s, me: (0, 0, 0)), True
    result = pl.pallas_call(
        functools.partial(front_kernel, runs, owners, turned, tail),
        grid_spec=pltpu.PrefetchScalarGridSpec(
            num_scalar_prefetch=1,
            grid=(steps,),
            in_specs=[
                pl.BlockSpec(memory_space=pltpu.SMEM),
                hist_spec,
                pl.BlockSpec((2, 1, inputs, span), lambda s, me: (0, 0, 0, first + s)),
                pl.BlockSpec(window.shape, lambda s, me: (0, 0, 0)),
                pl.BlockSpec((1, *table.shape[1:]), lambda s, me: (me[0], 0, 0)),
            ],
            out_specs=out_specs,
            scratch_shapes=[
                pltpu.VMEM((2, 2, span, inputs), jnp.bfloat16),
                pltpu.VMEM((BLOCK, 2 * SUBBAND_COUNT, inputs), jnp.bfloat16),
                pltpu.VMEM((inputs // 128, 2 * SUBBAND_COUNT * SPREAD, 128), jnp.float32),
            ],
        ),
        out_shape=outs,
        compiler_params=pltpu.CompilerParams(vmem_limit_bytes=VMEM),
        cost_estimate=COST,
        name="front",
    )(me, keep, hist, volts, window, table)
    count = owners * len(runs)
    return result[:count], result[count], result[count + 1] if tail else None


def after_kernel(*refs):
    pass


def after(value, *others):
    anywhere = pl.BlockSpec(memory_space=pl.ANY)
    return pl.pallas_call(
        after_kernel,
        out_shape=jax.ShapeDtypeStruct(value.shape, value.dtype),
        in_specs=[anywhere] * (1 + len(others)),
        out_specs=anywhere,
        input_output_aliases={0: 0},
        cost_estimate=COST,
        name="after",
    )(value, *others)


def with_scales_kernel(value_ref, scale_ref, out_ref, rows, sems):
    size = value_ref.shape[2]
    left = scale_ref[...]
    pieces = []
    for _ in range(3):
        piece = left.astype(jnp.bfloat16).astype(jnp.float32)
        pieces.append(jnp.broadcast_to(piece, rows.shape))
        left = left - piece
    place = lax.broadcasted_iota(jnp.int32, rows.shape, 0)
    chosen = jnp.where(place == 0, pieces[0], jnp.where(place == 1, pieces[1], pieces[2]))
    rows[...] = chosen.astype(jnp.bfloat16)
    copies = [
        pltpu.make_async_copy(value_ref.at[0, 0], out_ref.at[pl.ds(0, size)], sems.at[0]),
        pltpu.make_async_copy(value_ref.at[0, 1], out_ref.at[pl.ds(size, size)], sems.at[1]),
        pltpu.make_async_copy(rows, out_ref.at[pl.ds(2 * size, 16)], sems.at[2]),
    ]
    for copy in copies:
        copy.start()
    for copy in copies:
        copy.wait()


def with_scales(value, scale):
    size, inputs = value.shape[2:]
    anywhere = pl.BlockSpec(memory_space=pl.ANY)
    return pl.pallas_call(
        with_scales_kernel,
        out_shape=jax.ShapeDtypeStruct((2 * size + 16, inputs), value.dtype),
        in_specs=[anywhere, pl.BlockSpec(memory_space=pltpu.VMEM)],
        out_specs=anywhere,
        scratch_shapes=[pltpu.VMEM((16, inputs), value.dtype), pltpu.SemaphoreType.DMA((3,))],
        cost_estimate=COST,
        name="with_scales",
    )(value, scale)


def correlate_kernel(owners, picks, outs, sums, place_ref, *rest):
    count = len(picks)
    sum_refs, rest = rest[:sums], rest[sums:]
    pieces = [rest[n * owners : (n + 1) * owners] for n in range(count)]
    out_refs, (held, turned, sems) = rest[-3 - outs : -3], rest[-3:]
    me = place_ref[0]
    column = pl.program_id(0)
    per_half = owners // 2
    inputs, depth = turned.shape[3], held.shape[2]

    @pl.when(column == 0)
    def _():
        copies = []
        for d in range(owners):
            source = lax.rem(me - d + owners, owners)
            at = 0
            for n in range(count):
                size = pieces[n][d].shape[2]
                copies.append(
                    pltpu.make_async_copy(
                        pieces[n][d].at[picks[n]], held.at[source, :, pl.ds(at, size)], sems.at[n, d]
                    )
                )
                at += size
        for copy in copies:
            copy.start()
        for copy in copies:
            copy.wait()
        for h in range(outs):
            for r in range(per_half):
                source = place_ref[1 + h] * per_half + r
                real, imag = held[source, 0].T, held[source, 1].T
                turned[h, 0, r, :, pl.ds(0, depth)] = real
                turned[h, 0, r, :, pl.ds(depth, depth)] = imag
                turned[h, 1, r, :, pl.ds(0, depth)] = imag
                turned[h, 1, r, :, pl.ds(depth, depth)] = -real

    right = held[column].reshape(2 * depth, inputs)
    for h in range(outs):
        left = turned[h].reshape(2 * per_half * inputs, 2 * depth)
        both = jnp.dot(left, right, preferred_element_type=jnp.float32)
        both = both.reshape(2, per_half * inputs, inputs)
        if sums:
            both = both + sum_refs[h][...]
        out_refs[h][...] = both.astype(out_refs[h].dtype)


def correlate(place, pieces, picks, dtypes, sums, earlier):
    owners = len(pieces[0])
    inputs = pieces[0][0].shape[-1]
    depth = sum(piece[0].shape[2] for piece in pieces)
    rows = owners // 2 * inputs
    operands = [value for piece in pieces for value in piece] + list(earlier)
    columns = pl.BlockSpec((2, rows, inputs), lambda b: (0, 0, b))
    anywhere = pl.BlockSpec(memory_space=pl.ANY)
    outs = len(dtypes)
    return pl.pallas_call(
        functools.partial(correlate_kernel, owners, picks, outs, len(sums)),
        grid=(owners,),
        out_shape=[jax.ShapeDtypeStruct((2, rows, owners * inputs), dtype) for dtype in dtypes],
        in_specs=[pl.BlockSpec(memory_space=pltpu.SMEM)]
        + [columns] * len(sums)
        + [anywhere] * len(operands),
        out_specs=[columns] * outs,
        scratch_shapes=[
            pltpu.VMEM((owners, 2, depth, inputs), jnp.bfloat16),
            pltpu.VMEM((outs, 2, owners // 2, inputs, 2 * depth), jnp.bfloat16),
            pltpu.SemaphoreType.DMA((len(pieces), owners)),
        ],
        compiler_params=pltpu.CompilerParams(vmem_limit_bytes=VMEM),
        cost_estimate=COST,
        name="correlate",
    )(place, *sums, *operands)


def equalize_kernel(rows_ref, columns_ref, mine_ref, theirs_ref, *rest):
    out_ref = rest[-1]
    rows = rows_ref.shape[1]
    by_row = jnp.broadcast_to(rows_ref[...], (rows, rows)).T
    for at in range(0, columns_ref.shape[1], rows):
        columns = slice(at, at + rows)
        scale = by_row * columns_ref[:, columns]
        for part in range(2):
            total = mine_ref[part, :, columns] + theirs_ref[part, :, columns].astype(jnp.float32)
            out_ref[0, part, :, columns] = total * scale


def equalize(row_scales, column_scales, mine, theirs, out, group, groups, waits):
    rows, columns = mine.shape[1:]
    block = 128
    specs = [
        pl.BlockSpec((1, block), lambda r: (0, r)),
        pl.BlockSpec((1, columns), lambda r: (0, 0)),
        pl.BlockSpec((2, block, columns), lambda r: (0, r, 0)),
        pl.BlockSpec((2, block, columns), lambda r: (0, r, 0)),
    ]
    operands = [row_scales, column_scales, mine, theirs]
    aliases = {}
    if out is not None:
        specs.append(pl.BlockSpec(memory_space=pl.ANY))
        operands.append(out)
        aliases = {4: 0}
    specs += [pl.BlockSpec(memory_space=pl.ANY)] * len(waits)
    operands += waits
    return pl.pallas_call(
        equalize_kernel,
        grid=(rows // block,),
        out_shape=jax.ShapeDtypeStruct((groups, 2, rows, columns), jnp.float32),
        in_specs=specs,
        out_specs=pl.BlockSpec((1, 2, block, columns), lambda r: (group, 0, r, 0)),
        input_output_aliases=aliases,
        compiler_params=pltpu.CompilerParams(vmem_limit_bytes=VMEM),
        cost_estimate=COST,
        name="equalize",
    )(*operands)


def shift(value, d):
    count = lax.axis_size("station")
    return lax.ppermute(value, "station", [(s, (s + d) % count) for s in range(count)])


def passed_on(value):
    count = lax.axis_size("tm")
    return lax.ppermute(value, "tm", [(s, s + 1) for s in range(count - 1)])


def keep_table(flagged):
    fine = jnp.arange(SUBBAND_COUNT, dtype=jnp.int32)
    return jnp.all(flagged[:, :, None] != fine[None, None, :], axis=1).astype(jnp.float32)


def pipelined(volts, flagged):
    owners = lax.axis_size("station")
    me = lax.axis_index("station")
    half = lax.axis_index("tm")
    inputs = volts.shape[2]
    frames = volts.shape[3] // SUBBAND_COUNT
    frames_all = frames * lax.axis_size("tm")
    fine = SUBBAND_COUNT // owners
    groups = fine // GROUP
    blocks = frames // BLOCK

    keep_all = keep_table(flagged)
    keep_mine = lax.dynamic_index_in_dim(keep_all, lax.axis_index("band"), 0, keepdims=False)
    twice = jnp.concatenate([keep_mine, keep_mine])
    keep_ahead = lax.dynamic_slice_in_dim(twice, me * fine, SUBBAND_COUNT, 0)

    rows = twiddle_values().reshape(owners, groups, GROUP, 2, 2 * SUBBAND_COUNT)
    rows = rows.transpose(0, 1, 3, 2, 4)
    turns = [np.roll(rows, -z, 0).reshape(2 * SUBBAND_COUNT, -1) for z in range(owners)]
    table = jnp.asarray(np.stack(turns).astype(jnp.bfloat16))
    window = np.broadcast_to(window_values()[:, :, None], (TAPS, SUBBAND_COUNT, 128))
    window = jnp.asarray(np.ascontiguousarray(window))
    spot = jnp.reshape(me, (1,)).astype(jnp.int32)

    if groups != sum(RUNS) or RUNS[0] != 1:
        runs = (1,) * groups
    else:
        runs = RUNS
    parts, arrived, flat, out = [], [], [], None

    def send(n, waits, scale=None):
        got = [parts[n][0]]
        for d in range(1, owners):
            gates = list(waits.get(d, ()))
            if len(flat) >= IN_FLIGHT and not (n == 1 and d == 2):
                gates.append(flat[len(flat) - IN_FLIGHT])
            value = parts[n][d] if scale is None else with_scales(parts[n][d], scale)
            value = after(value, *gates) if gates else value
            with jax.named_scope(f"part{n}_shift{d}"):
                got.append(shift(value, d))
            flat.append(got[-1])
        arrived.append(got)

    power, halo, end = [], None, blocks
    for size in PARTS:
        end -= size
        spectra, part_power, tail = front(
            volts, None, end, size, (groups,), owners, keep_ahead, spot, window, table, halo is None
        )
        if tail is not None:
            halo = tail
        parts.append([x.reshape(groups, 2, GROUP * size * BLOCK, inputs) for x in spectra])
        power.append(part_power)
        if len(parts) == 1:
            send(0, {})
    with jax.named_scope("halo"):
        halo = passed_on(halo)
    spectra, part_power, _ = front(
        volts, halo, 0, end, runs, owners, keep_ahead, spot, window, table, False
    )
    power.append(part_power)
    for q, run in enumerate(runs):
        parts.append(
            [
                spectra[d * len(runs) + q].reshape(run, 2, GROUP * end * BLOCK, inputs)
                for d in range(owners)
            ]
        )

    local = jnp.sum(sum(power), axis=0)
    total = lax.psum(local, ("band", "tm"))
    scale = lax.rsqrt(total / (frames_all * jnp.sum(keep_all)) + 1e-06)
    kept = lax.dynamic_slice_in_dim(keep_mine, me * fine, fine, 0)
    counts = kept.reshape(groups, GROUP).sum(-1)
    denom = frames_all * jnp.maximum(counts, 1.0)
    place = jnp.stack([me, 1 - half, half]).astype(jnp.int32)
    shared = len(PARTS)
    def to_other(j, theirs):
        with jax.named_scope(f"rows{j}"):
            return lax.ppermute(theirs, "tm", [(0, 1), (1, 0)])

    homes = [(q, at) for q, run in enumerate(runs) for at in range(run)]

    def multiply(j, place, dtypes, sums=(), earlier=(), begin=0, end=shared + 1):
        q, at = homes[j]
        pieces = arrived[:shared] + arrived[shared + q : shared + q + 1]
        picks = (j,) * shared + (at,)
        return correlate(place, pieces[begin:end], picks[begin:end], dtypes, sums, earlier)

    both = [jnp.bfloat16, jnp.float32]
    last_spectra = parts[shared][0]
    for n in range(1, shared):
        send(n, {d: [last_spectra, arrived[0][2]] for d in range(1, owners) if d != 2})
    send(shared, {}, scale[None, :])
    got = arrived[shared]
    size = 2 * got[0].shape[2]
    by_shift = [scale]
    for d in range(1, owners):
        by_shift.append(got[d][size : size + 3].astype(jnp.float32).sum(0))
        got[d] = got[d][:size].reshape(got[0].shape)
    source = (me - jnp.arange(owners)) % owners
    chosen = (jnp.arange(owners)[:, None] == source[None, :]).astype(jnp.float32)
    scales = jnp.sum(chosen[:, :, None] * jnp.stack(by_shift)[None], axis=1).reshape(-1)
    per_half = scales.shape[0] // 2
    row_scales = lax.dynamic_slice_in_dim(scales, half * per_half, per_half, 0)

    column_scales = scales[None, :]
    row_scales = [(row_scales / denom[j])[None, :] for j in range(groups)]

    partial = multiply(groups - 1, place, [jnp.float32] * 2, end=shared)
    waiting = []

    def settle(out, earlier):
        for j, mine, theirs in waiting:
            out = equalize(row_scales[j], column_scales, mine, theirs, out, j, groups, earlier)
        waiting.clear()
        return out

    done = 0
    for q, run in enumerate(runs[:-1]):
        send(shared + q + 1, {owners - 1: partial} if q == 0 else {})
        results = [multiply(j, place, both) for j in range(done, done + run)]
        if waiting:
            out = settle(out, [x[0] for x in results])
        for j, (theirs, mine) in enumerate(results, done):
            if q + 2 < len(runs):
                theirs = after(theirs, *arrived[shared + q + 1][1:])
            waiting.append((j, mine, to_other(j, theirs)))
        done += run
    j = groups - 1
    theirs, mine = multiply(j, place, both, partial, [] if out is None else [out], begin=shared)
    out = settle(out, [theirs])
    waiting.append((j, mine, to_other(j, theirs)))
    out = settle(out, [])
    return out[None]


def twiddle_table():
    values = twiddle_values().transpose(2, 1, 0)
    return jnp.asarray(values).astype(jnp.bfloat16)


def pair_products(left, right):
    swapped = jnp.stack([left[..., 1, :], -left[..., 0, :]], 4)
    real = jnp.einsum("cgfird,cgfjrd->icgj", left, right, preferred_element_type=jnp.float32)
    imag = jnp.einsum("cgfird,cgfjrd->icgj", swapped, right, preferred_element_type=jnp.float32)
    return jnp.stack([real, imag], 3)


def plain(volts, flagged):
    coarse_dev = volts.shape[1]
    inputs_dev = volts.shape[2]
    spec_count = volts.shape[3] // SUBBAND_COUNT
    frames_all = spec_count * lax.axis_size("tm")
    frames = volts.reshape(2, coarse_dev, inputs_dev, spec_count, SUBBAND_COUNT)
    history = passed_on(frames[:, :, :, spec_count - (TAPS - 1) :, :])
    padded = jnp.concatenate([history, frames], 3)
    window = jnp.asarray(window_values())
    filtered = jnp.zeros((2, coarse_dev, inputs_dev, spec_count, SUBBAND_COUNT), jnp.float32)
    for tap in range(TAPS):
        filtered = filtered + window[tap] * padded[:, :, :, tap : tap + spec_count, :].astype(
            jnp.float32
        )
    filtered = filtered.astype(jnp.bfloat16)
    joined = jnp.concatenate([filtered[0], filtered[1]], -1)
    spectra = jnp.einsum(
        "nqvx,xdl->nlqdv", joined, twiddle_table(), preferred_element_type=jnp.float32
    ).astype(jnp.bfloat16)
    keep_all = keep_table(flagged)
    keep_mine = lax.dynamic_slice_in_dim(
        keep_all, lax.axis_index("band") * coarse_dev, coarse_dev, 0
    )
    values = spectra.astype(jnp.float32)
    local = jnp.sum(values * values * keep_mine[:, :, None, None, None], axis=(0, 1, 3, 4))
    total = lax.psum(local, ("band", "tm"))
    scale = lax.rsqrt(total / (frames_all * jnp.sum(keep_all)) + 1e-06)
    scales = lax.all_gather(scale, "station", axis=0, tiled=True)
    received = lax.all_to_all(spectra, "station", split_axis=1, concat_axis=2, tiled=True)
    fine_dev = received.shape[1]
    inputs_all = received.shape[2]
    kept = lax.dynamic_slice_in_dim(keep_mine, lax.axis_index("station") * fine_dev, fine_dev, 1)
    groups_dev = fine_dev // GROUP
    masked = received * kept[:, :, None, None, None].astype(jnp.bfloat16)
    blocks = masked.reshape(coarse_dev, groups_dev, GROUP, inputs_all, 2, spec_count)
    rows = inputs_all // lax.axis_size("tm")
    summed = lax.psum_scatter(pair_products(blocks, blocks), "tm", scatter_dimension=0, tiled=True)
    counts = kept.reshape(coarse_dev, groups_dev, GROUP).sum(-1)
    denom = frames_all * jnp.maximum(counts, 1.0)
    row_scales = lax.dynamic_slice_in_dim(scales, lax.axis_index("tm") * rows, rows, 0)
    pairs = row_scales[:, None] * scales[None, :]
    ordered = jnp.transpose(summed, (1, 2, 3, 0, 4))
    return ordered * pairs[None, None, None, :, :] / denom[:, :, None, None, None]


def shards(volts, flagged):
    owners = lax.axis_size("station")
    frames = volts.shape[3] // SUBBAND_COUNT
    fits = (
        volts.shape[1] == 1
        and volts.shape[2] % 128 == 0
        and owners % 2 == 0
        and (SUBBAND_COUNT // owners) % GROUP == 0
        and lax.axis_size("tm") == 2
        and frames % BLOCK == 0
        and SUBBAND_COUNT // owners // GROUP > 1
        and owners * volts.shape[2] // 2 % 128 == 0
        and frames // BLOCK > sum(PARTS)
    )
    return (pipelined if fits else plain)(volts, flagged)


def solution(mesh):
    placed = (P(None, "band", "station", "tm"), P())
    return jax.shard_map(
        shards,
        mesh=mesh,
        in_specs=placed,
        out_specs=P("band", "station", None, "tm", None),
        check_vma=False,
    )
```

```python
import functools
import math

import jax
import jax.numpy as jnp
import numpy as np
from jax import lax
from jax.experimental import pallas as pl
from jax.experimental.pallas import tpu as pltpu
from jax.sharding import PartitionSpec as P

SUBBAND_COUNT = 144
TAPS = 12
GROUP = 9
BLOCK = 16
PARTS = (1, 4)
RUNS = (1, 1, 1, 1)
SPREAD = BLOCK + 1
VMEM = 60 * 1024 * 1024
COST = pl.CostEstimate(flops=1024, bytes_accessed=1024, transcendentals=0)
IN_FLIGHT = 3


def window_values():
    total = TAPS * SUBBAND_COUNT
    place = np.arange(total, dtype=np.float64)
    shape = np.sinc((place - total / 2.0 + 0.5) / SUBBAND_COUNT)
    taper = 0.5 - 0.5 * np.cos(2.0 * math.pi * (place + 0.5) / total)
    return (shape * taper).reshape(TAPS, SUBBAND_COUNT).astype(np.float32)


def twiddle_values():
    f = np.arange(SUBBAND_COUNT, dtype=np.int64)[:, None]
    n = np.arange(SUBBAND_COUNT, dtype=np.int64)[None, :]
    angle = 2.0 * math.pi * (f * n % SUBBAND_COUNT) / SUBBAND_COUNT
    cosines, sines = np.cos(angle), np.sin(angle)
    real = np.concatenate([cosines, sines], 1)
    imag = np.concatenate([-sines, cosines], 1)
    return np.stack([real, imag], 1).astype(np.float32)


def front_kernel(
    runs, owners, turned, tail, me_ref, keep_ref, hist_ref, volts_ref, window_ref, table_ref, *rest
):
    splits = len(runs)
    outs, power_ref = rest[: owners * splits], rest[owners * splits]
    tail_ref = rest[owners * splits + 1] if tail else None
    homes = [(q, place) for q, run in enumerate(runs) for place in range(run)]
    ring, filt, spread = rest[-3:]
    step = pl.program_id(0)
    now = lax.rem(step, 2)
    before = 1 - now
    inputs = ring.shape[-1]
    tiles = inputs // 128
    span = BLOCK * SUBBAND_COUNT
    skipped = (BLOCK + 1 - TAPS) * SUBBAND_COUNT

    def turn(ref, slot, begin):
        def columns(c, _):
            at = pl.multiple_of(c * 128, 128)
            for part in range(2):
                ring[slot, part, pl.ds(at, 128), :] = ref[part, 0, :, pl.ds(at, 128)].T
            return 0

        lax.fori_loop(begin, span // 128, columns, 0, unroll=6 if begin == 0 else 5)

    @pl.when(step == 0)
    def _():
        if turned:
            for part in range(2):
                ring[1, part, pl.ds(skipped, span - skipped), :] = hist_ref[part]
        else:
            turn(hist_ref, 1, 3)
        power_ref[...] = jnp.zeros_like(power_ref)

    turn(volts_ref, now, 0)
    if tail:
        for part in range(2):
            tail_ref[part] = ring[now, part, pl.ds(skipped, span - skipped), :]

    def filter_rows(j, _):
        base = pl.multiple_of(j * 16, 16)
        for tile in range(tiles):
            lanes = pl.ds(tile * 128, 128)
            weights = [window_ref[k, pl.ds(base, 16), :] for k in range(TAPS)]
            for part in range(2):
                samples = []
                for t in range(1 - TAPS, BLOCK):
                    slot, frame = (now, t) if t >= 0 else (before, BLOCK + t)
                    at = pl.multiple_of(frame * SUBBAND_COUNT + base, 16)
                    samples.append(ring[slot, part, pl.ds(at, 16), lanes].astype(jnp.float32))
                for t in range(BLOCK):
                    total = weights[0] * samples[t]
                    for k in range(1, TAPS):
                        total = total + weights[k] * samples[t + k]
                    at = pl.multiple_of(part * SUBBAND_COUNT + base, 16)
                    filt[t, pl.ds(at, 16), lanes] = total.astype(jnp.bfloat16)
        return 0

    lax.fori_loop(0, SUBBAND_COUNT // 16, filter_rows, 0)

    def transform(t, _):
        result = jnp.dot(table_ref[0], filt[t], preferred_element_type=jnp.float32)
        for tile in range(tiles):
            spread[tile, pl.ds(t, 2 * SUBBAND_COUNT, stride=SPREAD), :] = result[
                :, tile * 128 : (tile + 1) * 128
            ]
        return 0

    lax.fori_loop(0, BLOCK, transform, 0, unroll=4)

    groups = SUBBAND_COUNT // owners // GROUP
    power = [jnp.zeros((BLOCK, 128), jnp.float32) for _ in range(tiles)]
    for d in range(owners):
        for j in range(groups):
            q, place = homes[j]
            out = outs[d * splits + q]

            def channel(f, power, d=d, j=j, out=out, place=place):
                keep = keep_ref[(d * groups + j) * GROUP + f]
                power = list(power)
                for part in range(2):
                    row = ((d * groups + j) * 2 + part) * GROUP + f
                    for tile in range(tiles):
                        value = spread[tile, pl.ds(row * SPREAD, BLOCK), :] * keep
                        value = value.astype(jnp.bfloat16)
                        out[place, part, f, :, tile * 128 : (tile + 1) * 128] = value
                        value = value.astype(jnp.float32)
                        power[tile] = power[tile] + value * value
                return tuple(power)

            power = lax.fori_loop(0, GROUP, channel, tuple(power), unroll=3)
    for tile in range(tiles):
        power_ref[:, tile * 128 : (tile + 1) * 128] += power[tile]


def front(volts, hist, first, steps, runs, owners, keep, me, window, table, tail):
    inputs = volts.shape[2]
    span = BLOCK * SUBBAND_COUNT
    frames = steps * BLOCK
    outs, out_specs = [], []
    for _ in range(owners):
        for run in runs:
            outs.append(jax.ShapeDtypeStruct((run, 2, GROUP, frames, inputs), jnp.bfloat16))
            out_specs.append(
                pl.BlockSpec((run, 2, GROUP, BLOCK, inputs), lambda s, me: (0, 0, 0, s, 0))
            )
    outs.append(jax.ShapeDtypeStruct((BLOCK, inputs), jnp.float32))
    out_specs.append(pl.BlockSpec((BLOCK, inputs), lambda s, me: (0, 0)))
    kept = (TAPS - 1) * SUBBAND_COUNT
    if tail:
        outs.append(jax.ShapeDtypeStruct((2, kept, inputs), jnp.bfloat16))
        out_specs.append(pl.BlockSpec((2, kept, inputs), lambda s, me: (0, 0, 0)))
    if hist is None:
        hist, hist_spec = volts, pl.BlockSpec((2, 1, inputs, span), lambda s, me: (0, 0, 0, first - 1))
        turned = False
    else:
        hist_spec, turned = pl.BlockSpec((2, kept, inputs), lambda s, me: (0, 0, 0)), True
    result = pl.pallas_call(
        functools.partial(front_kernel, runs, owners, turned, tail),
        grid_spec=pltpu.PrefetchScalarGridSpec(
            num_scalar_prefetch=1,
            grid=(steps,),
            in_specs=[
                pl.BlockSpec(memory_space=pltpu.SMEM),
                hist_spec,
                pl.BlockSpec((2, 1, inputs, span), lambda s, me: (0, 0, 0, first + s)),
                pl.BlockSpec(window.shape, lambda s, me: (0, 0, 0)),
                pl.BlockSpec((1, *table.shape[1:]), lambda s, me: (me[0], 0, 0)),
            ],
            out_specs=out_specs,
            scratch_shapes=[
                pltpu.VMEM((2, 2, span, inputs), jnp.bfloat16),
                pltpu.VMEM((BLOCK, 2 * SUBBAND_COUNT, inputs), jnp.bfloat16),
                pltpu.VMEM((inputs // 128, 2 * SUBBAND_COUNT * SPREAD, 128), jnp.float32),
            ],
        ),
        out_shape=outs,
        compiler_params=pltpu.CompilerParams(vmem_limit_bytes=VMEM),
        cost_estimate=COST,
        name="front",
    )(me, keep, hist, volts, window, table)
    count = owners * len(runs)
    return result[:count], result[count], result[count + 1] if tail else None


def after_kernel(*refs):
    pass


def after(value, *others):
    anywhere = pl.BlockSpec(memory_space=pl.ANY)
    return pl.pallas_call(
        after_kernel,
        out_shape=jax.ShapeDtypeStruct(value.shape, value.dtype),
        in_specs=[anywhere] * (1 + len(others)),
        out_specs=anywhere,
        input_output_aliases={0: 0},
        cost_estimate=COST,
        name="after",
    )(value, *others)


def with_scales_kernel(value_ref, scale_ref, out_ref):
    size = value_ref.shape[2]
    left = scale_ref[...]
    pieces = []
    for _ in range(3):
        piece = left.astype(jnp.bfloat16).astype(jnp.float32)
        pieces.append(jnp.broadcast_to(piece, (16, piece.shape[1])))
        left = left - piece
    place = lax.broadcasted_iota(jnp.int32, pieces[0].shape, 0)
    chosen = jnp.where(place == 0, pieces[0], jnp.where(place == 1, pieces[1], pieces[2]))
    out_ref[pl.ds(0, size), :] = value_ref[0, 0]
    out_ref[pl.ds(size, size), :] = value_ref[0, 1]
    out_ref[pl.ds(2 * size, 16), :] = chosen.astype(jnp.bfloat16)


def with_scales(value, scale):
    size, inputs = value.shape[2:]
    whole = pl.BlockSpec(memory_space=pltpu.VMEM)
    return pl.pallas_call(
        with_scales_kernel,
        out_shape=jax.ShapeDtypeStruct((2 * size + 16, inputs), value.dtype),
        in_specs=[whole, whole],
        out_specs=whole,
        compiler_params=pltpu.CompilerParams(vmem_limit_bytes=VMEM),
        cost_estimate=COST,
        name="with_scales",
    )(value, scale)


def correlate_kernel(owners, picks, outs, sums, place_ref, *rest):
    count = len(picks)
    sum_refs, rest = rest[:sums], rest[sums:]
    pieces = [rest[n * owners : (n + 1) * owners] for n in range(count)]
    out_refs, (held, turned, sems) = rest[-3 - outs : -3], rest[-3:]
    me = place_ref[0]
    column = pl.program_id(0)
    per_half = owners // 2
    inputs, depth = turned.shape[3], held.shape[2]

    @pl.when(column == 0)
    def _():
        copies = []
        for d in range(owners):
            source = lax.rem(me - d + owners, owners)
            at = 0
            for n in range(count):
                size = pieces[n][d].shape[2]
                copies.append(
                    pltpu.make_async_copy(
                        pieces[n][d].at[picks[n]], held.at[source, :, pl.ds(at, size)], sems.at[n, d]
                    )
                )
                at += size
        for copy in copies:
            copy.start()
        for copy in copies:
            copy.wait()
        for h in range(outs):
            for r in range(per_half):
                source = place_ref[1 + h] * per_half + r
                real, imag = held[source, 0].T, held[source, 1].T
                turned[h, 0, r, :, pl.ds(0, depth)] = real
                turned[h, 0, r, :, pl.ds(depth, depth)] = imag
                turned[h, 1, r, :, pl.ds(0, depth)] = imag
                turned[h, 1, r, :, pl.ds(depth, depth)] = -real

    right = held[column].reshape(2 * depth, inputs)
    for h in range(outs):
        left = turned[h].reshape(2 * per_half * inputs, 2 * depth)
        both = jnp.dot(left, right, preferred_element_type=jnp.float32)
        both = both.reshape(2, per_half * inputs, inputs)
        if sums:
            both = both + sum_refs[h][...]
        out_refs[h][...] = both.astype(out_refs[h].dtype)


def correlate(place, pieces, picks, dtypes, sums, earlier):
    owners = len(pieces[0])
    inputs = pieces[0][0].shape[-1]
    depth = sum(piece[0].shape[2] for piece in pieces)
    rows = owners // 2 * inputs
    operands = [value for piece in pieces for value in piece] + list(earlier)
    columns = pl.BlockSpec((2, rows, inputs), lambda b: (0, 0, b))
    anywhere = pl.BlockSpec(memory_space=pl.ANY)
    outs = len(dtypes)
    return pl.pallas_call(
        functools.partial(correlate_kernel, owners, picks, outs, len(sums)),
        grid=(owners,),
        out_shape=[jax.ShapeDtypeStruct((2, rows, owners * inputs), dtype) for dtype in dtypes],
        in_specs=[pl.BlockSpec(memory_space=pltpu.SMEM)]
        + [columns] * len(sums)
        + [anywhere] * len(operands),
        out_specs=[columns] * outs,
        scratch_shapes=[
            pltpu.VMEM((owners, 2, depth, inputs), jnp.bfloat16),
            pltpu.VMEM((outs, 2, owners // 2, inputs, 2 * depth), jnp.bfloat16),
            pltpu.SemaphoreType.DMA((len(pieces), owners)),
        ],
        compiler_params=pltpu.CompilerParams(vmem_limit_bytes=VMEM),
        cost_estimate=COST,
        name="correlate",
    )(place, *sums, *operands)


def equalize_kernel(rows_ref, columns_ref, mine_ref, theirs_ref, *rest):
    out_ref = rest[-1]
    rows = rows_ref.shape[1]
    by_row = jnp.broadcast_to(rows_ref[...], (rows, rows)).T
    for at in range(0, columns_ref.shape[1], rows):
        columns = slice(at, at + rows)
        scale = by_row * columns_ref[:, columns]
        for part in range(2):
            total = mine_ref[part, :, columns] + theirs_ref[part, :, columns].astype(jnp.float32)
            out_ref[0, part, :, columns] = total * scale


def equalize(row_scales, column_scales, mine, theirs, out, group, groups, waits):
    rows, columns = mine.shape[1:]
    block = 128
    specs = [
        pl.BlockSpec((1, block), lambda r: (0, r)),
        pl.BlockSpec((1, columns), lambda r: (0, 0)),
        pl.BlockSpec((2, block, columns), lambda r: (0, r, 0)),
        pl.BlockSpec((2, block, columns), lambda r: (0, r, 0)),
    ]
    operands = [row_scales, column_scales, mine, theirs]
    aliases = {}
    if out is not None:
        specs.append(pl.BlockSpec(memory_space=pl.ANY))
        operands.append(out)
        aliases = {4: 0}
    specs += [pl.BlockSpec(memory_space=pl.ANY)] * len(waits)
    operands += waits
    return pl.pallas_call(
        equalize_kernel,
        grid=(rows // block,),
        out_shape=jax.ShapeDtypeStruct((groups, 2, rows, columns), jnp.float32),
        in_specs=specs,
        out_specs=pl.BlockSpec((1, 2, block, columns), lambda r: (group, 0, r, 0)),
        input_output_aliases=aliases,
        compiler_params=pltpu.CompilerParams(vmem_limit_bytes=VMEM),
        cost_estimate=COST,
        name="equalize",
    )(*operands)


def shift(value, d):
    count = lax.axis_size("station")
    return lax.ppermute(value, "station", [(s, (s + d) % count) for s in range(count)])


def passed_on(value):
    count = lax.axis_size("tm")
    return lax.ppermute(value, "tm", [(s, s + 1) for s in range(count - 1)])


def keep_table(flagged):
    fine = jnp.arange(SUBBAND_COUNT, dtype=jnp.int32)
    return jnp.all(flagged[:, :, None] != fine[None, None, :], axis=1).astype(jnp.float32)


def pipelined(volts, flagged):
    owners = lax.axis_size("station")
    me = lax.axis_index("station")
    half = lax.axis_index("tm")
    inputs = volts.shape[2]
    frames = volts.shape[3] // SUBBAND_COUNT
    frames_all = frames * lax.axis_size("tm")
    fine = SUBBAND_COUNT // owners
    groups = fine // GROUP
    blocks = frames // BLOCK

    keep_all = keep_table(flagged)
    keep_mine = lax.dynamic_index_in_dim(keep_all, lax.axis_index("band"), 0, keepdims=False)
    twice = jnp.concatenate([keep_mine, keep_mine])
    keep_ahead = lax.dynamic_slice_in_dim(twice, me * fine, SUBBAND_COUNT, 0)

    rows = twiddle_values().reshape(owners, groups, GROUP, 2, 2 * SUBBAND_COUNT)
    rows = rows.transpose(0, 1, 3, 2, 4)
    turns = [np.roll(rows, -z, 0).reshape(2 * SUBBAND_COUNT, -1) for z in range(owners)]
    table = jnp.asarray(np.stack(turns).astype(jnp.bfloat16))
    window = np.broadcast_to(window_values()[:, :, None], (TAPS, SUBBAND_COUNT, 128))
    window = jnp.asarray(np.ascontiguousarray(window))
    spot = jnp.reshape(me, (1,)).astype(jnp.int32)

    if groups != sum(RUNS) or RUNS[0] != 1:
        runs = (1,) * groups
    else:
        runs = RUNS
    parts, arrived, flat, out = [], [], [], None

    def send(n, waits, scale=None):
        got = [parts[n][0]]
        for d in range(1, owners):
            gates = list(waits.get(d, ()))
            if len(flat) >= IN_FLIGHT and not (n == 1 and d == 2):
                gates.append(flat[len(flat) - IN_FLIGHT])
            value = parts[n][d] if scale is None else with_scales(parts[n][d], scale)
            value = after(value, *gates) if gates else value
            with jax.named_scope(f"part{n}_shift{d}"):
                got.append(shift(value, d))
            flat.append(got[-1])
        arrived.append(got)

    power, halo, end = [], None, blocks
    for size in PARTS:
        end -= size
        spectra, part_power, tail = front(
            volts, None, end, size, (groups,), owners, keep_ahead, spot, window, table, halo is None
        )
        if tail is not None:
            halo = tail
        parts.append([x.reshape(groups, 2, GROUP * size * BLOCK, inputs) for x in spectra])
        power.append(part_power)
        if len(parts) == 1:
            send(0, {})
    with jax.named_scope("halo"):
        halo = passed_on(halo)
    spectra, part_power, _ = front(
        volts, halo, 0, end, runs, owners, keep_ahead, spot, window, table, False
    )
    power.append(part_power)
    for q, run in enumerate(runs):
        parts.append(
            [
                spectra[d * len(runs) + q].reshape(run, 2, GROUP * end * BLOCK, inputs)
                for d in range(owners)
            ]
        )

    local = jnp.sum(sum(power), axis=0)
    total = lax.psum(local, ("band", "tm"))
    scale = lax.rsqrt(total / (frames_all * jnp.sum(keep_all)) + 1e-06)
    kept = lax.dynamic_slice_in_dim(keep_mine, me * fine, fine, 0)
    counts = kept.reshape(groups, GROUP).sum(-1)
    denom = frames_all * jnp.maximum(counts, 1.0)
    place = jnp.stack([me, 1 - half, half]).astype(jnp.int32)
    shared = len(PARTS)
    def to_other(j, theirs):
        with jax.named_scope(f"rows{j}"):
            return lax.ppermute(theirs, "tm", [(0, 1), (1, 0)])

    homes = [(q, at) for q, run in enumerate(runs) for at in range(run)]

    def multiply(j, place, dtypes, sums=(), earlier=(), begin=0, end=shared + 1):
        q, at = homes[j]
        pieces = arrived[:shared] + arrived[shared + q : shared + q + 1]
        picks = (j,) * shared + (at,)
        return correlate(place, pieces[begin:end], picks[begin:end], dtypes, sums, earlier)

    both = [jnp.bfloat16, jnp.float32]
    last_spectra = parts[shared][0]
    for n in range(1, shared):
        send(n, {d: [last_spectra, arrived[0][2]] for d in range(1, owners) if d != 2})
    send(shared, {}, scale[None, :])
    got = arrived[shared]
    size = 2 * got[0].shape[2]
    by_shift = [scale]
    for d in range(1, owners):
        by_shift.append(got[d][size : size + 3].astype(jnp.float32).sum(0))
        got[d] = got[d][:size].reshape(got[0].shape)
    source = (me - jnp.arange(owners)) % owners
    chosen = (jnp.arange(owners)[:, None] == source[None, :]).astype(jnp.float32)
    scales = jnp.sum(chosen[:, :, None] * jnp.stack(by_shift)[None], axis=1).reshape(-1)
    per_half = scales.shape[0] // 2
    row_scales = lax.dynamic_slice_in_dim(scales, half * per_half, per_half, 0)

    column_scales = scales[None, :]
    row_scales = [(row_scales / denom[j])[None, :] for j in range(groups)]

    partial = multiply(groups - 1, place, [jnp.float32] * 2, end=shared)
    waiting = []

    def settle(out, earlier):
        for j, mine, theirs in waiting:
            out = equalize(row_scales[j], column_scales, mine, theirs, out, j, groups, earlier)
        waiting.clear()
        return out

    done = 0
    for q, run in enumerate(runs[:-1]):
        send(shared + q + 1, {owners - 1: partial} if q == 0 else {})
        results = [multiply(j, place, both) for j in range(done, done + run)]
        if waiting:
            out = settle(out, [x[0] for x in results])
        for j, (theirs, mine) in enumerate(results, done):
            if q + 2 < len(runs):
                theirs = after(theirs, *arrived[shared + q + 1][1:])
            waiting.append((j, mine, to_other(j, theirs)))
        done += run
    j = groups - 1
    theirs, mine = multiply(j, place, both, partial, [] if out is None else [out], begin=shared)
    out = settle(out, [theirs])
    waiting.append((j, mine, to_other(j, theirs)))
    out = settle(out, [])
    return out[None]


def twiddle_table():
    values = twiddle_values().transpose(2, 1, 0)
    return jnp.asarray(values).astype(jnp.bfloat16)


def pair_products(left, right):
    swapped = jnp.stack([left[..., 1, :], -left[..., 0, :]], 4)
    real = jnp.einsum("cgfird,cgfjrd->icgj", left, right, preferred_element_type=jnp.float32)
    imag = jnp.einsum("cgfird,cgfjrd->icgj", swapped, right, preferred_element_type=jnp.float32)
    return jnp.stack([real, imag], 3)


def plain(volts, flagged):
    coarse_dev = volts.shape[1]
    inputs_dev = volts.shape[2]
    spec_count = volts.shape[3] // SUBBAND_COUNT
    frames_all = spec_count * lax.axis_size("tm")
    frames = volts.reshape(2, coarse_dev, inputs_dev, spec_count, SUBBAND_COUNT)
    history = passed_on(frames[:, :, :, spec_count - (TAPS - 1) :, :])
    padded = jnp.concatenate([history, frames], 3)
    window = jnp.asarray(window_values())
    filtered = jnp.zeros((2, coarse_dev, inputs_dev, spec_count, SUBBAND_COUNT), jnp.float32)
    for tap in range(TAPS):
        filtered = filtered + window[tap] * padded[:, :, :, tap : tap + spec_count, :].astype(
            jnp.float32
        )
    filtered = filtered.astype(jnp.bfloat16)
    joined = jnp.concatenate([filtered[0], filtered[1]], -1)
    spectra = jnp.einsum(
        "nqvx,xdl->nlqdv", joined, twiddle_table(), preferred_element_type=jnp.float32
    ).astype(jnp.bfloat16)
    keep_all = keep_table(flagged)
    keep_mine = lax.dynamic_slice_in_dim(
        keep_all, lax.axis_index("band") * coarse_dev, coarse_dev, 0
    )
    values = spectra.astype(jnp.float32)
    local = jnp.sum(values * values * keep_mine[:, :, None, None, None], axis=(0, 1, 3, 4))
    total = lax.psum(local, ("band", "tm"))
    scale = lax.rsqrt(total / (frames_all * jnp.sum(keep_all)) + 1e-06)
    scales = lax.all_gather(scale, "station", axis=0, tiled=True)
    received = lax.all_to_all(spectra, "station", split_axis=1, concat_axis=2, tiled=True)
    fine_dev = received.shape[1]
    inputs_all = received.shape[2]
    kept = lax.dynamic_slice_in_dim(keep_mine, lax.axis_index("station") * fine_dev, fine_dev, 1)
    groups_dev = fine_dev // GROUP
    masked = received * kept[:, :, None, None, None].astype(jnp.bfloat16)
    blocks = masked.reshape(coarse_dev, groups_dev, GROUP, inputs_all, 2, spec_count)
    rows = inputs_all // lax.axis_size("tm")
    summed = lax.psum_scatter(pair_products(blocks, blocks), "tm", scatter_dimension=0, tiled=True)
    counts = kept.reshape(coarse_dev, groups_dev, GROUP).sum(-1)
    denom = frames_all * jnp.maximum(counts, 1.0)
    row_scales = lax.dynamic_slice_in_dim(scales, lax.axis_index("tm") * rows, rows, 0)
    pairs = row_scales[:, None] * scales[None, :]
    ordered = jnp.transpose(summed, (1, 2, 3, 0, 4))
    return ordered * pairs[None, None, None, :, :] / denom[:, :, None, None, None]


def shards(volts, flagged):
    owners = lax.axis_size("station")
    frames = volts.shape[3] // SUBBAND_COUNT
    fits = (
        volts.shape[1] == 1
        and volts.shape[2] % 128 == 0
        and owners % 2 == 0
        and (SUBBAND_COUNT // owners) % GROUP == 0
        and lax.axis_size("tm") == 2
        and frames % BLOCK == 0
        and SUBBAND_COUNT // owners // GROUP > 1
        and owners * volts.shape[2] // 2 % 128 == 0
        and frames // BLOCK > sum(PARTS)
    )
    return (pipelined if fits else plain)(volts, flagged)


def solution(mesh):
    placed = (P(None, "band", "station", "tm"), P())
    return jax.shard_map(
        shards,
        mesh=mesh,
        in_specs=placed,
        out_specs=P("band", "station", None, "tm", None),
        check_vma=False,
    )
```

```python
import functools
import math

import jax
import jax.numpy as jnp
import numpy as np
from jax import lax
from jax.experimental import pallas as pl
from jax.experimental.pallas import tpu as pltpu
from jax.sharding import PartitionSpec as P

SUBBAND_COUNT = 144
TAPS = 12
GROUP = 9
BLOCK = 16
PARTS = (1, 4)
RUNS = (1, 1, 1, 1)
SPREAD = BLOCK + 1
VMEM = 60 * 1024 * 1024
COST = pl.CostEstimate(flops=1024, bytes_accessed=1024, transcendentals=0)
IN_FLIGHT = 3


def window_values():
    total = TAPS * SUBBAND_COUNT
    place = np.arange(total, dtype=np.float64)
    shape = np.sinc((place - total / 2.0 + 0.5) / SUBBAND_COUNT)
    taper = 0.5 - 0.5 * np.cos(2.0 * math.pi * (place + 0.5) / total)
    return (shape * taper).reshape(TAPS, SUBBAND_COUNT).astype(np.float32)


def twiddle_values():
    f = np.arange(SUBBAND_COUNT, dtype=np.int64)[:, None]
    n = np.arange(SUBBAND_COUNT, dtype=np.int64)[None, :]
    angle = 2.0 * math.pi * (f * n % SUBBAND_COUNT) / SUBBAND_COUNT
    cosines, sines = np.cos(angle), np.sin(angle)
    real = np.concatenate([cosines, sines], 1)
    imag = np.concatenate([-sines, cosines], 1)
    return np.stack([real, imag], 1).astype(np.float32)


def front_kernel(
    runs, owners, turned, tail, me_ref, keep_ref, hist_ref, volts_ref, window_ref, table_ref, *rest
):
    splits = len(runs)
    outs, power_ref = rest[: owners * splits], rest[owners * splits]
    tail_ref = rest[owners * splits + 1] if tail else None
    homes = [(q, place) for q, run in enumerate(runs) for place in range(run)]
    ring, filt, spread = rest[-3:]
    step = pl.program_id(0)
    now = lax.rem(step, 2)
    before = 1 - now
    inputs = ring.shape[-1]
    tiles = inputs // 128
    span = BLOCK * SUBBAND_COUNT
    skipped = (BLOCK + 1 - TAPS) * SUBBAND_COUNT

    def turn(ref, slot, begin):
        def columns(c, _):
            at = pl.multiple_of(c * 128, 128)
            for part in range(2):
                ring[slot, part, pl.ds(at, 128), :] = ref[part, 0, :, pl.ds(at, 128)].T
            return 0

        lax.fori_loop(begin, span // 128, columns, 0, unroll=6 if begin == 0 else 5)

    @pl.when(step == 0)
    def _():
        if turned:
            for part in range(2):
                ring[1, part, pl.ds(skipped, span - skipped), :] = hist_ref[part]
        else:
            turn(hist_ref, 1, 3)
        power_ref[...] = jnp.zeros_like(power_ref)

    turn(volts_ref, now, 0)
    if tail:
        for part in range(2):
            tail_ref[part] = ring[now, part, pl.ds(skipped, span - skipped), :]

    def filter_rows(j, _):
        base = pl.multiple_of(j * 16, 16)
        for tile in range(tiles):
            lanes = pl.ds(tile * 128, 128)
            weights = [window_ref[k, pl.ds(base, 16), :] for k in range(TAPS)]
            for part in range(2):
                samples = []
                for t in range(1 - TAPS, BLOCK):
                    slot, frame = (now, t) if t >= 0 else (before, BLOCK + t)
                    at = pl.multiple_of(frame * SUBBAND_COUNT + base, 16)
                    samples.append(ring[slot, part, pl.ds(at, 16), lanes].astype(jnp.float32))
                for t in range(BLOCK):
                    total = weights[0] * samples[t]
                    for k in range(1, TAPS):
                        total = total + weights[k] * samples[t + k]
                    at = pl.multiple_of(part * SUBBAND_COUNT + base, 16)
                    filt[t, pl.ds(at, 16), lanes] = total.astype(jnp.bfloat16)
        return 0

    lax.fori_loop(0, SUBBAND_COUNT // 16, filter_rows, 0)

    def transform(t, _):
        result = jnp.dot(table_ref[0], filt[t], preferred_element_type=jnp.float32)
        for tile in range(tiles):
            spread[tile, pl.ds(t, 2 * SUBBAND_COUNT, stride=SPREAD), :] = result[
                :, tile * 128 : (tile + 1) * 128
            ]
        return 0

    lax.fori_loop(0, BLOCK, transform, 0, unroll=4)

    groups = SUBBAND_COUNT // owners // GROUP
    power = [jnp.zeros((BLOCK, 128), jnp.float32) for _ in range(tiles)]
    for d in range(owners):
        for j in range(groups):
            q, place = homes[j]
            out = outs[d * splits + q]

            def channel(f, power, d=d, j=j, out=out, place=place):
                keep = keep_ref[(d * groups + j) * GROUP + f]
                power = list(power)
                for part in range(2):
                    row = ((d * groups + j) * 2 + part) * GROUP + f
                    for tile in range(tiles):
                        value = spread[tile, pl.ds(row * SPREAD, BLOCK), :] * keep
                        value = value.astype(jnp.bfloat16)
                        out[place, part, f, :, tile * 128 : (tile + 1) * 128] = value
                        value = value.astype(jnp.float32)
                        power[tile] = power[tile] + value * value
                return tuple(power)

            power = lax.fori_loop(0, GROUP, channel, tuple(power), unroll=3)
    for tile in range(tiles):
        power_ref[:, tile * 128 : (tile + 1) * 128] += power[tile]


def front(volts, hist, first, steps, runs, owners, keep, me, window, table, tail):
    inputs = volts.shape[2]
    span = BLOCK * SUBBAND_COUNT
    frames = steps * BLOCK
    outs, out_specs = [], []
    for _ in range(owners):
        for run in runs:
            outs.append(jax.ShapeDtypeStruct((run, 2, GROUP, frames, inputs), jnp.bfloat16))
            out_specs.append(
                pl.BlockSpec((run, 2, GROUP, BLOCK, inputs), lambda s, me: (0, 0, 0, s, 0))
            )
    outs.append(jax.ShapeDtypeStruct((BLOCK, inputs), jnp.float32))
    out_specs.append(pl.BlockSpec((BLOCK, inputs), lambda s, me: (0, 0)))
    kept = (TAPS - 1) * SUBBAND_COUNT
    if tail:
        outs.append(jax.ShapeDtypeStruct((2, kept, inputs), jnp.bfloat16))
        out_specs.append(pl.BlockSpec((2, kept, inputs), lambda s, me: (0, 0, 0)))
    if hist is None:
        hist, hist_spec = volts, pl.BlockSpec((2, 1, inputs, span), lambda s, me: (0, 0, 0, first - 1))
        turned = False
    else:
        hist_spec, turned = pl.BlockSpec((2, kept, inputs), lambda s, me: (0, 0, 0)), True
    result = pl.pallas_call(
        functools.partial(front_kernel, runs, owners, turned, tail),
        grid_spec=pltpu.PrefetchScalarGridSpec(
            num_scalar_prefetch=1,
            grid=(steps,),
            in_specs=[
                pl.BlockSpec(memory_space=pltpu.SMEM),
                hist_spec,
                pl.BlockSpec((2, 1, inputs, span), lambda s, me: (0, 0, 0, first + s)),
                pl.BlockSpec(window.shape, lambda s, me: (0, 0, 0)),
                pl.BlockSpec((1, *table.shape[1:]), lambda s, me: (me[0], 0, 0)),
            ],
            out_specs=out_specs,
            scratch_shapes=[
                pltpu.VMEM((2, 2, span, inputs), jnp.bfloat16),
                pltpu.VMEM((BLOCK, 2 * SUBBAND_COUNT, inputs), jnp.bfloat16),
                pltpu.VMEM((inputs // 128, 2 * SUBBAND_COUNT * SPREAD, 128), jnp.float32),
            ],
        ),
        out_shape=outs,
        compiler_params=pltpu.CompilerParams(vmem_limit_bytes=VMEM),
        cost_estimate=COST,
        name="front",
    )(me, keep, hist, volts, window, table)
    count = owners * len(runs)
    return result[:count], result[count], result[count + 1] if tail else None


def after_kernel(*refs):
    pass


def after(value, *others):
    anywhere = pl.BlockSpec(memory_space=pl.ANY)
    return pl.pallas_call(
        after_kernel,
        out_shape=jax.ShapeDtypeStruct(value.shape, value.dtype),
        in_specs=[anywhere] * (1 + len(others)),
        out_specs=anywhere,
        input_output_aliases={0: 0},
        cost_estimate=COST,
        name="after",
    )(value, *others)


def with_scales_kernel(value_ref, scale_ref, out_ref):
    size = value_ref.shape[2]
    left = scale_ref[...]
    pieces = []
    for _ in range(3):
        piece = left.astype(jnp.bfloat16).astype(jnp.float32)
        pieces.append(jnp.broadcast_to(piece, (16, piece.shape[1])))
        left = left - piece
    place = lax.broadcasted_iota(jnp.int32, pieces[0].shape, 0)
    chosen = jnp.where(place == 0, pieces[0], jnp.where(place == 1, pieces[1], pieces[2]))
    out_ref[pl.ds(0, size), :] = value_ref[0, 0]
    out_ref[pl.ds(size, size), :] = value_ref[0, 1]
    out_ref[pl.ds(2 * size, 16), :] = chosen.astype(jnp.bfloat16)


def with_scales(value, scale):
    size, inputs = value.shape[2:]
    whole = pl.BlockSpec(memory_space=pltpu.VMEM)
    return pl.pallas_call(
        with_scales_kernel,
        out_shape=jax.ShapeDtypeStruct((2 * size + 16, inputs), value.dtype),
        in_specs=[whole, whole],
        out_specs=whole,
        compiler_params=pltpu.CompilerParams(vmem_limit_bytes=VMEM),
        cost_estimate=COST,
        name="with_scales",
    )(value, scale)


def correlate_kernel(owners, picks, outs, sums, place_ref, *rest):
    count = len(picks)
    sum_refs, rest = rest[:sums], rest[sums:]
    pieces = [rest[n * owners : (n + 1) * owners] for n in range(count)]
    out_refs, (held, turned, sems) = rest[-3 - outs : -3], rest[-3:]
    me = place_ref[0]
    column = pl.program_id(0)
    per_half = owners // 2
    inputs, depth = turned.shape[3], held.shape[2]

    @pl.when(column == 0)
    def _():
        copies = []
        for d in range(owners):
            source = lax.rem(me - d + owners, owners)
            at = 0
            for n in range(count):
                size = pieces[n][d].shape[2]
                copies.append(
                    pltpu.make_async_copy(
                        pieces[n][d].at[picks[n]], held.at[source, :, pl.ds(at, size)], sems.at[n, d]
                    )
                )
                at += size
        for copy in copies:
            copy.start()
        for copy in copies:
            copy.wait()
        for h in range(outs):
            for r in range(per_half):
                source = place_ref[1 + h] * per_half + r
                real, imag = held[source, 0].T, held[source, 1].T
                turned[h, 0, r, :, pl.ds(0, depth)] = real
                turned[h, 0, r, :, pl.ds(depth, depth)] = imag
                turned[h, 1, r, :, pl.ds(0, depth)] = imag
                turned[h, 1, r, :, pl.ds(depth, depth)] = -real

    right = held[column].reshape(2 * depth, inputs)
    for h in range(outs):
        left = turned[h].reshape(2 * per_half * inputs, 2 * depth)
        both = jnp.dot(left, right, preferred_element_type=jnp.float32)
        both = both.reshape(2, per_half * inputs, inputs)
        if sums:
            both = both + sum_refs[h][...]
        out_refs[h][...] = both.astype(out_refs[h].dtype)


def correlate(place, pieces, picks, dtypes, sums, earlier):
    owners = len(pieces[0])
    inputs = pieces[0][0].shape[-1]
    depth = sum(piece[0].shape[2] for piece in pieces)
    rows = owners // 2 * inputs
    operands = [value for piece in pieces for value in piece] + list(earlier)
    columns = pl.BlockSpec((2, rows, inputs), lambda b: (0, 0, b))
    anywhere = pl.BlockSpec(memory_space=pl.ANY)
    outs = len(dtypes)
    return pl.pallas_call(
        functools.partial(correlate_kernel, owners, picks, outs, len(sums)),
        grid=(owners,),
        out_shape=[jax.ShapeDtypeStruct((2, rows, owners * inputs), dtype) for dtype in dtypes],
        in_specs=[pl.BlockSpec(memory_space=pltpu.SMEM)]
        + [columns] * len(sums)
        + [anywhere] * len(operands),
        out_specs=[columns] * outs,
        scratch_shapes=[
            pltpu.VMEM((owners, 2, depth, inputs), jnp.bfloat16),
            pltpu.VMEM((outs, 2, owners // 2, inputs, 2 * depth), jnp.bfloat16),
            pltpu.SemaphoreType.DMA((len(pieces), owners)),
        ],
        compiler_params=pltpu.CompilerParams(vmem_limit_bytes=VMEM),
        cost_estimate=COST,
        name="correlate",
    )(place, *sums, *operands)


def equalize_kernel(rows_ref, columns_ref, mine_ref, theirs_ref, *rest):
    out_ref = rest[-1]
    rows = rows_ref.shape[1]
    by_row = jnp.broadcast_to(rows_ref[...], (rows, rows)).T
    for at in range(0, columns_ref.shape[1], rows):
        columns = slice(at, at + rows)
        scale = by_row * columns_ref[:, columns]
        for part in range(2):
            total = mine_ref[part, :, columns] + theirs_ref[part, :, columns].astype(jnp.float32)
            out_ref[0, part, :, columns] = total * scale


def equalize(row_scales, column_scales, mine, theirs, out, group, groups, waits):
    rows, columns = mine.shape[1:]
    block = 128
    specs = [
        pl.BlockSpec((1, block), lambda r: (0, r)),
        pl.BlockSpec((1, columns), lambda r: (0, 0)),
        pl.BlockSpec((2, block, columns), lambda r: (0, r, 0)),
        pl.BlockSpec((2, block, columns), lambda r: (0, r, 0)),
    ]
    operands = [row_scales, column_scales, mine, theirs]
    aliases = {}
    if out is not None:
        specs.append(pl.BlockSpec(memory_space=pl.ANY))
        operands.append(out)
        aliases = {4: 0}
    specs += [pl.BlockSpec(memory_space=pl.ANY)] * len(waits)
    operands += waits
    return pl.pallas_call(
        equalize_kernel,
        grid=(rows // block,),
        out_shape=jax.ShapeDtypeStruct((groups, 2, rows, columns), jnp.float32),
        in_specs=specs,
        out_specs=pl.BlockSpec((1, 2, block, columns), lambda r: (group, 0, r, 0)),
        input_output_aliases=aliases,
        compiler_params=pltpu.CompilerParams(vmem_limit_bytes=VMEM),
        cost_estimate=COST,
        name="equalize",
    )(*operands)


def shift(value, d):
    count = lax.axis_size("station")
    return lax.ppermute(value, "station", [(s, (s + d) % count) for s in range(count)])


def passed_on(value):
    count = lax.axis_size("tm")
    return lax.ppermute(value, "tm", [(s, s + 1) for s in range(count - 1)])


def keep_table(flagged):
    fine = jnp.arange(SUBBAND_COUNT, dtype=jnp.int32)
    return jnp.all(flagged[:, :, None] != fine[None, None, :], axis=1).astype(jnp.float32)


def pipelined(volts, flagged):
    owners = lax.axis_size("station")
    me = lax.axis_index("station")
    half = lax.axis_index("tm")
    inputs = volts.shape[2]
    frames = volts.shape[3] // SUBBAND_COUNT
    frames_all = frames * lax.axis_size("tm")
    fine = SUBBAND_COUNT // owners
    groups = fine // GROUP
    blocks = frames // BLOCK

    keep_all = keep_table(flagged)
    keep_mine = lax.dynamic_index_in_dim(keep_all, lax.axis_index("band"), 0, keepdims=False)
    twice = jnp.concatenate([keep_mine, keep_mine])
    keep_ahead = lax.dynamic_slice_in_dim(twice, me * fine, SUBBAND_COUNT, 0)

    rows = twiddle_values().reshape(owners, groups, GROUP, 2, 2 * SUBBAND_COUNT)
    rows = rows.transpose(0, 1, 3, 2, 4)
    turns = [np.roll(rows, -z, 0).reshape(2 * SUBBAND_COUNT, -1) for z in range(owners)]
    table = jnp.asarray(np.stack(turns).astype(jnp.bfloat16))
    window = np.broadcast_to(window_values()[:, :, None], (TAPS, SUBBAND_COUNT, 128))
    window = jnp.asarray(np.ascontiguousarray(window))
    spot = jnp.reshape(me, (1,)).astype(jnp.int32)

    if groups != sum(RUNS) or RUNS[0] != 1:
        runs = (1,) * groups
    else:
        runs = RUNS
    parts, arrived, flat, out = [], [], [], None

    def send(n, waits, scale=None):
        got = [parts[n][0]]
        for d in range(1, owners):
            gates = list(waits.get(d, ()))
            if len(flat) >= IN_FLIGHT and not (n == 1 and d == 2):
                gates.append(flat[len(flat) - IN_FLIGHT])
            value = parts[n][d] if scale is None else with_scales(parts[n][d], scale)
            value = after(value, *gates) if gates else value
            with jax.named_scope(f"part{n}_shift{d}"):
                got.append(shift(value, d))
            flat.append(got[-1])
        arrived.append(got)

    power, halo, end = [], None, blocks
    for size in PARTS:
        end -= size
        spectra, part_power, tail = front(
            volts, None, end, size, (groups,), owners, keep_ahead, spot, window, table, halo is None
        )
        if tail is not None:
            halo = tail
        parts.append([x.reshape(groups, 2, GROUP * size * BLOCK, inputs) for x in spectra])
        power.append(part_power)
        if len(parts) == 1:
            send(0, {})
    with jax.named_scope("halo"):
        halo = passed_on(halo)
    spectra, part_power, _ = front(
        volts, halo, 0, end, runs, owners, keep_ahead, spot, window, table, False
    )
    power.append(part_power)
    for q, run in enumerate(runs):
        parts.append(
            [
                spectra[d * len(runs) + q].reshape(run, 2, GROUP * end * BLOCK, inputs)
                for d in range(owners)
            ]
        )

    local = jnp.sum(sum(power), axis=0)
    total = lax.psum(local, ("band", "tm"))
    scale = lax.rsqrt(total / (frames_all * jnp.sum(keep_all)) + 1e-06)
    kept = lax.dynamic_slice_in_dim(keep_mine, me * fine, fine, 0)
    counts = kept.reshape(groups, GROUP).sum(-1)
    denom = frames_all * jnp.maximum(counts, 1.0)
    place = jnp.stack([me, 1 - half, half]).astype(jnp.int32)
    shared = len(PARTS)
    def to_other(j, theirs):
        with jax.named_scope(f"rows{j}"):
            return lax.ppermute(theirs, "tm", [(0, 1), (1, 0)])

    homes = [(q, at) for q, run in enumerate(runs) for at in range(run)]

    def multiply(j, place, dtypes, sums=(), earlier=(), begin=0, end=shared + 1):
        q, at = homes[j]
        pieces = arrived[:shared] + arrived[shared + q : shared + q + 1]
        picks = (j,) * shared + (at,)
        return correlate(place, pieces[begin:end], picks[begin:end], dtypes, sums, earlier)

    both = [jnp.bfloat16, jnp.float32]
    last_spectra = parts[shared][0]
    for n in range(1, shared):
        send(n, {d: [last_spectra, arrived[0][2]] for d in range(1, owners) if d != 2})
    send(shared, {}, scale[None, :])
    got = arrived[shared]
    size = 2 * got[0].shape[2]
    by_shift = [scale]
    for d in range(1, owners):
        by_shift.append(got[d][size : size + 3].astype(jnp.float32).sum(0))
        got[d] = got[d][:size].reshape(got[0].shape)
    source = (me - jnp.arange(owners)) % owners
    chosen = (jnp.arange(owners)[:, None] == source[None, :]).astype(jnp.float32)
    scales = jnp.sum(chosen[:, :, None] * jnp.stack(by_shift)[None], axis=1).reshape(-1)
    per_half = scales.shape[0] // 2
    row_scales = lax.dynamic_slice_in_dim(scales, half * per_half, per_half, 0)

    column_scales = scales[None, :]
    row_scales = [(row_scales / denom[j])[None, :] for j in range(groups)]

    waiting = []

    def settle(out, earlier):
        for j, mine, theirs in waiting:
            out = equalize(row_scales[j], column_scales, mine, theirs, out, j, groups, earlier)
        waiting.clear()
        return out

    done = 0
    for q, run in enumerate(runs[:-1]):
        send(shared + q + 1, {})
        results = [multiply(j, place, both) for j in range(done, done + run)]
        if waiting:
            out = settle(out, [x[0] for x in results])
        for j, (theirs, mine) in enumerate(results, done):
            if q + 2 < len(runs):
                theirs = after(theirs, *arrived[shared + q + 1][1:])
            waiting.append((j, mine, to_other(j, theirs)))
        done += run
    j = groups - 1
    gates = [] if out is None else [out]
    partial = multiply(j, place, [jnp.float32] * 2, earlier=gates, end=shared)
    theirs, mine = multiply(j, place, both, partial, [] if out is None else [out], begin=shared)
    out = settle(out, [theirs])
    waiting.append((j, mine, to_other(j, theirs)))
    out = settle(out, [])
    return out[None]


def twiddle_table():
    values = twiddle_values().transpose(2, 1, 0)
    return jnp.asarray(values).astype(jnp.bfloat16)


def pair_products(left, right):
    swapped = jnp.stack([left[..., 1, :], -left[..., 0, :]], 4)
    real = jnp.einsum("cgfird,cgfjrd->icgj", left, right, preferred_element_type=jnp.float32)
    imag = jnp.einsum("cgfird,cgfjrd->icgj", swapped, right, preferred_element_type=jnp.float32)
    return jnp.stack([real, imag], 3)


def plain(volts, flagged):
    coarse_dev = volts.shape[1]
    inputs_dev = volts.shape[2]
    spec_count = volts.shape[3] // SUBBAND_COUNT
    frames_all = spec_count * lax.axis_size("tm")
    frames = volts.reshape(2, coarse_dev, inputs_dev, spec_count, SUBBAND_COUNT)
    history = passed_on(frames[:, :, :, spec_count - (TAPS - 1) :, :])
    padded = jnp.concatenate([history, frames], 3)
    window = jnp.asarray(window_values())
    filtered = jnp.zeros((2, coarse_dev, inputs_dev, spec_count, SUBBAND_COUNT), jnp.float32)
    for tap in range(TAPS):
        filtered = filtered + window[tap] * padded[:, :, :, tap : tap + spec_count, :].astype(
            jnp.float32
        )
    filtered = filtered.astype(jnp.bfloat16)
    joined = jnp.concatenate([filtered[0], filtered[1]], -1)
    spectra = jnp.einsum(
        "nqvx,xdl->nlqdv", joined, twiddle_table(), preferred_element_type=jnp.float32
    ).astype(jnp.bfloat16)
    keep_all = keep_table(flagged)
    keep_mine = lax.dynamic_slice_in_dim(
        keep_all, lax.axis_index("band") * coarse_dev, coarse_dev, 0
    )
    values = spectra.astype(jnp.float32)
    local = jnp.sum(values * values * keep_mine[:, :, None, None, None], axis=(0, 1, 3, 4))
    total = lax.psum(local, ("band", "tm"))
    scale = lax.rsqrt(total / (frames_all * jnp.sum(keep_all)) + 1e-06)
    scales = lax.all_gather(scale, "station", axis=0, tiled=True)
    received = lax.all_to_all(spectra, "station", split_axis=1, concat_axis=2, tiled=True)
    fine_dev = received.shape[1]
    inputs_all = received.shape[2]
    kept = lax.dynamic_slice_in_dim(keep_mine, lax.axis_index("station") * fine_dev, fine_dev, 1)
    groups_dev = fine_dev // GROUP
    masked = received * kept[:, :, None, None, None].astype(jnp.bfloat16)
    blocks = masked.reshape(coarse_dev, groups_dev, GROUP, inputs_all, 2, spec_count)
    rows = inputs_all // lax.axis_size("tm")
    summed = lax.psum_scatter(pair_products(blocks, blocks), "tm", scatter_dimension=0, tiled=True)
    counts = kept.reshape(coarse_dev, groups_dev, GROUP).sum(-1)
    denom = frames_all * jnp.maximum(counts, 1.0)
    row_scales = lax.dynamic_slice_in_dim(scales, lax.axis_index("tm") * rows, rows, 0)
    pairs = row_scales[:, None] * scales[None, :]
    ordered = jnp.transpose(summed, (1, 2, 3, 0, 4))
    return ordered * pairs[None, None, None, :, :] / denom[:, :, None, None, None]


def shards(volts, flagged):
    owners = lax.axis_size("station")
    frames = volts.shape[3] // SUBBAND_COUNT
    fits = (
        volts.shape[1] == 1
        and volts.shape[2] % 128 == 0
        and owners % 2 == 0
        and (SUBBAND_COUNT // owners) % GROUP == 0
        and lax.axis_size("tm") == 2
        and frames % BLOCK == 0
        and SUBBAND_COUNT // owners // GROUP > 1
        and owners * volts.shape[2] // 2 % 128 == 0
        and frames // BLOCK > sum(PARTS)
    )
    return (pipelined if fits else plain)(volts, flagged)


def solution(mesh):
    placed = (P(None, "band", "station", "tm"), P())
    return jax.shard_map(
        shards,
        mesh=mesh,
        in_specs=placed,
        out_specs=P("band", "station", None, "tm", None),
        check_vma=False,
    )
```

```python
import functools
import math

import jax
import jax.numpy as jnp
import numpy as np
from jax import lax
from jax.experimental import pallas as pl
from jax.experimental.pallas import tpu as pltpu
from jax.sharding import PartitionSpec as P

SUBBAND_COUNT = 144
TAPS = 12
GROUP = 9
BLOCK = 16
PARTS = (1, 3)
RUNS = (1, 1, 1, 1)
SPREAD = BLOCK + 1
VMEM = 60 * 1024 * 1024
COST = pl.CostEstimate(flops=1024, bytes_accessed=1024, transcendentals=0)
IN_FLIGHT = 3


def window_values():
    total = TAPS * SUBBAND_COUNT
    place = np.arange(total, dtype=np.float64)
    shape = np.sinc((place - total / 2.0 + 0.5) / SUBBAND_COUNT)
    taper = 0.5 - 0.5 * np.cos(2.0 * math.pi * (place + 0.5) / total)
    return (shape * taper).reshape(TAPS, SUBBAND_COUNT).astype(np.float32)


def twiddle_values():
    f = np.arange(SUBBAND_COUNT, dtype=np.int64)[:, None]
    n = np.arange(SUBBAND_COUNT, dtype=np.int64)[None, :]
    angle = 2.0 * math.pi * (f * n % SUBBAND_COUNT) / SUBBAND_COUNT
    cosines, sines = np.cos(angle), np.sin(angle)
    real = np.concatenate([cosines, sines], 1)
    imag = np.concatenate([-sines, cosines], 1)
    return np.stack([real, imag], 1).astype(np.float32)


def front_kernel(
    runs, owners, turned, tail, me_ref, keep_ref, hist_ref, volts_ref, window_ref, table_ref, *rest
):
    splits = len(runs)
    outs, power_ref = rest[: owners * splits], rest[owners * splits]
    tail_ref = rest[owners * splits + 1] if tail else None
    homes = [(q, place) for q, run in enumerate(runs) for place in range(run)]
    ring, filt, spread = rest[-3:]
    step = pl.program_id(0)
    now = lax.rem(step, 2)
    before = 1 - now
    inputs = ring.shape[-1]
    tiles = inputs // 128
    span = BLOCK * SUBBAND_COUNT
    skipped = (BLOCK + 1 - TAPS) * SUBBAND_COUNT

    def turn(ref, slot, begin):
        def columns(c, _):
            at = pl.multiple_of(c * 128, 128)
            for part in range(2):
                ring[slot, part, pl.ds(at, 128), :] = ref[part, 0, :, pl.ds(at, 128)].T
            return 0

        lax.fori_loop(begin, span // 128, columns, 0, unroll=6 if begin == 0 else 5)

    @pl.when(step == 0)
    def _():
        if turned:
            for part in range(2):
                ring[1, part, pl.ds(skipped, span - skipped), :] = hist_ref[part]
        else:
            turn(hist_ref, 1, 3)
        power_ref[...] = jnp.zeros_like(power_ref)

    turn(volts_ref, now, 0)
    if tail:
        for part in range(2):
            tail_ref[part] = ring[now, part, pl.ds(skipped, span - skipped), :]

    def filter_rows(j, _):
        base = pl.multiple_of(j * 16, 16)
        for tile in range(tiles):
            lanes = pl.ds(tile * 128, 128)
            weights = [window_ref[k, pl.ds(base, 16), :] for k in range(TAPS)]
            for part in range(2):
                samples = []
                for t in range(1 - TAPS, BLOCK):
                    slot, frame = (now, t) if t >= 0 else (before, BLOCK + t)
                    at = pl.multiple_of(frame * SUBBAND_COUNT + base, 16)
                    samples.append(ring[slot, part, pl.ds(at, 16), lanes].astype(jnp.float32))
                for t in range(BLOCK):
                    total = weights[0] * samples[t]
                    for k in range(1, TAPS):
                        total = total + weights[k] * samples[t + k]
                    at = pl.multiple_of(part * SUBBAND_COUNT + base, 16)
                    filt[t, pl.ds(at, 16), lanes] = total.astype(jnp.bfloat16)
        return 0

    lax.fori_loop(0, SUBBAND_COUNT // 16, filter_rows, 0)

    def transform(t, _):
        result = jnp.dot(table_ref[0], filt[t], preferred_element_type=jnp.float32)
        for tile in range(tiles):
            spread[tile, pl.ds(t, 2 * SUBBAND_COUNT, stride=SPREAD), :] = result[
                :, tile * 128 : (tile + 1) * 128
            ]
        return 0

    lax.fori_loop(0, BLOCK, transform, 0, unroll=4)

    groups = SUBBAND_COUNT // owners // GROUP
    power = [jnp.zeros((BLOCK, 128), jnp.float32) for _ in range(tiles)]
    for d in range(owners):
        for j in range(groups):
            q, place = homes[j]
            out = outs[d * splits + q]

            def channel(f, power, d=d, j=j, out=out, place=place):
                keep = keep_ref[(d * groups + j) * GROUP + f]
                power = list(power)
                for part in range(2):
                    row = ((d * groups + j) * 2 + part) * GROUP + f
                    for tile in range(tiles):
                        value = spread[tile, pl.ds(row * SPREAD, BLOCK), :] * keep
                        value = value.astype(jnp.bfloat16)
                        out[place, part, f, :, tile * 128 : (tile + 1) * 128] = value
                        value = value.astype(jnp.float32)
                        power[tile] = power[tile] + value * value
                return tuple(power)

            power = lax.fori_loop(0, GROUP, channel, tuple(power), unroll=3)
    for tile in range(tiles):
        power_ref[:, tile * 128 : (tile + 1) * 128] += power[tile]


def front(volts, hist, first, steps, runs, owners, keep, me, window, table, tail):
    inputs = volts.shape[2]
    span = BLOCK * SUBBAND_COUNT
    frames = steps * BLOCK
    outs, out_specs = [], []
    for _ in range(owners):
        for run in runs:
            outs.append(jax.ShapeDtypeStruct((run, 2, GROUP, frames, inputs), jnp.bfloat16))
            out_specs.append(
                pl.BlockSpec((run, 2, GROUP, BLOCK, inputs), lambda s, me: (0, 0, 0, s, 0))
            )
    outs.append(jax.ShapeDtypeStruct((BLOCK, inputs), jnp.float32))
    out_specs.append(pl.BlockSpec((BLOCK, inputs), lambda s, me: (0, 0)))
    kept = (TAPS - 1) * SUBBAND_COUNT
    if tail:
        outs.append(jax.ShapeDtypeStruct((2, kept, inputs), jnp.bfloat16))
        out_specs.append(pl.BlockSpec((2, kept, inputs), lambda s, me: (0, 0, 0)))
    if hist is None:
        hist, hist_spec = volts, pl.BlockSpec((2, 1, inputs, span), lambda s, me: (0, 0, 0, first - 1))
        turned = False
    else:
        hist_spec, turned = pl.BlockSpec((2, kept, inputs), lambda s, me: (0, 0, 0)), True
    result = pl.pallas_call(
        functools.partial(front_kernel, runs, owners, turned, tail),
        grid_spec=pltpu.PrefetchScalarGridSpec(
            num_scalar_prefetch=1,
            grid=(steps,),
            in_specs=[
                pl.BlockSpec(memory_space=pltpu.SMEM),
                hist_spec,
                pl.BlockSpec((2, 1, inputs, span), lambda s, me: (0, 0, 0, first + s)),
                pl.BlockSpec(window.shape, lambda s, me: (0, 0, 0)),
                pl.BlockSpec((1, *table.shape[1:]), lambda s, me: (me[0], 0, 0)),
            ],
            out_specs=out_specs,
            scratch_shapes=[
                pltpu.VMEM((2, 2, span, inputs), jnp.bfloat16),
                pltpu.VMEM((BLOCK, 2 * SUBBAND_COUNT, inputs), jnp.bfloat16),
                pltpu.VMEM((inputs // 128, 2 * SUBBAND_COUNT * SPREAD, 128), jnp.float32),
            ],
        ),
        out_shape=outs,
        compiler_params=pltpu.CompilerParams(vmem_limit_bytes=VMEM),
        cost_estimate=COST,
        name="front",
    )(me, keep, hist, volts, window, table)
    count = owners * len(runs)
    return result[:count], result[count], result[count + 1] if tail else None


def after_kernel(*refs):
    pass


def after(value, *others):
    anywhere = pl.BlockSpec(memory_space=pl.ANY)
    return pl.pallas_call(
        after_kernel,
        out_shape=jax.ShapeDtypeStruct(value.shape, value.dtype),
        in_specs=[anywhere] * (1 + len(others)),
        out_specs=anywhere,
        input_output_aliases={0: 0},
        cost_estimate=COST,
        name="after",
    )(value, *others)


def with_scales_kernel(value_ref, scale_ref, out_ref):
    size = value_ref.shape[2]
    left = scale_ref[...]
    pieces = []
    for _ in range(3):
        piece = left.astype(jnp.bfloat16).astype(jnp.float32)
        pieces.append(jnp.broadcast_to(piece, (16, piece.shape[1])))
        left = left - piece
    place = lax.broadcasted_iota(jnp.int32, pieces[0].shape, 0)
    chosen = jnp.where(place == 0, pieces[0], jnp.where(place == 1, pieces[1], pieces[2]))
    out_ref[pl.ds(0, size), :] = value_ref[0, 0]
    out_ref[pl.ds(size, size), :] = value_ref[0, 1]
    out_ref[pl.ds(2 * size, 16), :] = chosen.astype(jnp.bfloat16)


def with_scales(value, scale):
    size, inputs = value.shape[2:]
    whole = pl.BlockSpec(memory_space=pltpu.VMEM)
    return pl.pallas_call(
        with_scales_kernel,
        out_shape=jax.ShapeDtypeStruct((2 * size + 16, inputs), value.dtype),
        in_specs=[whole, whole],
        out_specs=whole,
        compiler_params=pltpu.CompilerParams(vmem_limit_bytes=VMEM),
        cost_estimate=COST,
        name="with_scales",
    )(value, scale)


def correlate_kernel(owners, picks, outs, sums, place_ref, *rest):
    count = len(picks)
    sum_refs, rest = rest[:sums], rest[sums:]
    pieces = [rest[n * owners : (n + 1) * owners] for n in range(count)]
    out_refs, (held, turned, sems) = rest[-3 - outs : -3], rest[-3:]
    me = place_ref[0]
    column = pl.program_id(0)
    per_half = owners // 2
    inputs, depth = turned.shape[3], held.shape[2]

    @pl.when(column == 0)
    def _():
        copies = []
        for d in range(owners):
            source = lax.rem(me - d + owners, owners)
            at = 0
            for n in range(count):
                size = pieces[n][d].shape[2]
                copies.append(
                    pltpu.make_async_copy(
                        pieces[n][d].at[picks[n]], held.at[source, :, pl.ds(at, size)], sems.at[n, d]
                    )
                )
                at += size
        for copy in copies:
            copy.start()
        for copy in copies:
            copy.wait()
        for h in range(outs):
            for r in range(per_half):
                source = place_ref[1 + h] * per_half + r
                real, imag = held[source, 0].T, held[source, 1].T
                turned[h, 0, r, :, pl.ds(0, depth)] = real
                turned[h, 0, r, :, pl.ds(depth, depth)] = imag
                turned[h, 1, r, :, pl.ds(0, depth)] = imag
                turned[h, 1, r, :, pl.ds(depth, depth)] = -real

    right = held[column].reshape(2 * depth, inputs)
    for h in range(outs):
        left = turned[h].reshape(2 * per_half * inputs, 2 * depth)
        both = jnp.dot(left, right, preferred_element_type=jnp.float32)
        both = both.reshape(2, per_half * inputs, inputs)
        if sums:
            both = both + sum_refs[h][...]
        out_refs[h][...] = both.astype(out_refs[h].dtype)


def correlate(place, pieces, picks, dtypes, sums, earlier):
    owners = len(pieces[0])
    inputs = pieces[0][0].shape[-1]
    depth = sum(piece[0].shape[2] for piece in pieces)
    rows = owners // 2 * inputs
    operands = [value for piece in pieces for value in piece] + list(earlier)
    columns = pl.BlockSpec((2, rows, inputs), lambda b: (0, 0, b))
    anywhere = pl.BlockSpec(memory_space=pl.ANY)
    outs = len(dtypes)
    return pl.pallas_call(
        functools.partial(correlate_kernel, owners, picks, outs, len(sums)),
        grid=(owners,),
        out_shape=[jax.ShapeDtypeStruct((2, rows, owners * inputs), dtype) for dtype in dtypes],
        in_specs=[pl.BlockSpec(memory_space=pltpu.SMEM)]
        + [columns] * len(sums)
        + [anywhere] * len(operands),
        out_specs=[columns] * outs,
        scratch_shapes=[
            pltpu.VMEM((owners, 2, depth, inputs), jnp.bfloat16),
            pltpu.VMEM((outs, 2, owners // 2, inputs, 2 * depth), jnp.bfloat16),
            pltpu.SemaphoreType.DMA((len(pieces), owners)),
        ],
        compiler_params=pltpu.CompilerParams(vmem_limit_bytes=VMEM),
        cost_estimate=COST,
        name="correlate",
    )(place, *sums, *operands)


def equalize_kernel(rows_ref, columns_ref, mine_ref, theirs_ref, *rest):
    out_ref = rest[-1]
    rows = rows_ref.shape[1]
    by_row = jnp.broadcast_to(rows_ref[...], (rows, rows)).T
    for at in range(0, columns_ref.shape[1], rows):
        columns = slice(at, at + rows)
        scale = by_row * columns_ref[:, columns]
        for part in range(2):
            total = mine_ref[part, :, columns] + theirs_ref[part, :, columns].astype(jnp.float32)
            out_ref[0, part, :, columns] = total * scale


def equalize(row_scales, column_scales, mine, theirs, out, group, groups, waits):
    rows, columns = mine.shape[1:]
    block = 128
    specs = [
        pl.BlockSpec((1, block), lambda r: (0, r)),
        pl.BlockSpec((1, columns), lambda r: (0, 0)),
        pl.BlockSpec((2, block, columns), lambda r: (0, r, 0)),
        pl.BlockSpec((2, block, columns), lambda r: (0, r, 0)),
    ]
    operands = [row_scales, column_scales, mine, theirs]
    aliases = {}
    if out is not None:
        specs.append(pl.BlockSpec(memory_space=pl.ANY))
        operands.append(out)
        aliases = {4: 0}
    specs += [pl.BlockSpec(memory_space=pl.ANY)] * len(waits)
    operands += waits
    return pl.pallas_call(
        equalize_kernel,
        grid=(rows // block,),
        out_shape=jax.ShapeDtypeStruct((groups, 2, rows, columns), jnp.float32),
        in_specs=specs,
        out_specs=pl.BlockSpec((1, 2, block, columns), lambda r: (group, 0, r, 0)),
        input_output_aliases=aliases,
        compiler_params=pltpu.CompilerParams(vmem_limit_bytes=VMEM),
        cost_estimate=COST,
        name="equalize",
    )(*operands)


def shift(value, d):
    count = lax.axis_size("station")
    return lax.ppermute(value, "station", [(s, (s + d) % count) for s in range(count)])


def passed_on(value):
    count = lax.axis_size("tm")
    return lax.ppermute(value, "tm", [(s, s + 1) for s in range(count - 1)])


def keep_table(flagged):
    fine = jnp.arange(SUBBAND_COUNT, dtype=jnp.int32)
    return jnp.all(flagged[:, :, None] != fine[None, None, :], axis=1).astype(jnp.float32)


def pipelined(volts, flagged):
    owners = lax.axis_size("station")
    me = lax.axis_index("station")
    half = lax.axis_index("tm")
    inputs = volts.shape[2]
    frames = volts.shape[3] // SUBBAND_COUNT
    frames_all = frames * lax.axis_size("tm")
    fine = SUBBAND_COUNT // owners
    groups = fine // GROUP
    blocks = frames // BLOCK

    keep_all = keep_table(flagged)
    keep_mine = lax.dynamic_index_in_dim(keep_all, lax.axis_index("band"), 0, keepdims=False)
    twice = jnp.concatenate([keep_mine, keep_mine])
    keep_ahead = lax.dynamic_slice_in_dim(twice, me * fine, SUBBAND_COUNT, 0)

    rows = twiddle_values().reshape(owners, groups, GROUP, 2, 2 * SUBBAND_COUNT)
    rows = rows.transpose(0, 1, 3, 2, 4)
    turns = [np.roll(rows, -z, 0).reshape(2 * SUBBAND_COUNT, -1) for z in range(owners)]
    table = jnp.asarray(np.stack(turns).astype(jnp.bfloat16))
    window = np.broadcast_to(window_values()[:, :, None], (TAPS, SUBBAND_COUNT, 128))
    window = jnp.asarray(np.ascontiguousarray(window))
    spot = jnp.reshape(me, (1,)).astype(jnp.int32)

    if groups != sum(RUNS) or RUNS[0] != 1:
        runs = (1,) * groups
    else:
        runs = RUNS
    parts, arrived, flat, out = [], [], [], None

    def send(n, waits, scale=None):
        got = [parts[n][0]]
        for d in range(1, owners):
            gates = list(waits.get(d, ()))
            if len(flat) >= IN_FLIGHT and not (n == 1 and d == 2):
                gates.append(flat[len(flat) - IN_FLIGHT])
            value = parts[n][d] if scale is None else with_scales(parts[n][d], scale)
            value = after(value, *gates) if gates else value
            with jax.named_scope(f"part{n}_shift{d}"):
                got.append(shift(value, d))
            flat.append(got[-1])
        arrived.append(got)

    power, halo, end = [], None, blocks
    for size in PARTS:
        end -= size
        spectra, part_power, tail = front(
            volts, None, end, size, (groups,), owners, keep_ahead, spot, window, table, halo is None
        )
        if tail is not None:
            halo = tail
        parts.append([x.reshape(groups, 2, GROUP * size * BLOCK, inputs) for x in spectra])
        power.append(part_power)
        if len(parts) == 1:
            send(0, {})
    with jax.named_scope("halo"):
        halo = passed_on(halo)
    spectra, part_power, _ = front(
        volts, halo, 0, end, runs, owners, keep_ahead, spot, window, table, False
    )
    power.append(part_power)
    for q, run in enumerate(runs):
        parts.append(
            [
                spectra[d * len(runs) + q].reshape(run, 2, GROUP * end * BLOCK, inputs)
                for d in range(owners)
            ]
        )

    local = jnp.sum(sum(power), axis=0)
    total = lax.psum(local, ("band", "tm"))
    scale = lax.rsqrt(total / (frames_all * jnp.sum(keep_all)) + 1e-06)
    kept = lax.dynamic_slice_in_dim(keep_mine, me * fine, fine, 0)
    counts = kept.reshape(groups, GROUP).sum(-1)
    denom = frames_all * jnp.maximum(counts, 1.0)
    place = jnp.stack([me, 1 - half, half]).astype(jnp.int32)
    shared = len(PARTS)
    def to_other(j, theirs):
        with jax.named_scope(f"rows{j}"):
            return lax.ppermute(theirs, "tm", [(0, 1), (1, 0)])

    homes = [(q, at) for q, run in enumerate(runs) for at in range(run)]

    def multiply(j, place, dtypes, sums=(), earlier=(), begin=0, end=shared + 1):
        q, at = homes[j]
        pieces = arrived[:shared] + arrived[shared + q : shared + q + 1]
        picks = (j,) * shared + (at,)
        return correlate(place, pieces[begin:end], picks[begin:end], dtypes, sums, earlier)

    both = [jnp.bfloat16, jnp.float32]
    last_spectra = parts[shared][0]
    for n in range(1, shared):
        send(n, {d: [last_spectra, arrived[0][2]] for d in range(1, owners) if d != 2})
    send(shared, {}, scale[None, :])
    got = arrived[shared]
    size = 2 * got[0].shape[2]
    by_shift = [scale]
    for d in range(1, owners):
        by_shift.append(got[d][size : size + 3].astype(jnp.float32).sum(0))
        got[d] = got[d][:size].reshape(got[0].shape)
    source = (me - jnp.arange(owners)) % owners
    chosen = (jnp.arange(owners)[:, None] == source[None, :]).astype(jnp.float32)
    scales = jnp.sum(chosen[:, :, None] * jnp.stack(by_shift)[None], axis=1).reshape(-1)
    per_half = scales.shape[0] // 2
    row_scales = lax.dynamic_slice_in_dim(scales, half * per_half, per_half, 0)

    column_scales = scales[None, :]
    row_scales = [(row_scales / denom[j])[None, :] for j in range(groups)]

    waiting = []

    def settle(out, earlier):
        for j, mine, theirs in waiting:
            out = equalize(row_scales[j], column_scales, mine, theirs, out, j, groups, earlier)
        waiting.clear()
        return out

    done = 0
    for q, run in enumerate(runs[:-1]):
        send(shared + q + 1, {})
        results = [multiply(j, place, both) for j in range(done, done + run)]
        if waiting:
            out = settle(out, [x[0] for x in results])
        for j, (theirs, mine) in enumerate(results, done):
            if q + 2 < len(runs):
                theirs = after(theirs, *arrived[shared + q + 1][1:])
            waiting.append((j, mine, to_other(j, theirs)))
        done += run
    j = groups - 1
    gates = [] if out is None else [out]
    partial = multiply(j, place, [jnp.float32] * 2, earlier=gates, end=shared)
    theirs, mine = multiply(j, place, both, partial, [] if out is None else [out], begin=shared)
    out = settle(out, [theirs])
    waiting.append((j, mine, to_other(j, theirs)))
    out = settle(out, [])
    return out[None]


def twiddle_table():
    values = twiddle_values().transpose(2, 1, 0)
    return jnp.asarray(values).astype(jnp.bfloat16)


def pair_products(left, right):
    swapped = jnp.stack([left[..., 1, :], -left[..., 0, :]], 4)
    real = jnp.einsum("cgfird,cgfjrd->icgj", left, right, preferred_element_type=jnp.float32)
    imag = jnp.einsum("cgfird,cgfjrd->icgj", swapped, right, preferred_element_type=jnp.float32)
    return jnp.stack([real, imag], 3)


def plain(volts, flagged):
    coarse_dev = volts.shape[1]
    inputs_dev = volts.shape[2]
    spec_count = volts.shape[3] // SUBBAND_COUNT
    frames_all = spec_count * lax.axis_size("tm")
    frames = volts.reshape(2, coarse_dev, inputs_dev, spec_count, SUBBAND_COUNT)
    history = passed_on(frames[:, :, :, spec_count - (TAPS - 1) :, :])
    padded = jnp.concatenate([history, frames], 3)
    window = jnp.asarray(window_values())
    filtered = jnp.zeros((2, coarse_dev, inputs_dev, spec_count, SUBBAND_COUNT), jnp.float32)
    for tap in range(TAPS):
        filtered = filtered + window[tap] * padded[:, :, :, tap : tap + spec_count, :].astype(
            jnp.float32
        )
    filtered = filtered.astype(jnp.bfloat16)
    joined = jnp.concatenate([filtered[0], filtered[1]], -1)
    spectra = jnp.einsum(
        "nqvx,xdl->nlqdv", joined, twiddle_table(), preferred_element_type=jnp.float32
    ).astype(jnp.bfloat16)
    keep_all = keep_table(flagged)
    keep_mine = lax.dynamic_slice_in_dim(
        keep_all, lax.axis_index("band") * coarse_dev, coarse_dev, 0
    )
    values = spectra.astype(jnp.float32)
    local = jnp.sum(values * values * keep_mine[:, :, None, None, None], axis=(0, 1, 3, 4))
    total = lax.psum(local, ("band", "tm"))
    scale = lax.rsqrt(total / (frames_all * jnp.sum(keep_all)) + 1e-06)
    scales = lax.all_gather(scale, "station", axis=0, tiled=True)
    received = lax.all_to_all(spectra, "station", split_axis=1, concat_axis=2, tiled=True)
    fine_dev = received.shape[1]
    inputs_all = received.shape[2]
    kept = lax.dynamic_slice_in_dim(keep_mine, lax.axis_index("station") * fine_dev, fine_dev, 1)
    groups_dev = fine_dev // GROUP
    masked = received * kept[:, :, None, None, None].astype(jnp.bfloat16)
    blocks = masked.reshape(coarse_dev, groups_dev, GROUP, inputs_all, 2, spec_count)
    rows = inputs_all // lax.axis_size("tm")
    summed = lax.psum_scatter(pair_products(blocks, blocks), "tm", scatter_dimension=0, tiled=True)
    counts = kept.reshape(coarse_dev, groups_dev, GROUP).sum(-1)
    denom = frames_all * jnp.maximum(counts, 1.0)
    row_scales = lax.dynamic_slice_in_dim(scales, lax.axis_index("tm") * rows, rows, 0)
    pairs = row_scales[:, None] * scales[None, :]
    ordered = jnp.transpose(summed, (1, 2, 3, 0, 4))
    return ordered * pairs[None, None, None, :, :] / denom[:, :, None, None, None]


def shards(volts, flagged):
    owners = lax.axis_size("station")
    frames = volts.shape[3] // SUBBAND_COUNT
    fits = (
        volts.shape[1] == 1
        and volts.shape[2] % 128 == 0
        and owners % 2 == 0
        and (SUBBAND_COUNT // owners) % GROUP == 0
        and lax.axis_size("tm") == 2
        and frames % BLOCK == 0
        and SUBBAND_COUNT // owners // GROUP > 1
        and owners * volts.shape[2] // 2 % 128 == 0
        and frames // BLOCK > sum(PARTS)
    )
    return (pipelined if fits else plain)(volts, flagged)


def solution(mesh):
    placed = (P(None, "band", "station", "tm"), P())
    return jax.shard_map(
        shards,
        mesh=mesh,
        in_specs=placed,
        out_specs=P("band", "station", None, "tm", None),
        check_vma=False,
    )
```
